256 devices in a mesh: gx: 16 (over y, z_lo), gy: 16 (over x, z_hi, core).
Axes of the slice: x: 4, y: 4, z: 8 (z_hi: 2, z_lo: 4; z = z_hi * 4 + z_lo), core: 2. Of those that a mesh axis runs over, the one named last changes fastest.
Arguments:
- water_depth: float32 [2048, 8192], P('gx', 'gy'), may hold values from 0.5 to 2
- momentum_x: float32 [2048, 8192], P('gx', 'gy'), may hold values from -1.5 to 1.5
- momentum_y: float32 [2048, 8192], P('gx', 'gy'), may hold values from -1.5 to 1.5
- wet_mask: int32 [2048, 8192], P('gx', 'gy'), may hold values from 0 to 1, as said below
- damage_class: int32 [2048, 8192], P('gx', 'gy'), may hold values from 0 to 7
- damage_rates: float32 [8], replicated, may hold values from 0.2 to 2
- dam_cell: int32 [64], replicated, may hold values from 0 to 16777215, as said below
- releases: float32 [64, 2], replicated, may hold values from 0.5 to 4
Outputs:
- final_depth: float32 [2048, 8192], P('gx', 'gy')
- depth_adjoint: float32 [2048, 8192], P('gx', 'gy')
- release_grad: float32 [64, 2], replicated
The draws below stay inside these ranges and needn't reach their ends.
Inputs may be any that keep to these rules, and one draw needn't show every extreme that they name: Every dam's inflow cell has wet_mask 1. `dam_cell`: a cell index row * 8192 + column.
All inputs are finite; a program needn't handle non-finite values.
Results may differ from the reference program's by a relative error of at most 0.0003.
Values sent between devices are 32-bit elements; how exact they have to be, the bound alone decides.
No kernel may reach another device: no remote copies, remote signals or barrier semaphores. Data moves between devices by JAX's collectives and lax.ppermute only.
A program may use at most 64 MiB of HBM per device.

```python
import math
import jax
import jax.numpy as jnp
from jax import lax

STEPS = 2
DAMS = 64
CLASSES = 8
NX = 2048
NY = 8192
N_GX = 16


def dam_sites(key):
    return jax.random.randint(jax.random.fold_in(key, 41), (DAMS,), 0, NX * NY).astype(jnp.int32)


def draw_dam_cell(key, part):
    return dam_sites(key)


def draw_wet_mask(key, part):
    cells = dam_sites(key)
    levels = jax.random.randint(jax.random.fold_in(key, 42), (NX, NY), 0, 100)
    wet = jnp.where(levels < 88, 1, 0).astype(jnp.int32)
    return wet.at[cells // NY, cells % NY].set(1)


def place_ends(entries, rng, smallest, high):
    longest = entries.shape.index(max(entries.shape))
    spots = []
    for shift in (0, 1):
        where = [jax.random.randint(jax.random.fold_in(rng, axis), (), 0, length) for axis, length in enumerate(entries.shape)]
        where[longest] = (where[longest] + shift) % entries.shape[longest]
        spots.append(tuple(where))
    return entries.at[spots[0]].set(smallest).at[spots[1]].set(high)


def level_of(own_key, extent, shards, smallest, high):
    loudness, own = 1.0, jax.random.fold_in(own_key, 6)
    for axis_at, parts in shards:
        draws = jnp.exp(jax.random.uniform(jax.random.fold_in(own, axis_at), (parts,), jnp.float32, smallest / len(shards), high / len(shards)))
        loudness = loudness * jnp.repeat(draws, extent[axis_at] // parts).reshape([-1 if axis == axis_at else 1 for axis in range(len(extent))])
    return loudness


def gaussian(key, extent, deviation, bound, shards=(), kind=jnp.bfloat16):
    entries = deviation * jax.random.normal(key, extent, jnp.float32)
    if shards:
        entries = entries * level_of(key, extent, shards, -0.22, 0.18)
    return jnp.clip(entries, -bound, bound).astype(kind)


def setup_inputs(seed: int = 0) -> dict:
    seeds = jax.random.split(jax.random.key(seed), 9)
    water_depth = jnp.clip(0.5 + 1.5 * jax.random.uniform(seeds[0], (NX, NY), jnp.float32) ** level_of(seeds[0], (NX, NY), ((0, 16), (1, 16)), -0.2, 0.2), 0.5, 2.0)
    momentum_x = gaussian(seeds[1], (NX, NY), 0.6, 1.5, ((0, 16), (1, 16)), jnp.float32)
    momentum_y = gaussian(seeds[2], (NX, NY), 0.6, 1.5, ((0, 16), (1, 16)), jnp.float32)
    wet_mask = draw_wet_mask(jax.random.fold_in(seeds[8], 71), 0)
    damage_class = place_ends(jax.random.randint(seeds[4], (NX, NY), 0, CLASSES), jax.random.fold_in(seeds[4], 1), 0, CLASSES - 1).astype(jnp.int32)
    damage_rates = jnp.clip(jnp.exp(jax.random.uniform(seeds[5], (CLASSES,), jnp.float32, math.log(0.2), math.log(2.0))), 0.2, 2.0)
    dam_cell = draw_dam_cell(jax.random.fold_in(seeds[8], 71), 0)
    releases = jnp.clip(jnp.exp(jax.random.uniform(seeds[7], (DAMS, STEPS), jnp.float32, math.log(0.5), math.log(4.0))), 0.5, 4.0)
    return dict(water_depth=water_depth, momentum_x=momentum_x, momentum_y=momentum_y, wet_mask=wet_mask, damage_class=damage_class, damage_rates=damage_rates, dam_cell=dam_cell, releases=releases)


GRAVITY = 9.81
TIME_RATIO = 0.05
INFLOW_GAIN = 0.25

def face_flux(h_left, n_left, t_left, h_right, n_right, t_right):
    u_left = n_left / h_left
    u_right = n_right / h_right
    c_left = jnp.sqrt(GRAVITY * h_left)
    c_right = jnp.sqrt(GRAVITY * h_right)
    slowest = jnp.minimum(jnp.minimum(u_left - c_left, u_right - c_right), 0.0)
    fastest = jnp.maximum(jnp.maximum(u_left + c_left, u_right + c_right), 0.0)
    inverse = 1.0 / (fastest - slowest)
    left_flux = (n_left, n_left * u_left + 0.5 * GRAVITY * h_left * h_left, t_left * u_left)
    right_flux = (n_right, n_right * u_right + 0.5 * GRAVITY * h_right * h_right, t_right * u_right)
    jumps = (h_right - h_left, n_right - n_left, t_right - t_left)
    return tuple(((fastest * a - slowest * b + slowest * fastest * c) * inverse for a, b, c in zip(left_flux, right_flux, jumps)))

def walled(h_low, n_low, t_low, wet_low, h_high, n_high, t_high, wet_high):
    return (jnp.where(wet_low, h_low, h_high), jnp.where(wet_low, n_low, -n_high), jnp.where(wet_low, t_low, t_high), jnp.where(wet_high, h_high, h_low), jnp.where(wet_high, n_high, -n_low), jnp.where(wet_high, t_high, t_low))

def advance(fields, wetness):
    height = jnp.where(wetness, fields[0], 1.0)
    flow_x = jnp.where(wetness, fields[1], 0.0)
    flow_y = jnp.where(wetness, fields[2], 0.0)
    flux_rows = face_flux(*walled(height[:-1, 1:-1], flow_x[:-1, 1:-1], flow_y[:-1, 1:-1], wetness[:-1, 1:-1], height[1:, 1:-1], flow_x[1:, 1:-1], flow_y[1:, 1:-1], wetness[1:, 1:-1]))
    flux_cols = face_flux(*walled(height[1:-1, :-1], flow_y[1:-1, :-1], flow_x[1:-1, :-1], wetness[1:-1, :-1], height[1:-1, 1:], flow_y[1:-1, 1:], flow_x[1:-1, 1:], wetness[1:-1, 1:]))
    change_h = flux_rows[0][1:] - flux_rows[0][:-1] + flux_cols[0][:, 1:] - flux_cols[0][:, :-1]
    change_x = flux_rows[1][1:] - flux_rows[1][:-1] + flux_cols[2][:, 1:] - flux_cols[2][:, :-1]
    change_y = flux_rows[2][1:] - flux_rows[2][:-1] + flux_cols[1][:, 1:] - flux_cols[1][:, :-1]
    inside_wet = wetness[1:-1, 1:-1]
    previous = fields[:, 1:-1, 1:-1]
    return jnp.stack((jnp.where(inside_wet, previous[0] - TIME_RATIO * change_h, previous[0]), jnp.where(inside_wet, previous[1] - TIME_RATIO * change_x, previous[1]), jnp.where(inside_wet, previous[2] - TIME_RATIO * change_y, previous[2])))

def add_inflow(height, amounts, dam_rows, dam_cols, row_start, col_start):
    local_rows = dam_rows - row_start
    local_cols = dam_cols - col_start
    inside = (local_rows >= 0) & (local_rows < height.shape[0]) & (local_cols >= 0) & (local_cols < height.shape[1])
    return height.at[jnp.clip(local_rows, 0, height.shape[0] - 1), jnp.clip(local_cols, 0, height.shape[1] - 1)].add(jnp.where(inside, INFLOW_GAIN * amounts, 0.0))

def forward_step(fields, wetness, amounts, dam_rows, dam_cols, row_start, col_start):
    advanced = advance(fields, wetness)
    height = add_inflow(advanced[0], amounts, dam_rows, dam_cols, row_start + 1, col_start + 1)
    return jnp.concatenate((height[None], advanced[1:]), axis=0)

def cell_rates(damage_class, damage_rates, wet_mask):
    class_rate = jnp.zeros(damage_class.shape, jnp.float32)
    for class_index in range(damage_rates.shape[0]):
        class_rate = class_rate + jnp.where(damage_class == class_index, damage_rates[class_index], 0.0)
    return jnp.where(wet_mask > 0, class_rate, 0.0)

def reference(water_depth, momentum_x, momentum_y, wet_mask, damage_class, damage_rates, dam_cell, releases):
    total_rows, total_cols = water_depth.shape
    dam_rows = (dam_cell // total_cols).astype(jnp.int32)
    dam_cols = (dam_cell % total_cols).astype(jnp.int32)
    margin = 2 * STEPS
    fields = jnp.stack((water_depth, momentum_x, momentum_y))
    padded = jnp.pad(fields, ((0, 0), (margin, margin), (margin, margin)))
    wet_padded = jnp.pad(wet_mask, margin) > 0
    weight = cell_rates(damage_class, damage_rates, wet_mask)
    weight_padded = jnp.pad(weight, STEPS)
    rows_block = total_rows // N_GX
    width = total_cols + 2 * margin
    zero_index = jnp.zeros((), jnp.int32)

    def one_block(block_index):
        row_start = (block_index * rows_block).astype(jnp.int32)
        block_fields = lax.dynamic_slice(padded, (zero_index, row_start, zero_index), (3, rows_block + 2 * margin, width))
        wet_block = lax.dynamic_slice(wet_padded, (row_start, zero_index), (rows_block + 2 * margin, width))
        weights = lax.dynamic_slice(weight_padded, (row_start, zero_index), (rows_block + 2 * STEPS, total_cols + 2 * STEPS))
        owned_dams = (dam_rows >= row_start) & (dam_rows < row_start + rows_block)

        def advance_block(start_fields, own_releases):
            amounts = jnp.where(owned_dams[:, None], own_releases, releases)
            current = start_fields
            for step_index in range(STEPS):
                wet_now = wet_block[step_index:wet_block.shape[0] - step_index, step_index:width - step_index]
                current = forward_step(current, wet_now, amounts[:, step_index], dam_rows, dam_cols, row_start - margin + step_index, step_index - margin)
            return current
        ending, pullback = jax.vjp(advance_block, block_fields, releases)
        final_adjoint = jnp.stack((weights * ending[0], jnp.zeros_like(weights), jnp.zeros_like(weights)))
        field_grad, release_part = pullback(final_adjoint)
        return (ending[0, STEPS:-STEPS, STEPS:-STEPS], field_grad[0, margin:-margin, margin:-margin], release_part)
    depths, adjoints, release_parts = lax.map(one_block, jnp.arange(N_GX, dtype=jnp.int32))
    return (depths.reshape(total_rows, total_cols), adjoints.reshape(total_rows, total_cols), lax.optimization_barrier(jnp.sum(release_parts, axis=0)))
```

```python
import jax
import jax.numpy as jnp
from jax import lax
from jax.experimental import pallas as pl
from jax.experimental.pallas import tpu as pltpu
from jax.sharding import PartitionSpec as P

GRAVITY = 9.81
TIME_RATIO = 0.05
INFLOW_GAIN = 0.25

LANES = 128
REACH = 4
EDGE = 8
FIELDS = 4
STRIP = FIELDS * REACH


def class_rate(classes, rates_ref):
    rate = jnp.full(classes.shape, rates_ref[0], jnp.float32)
    for index in range(1, rates_ref.shape[0]):
        rate = jnp.where(classes == index, rates_ref[index], rate)
    return rate


def edge_columns_kernel(h_ref, x_ref, y_ref, wet_ref, class_ref, rates_ref, low_ref, high_ref):
    rows, cols = h_ref.shape
    lane = lax.broadcasted_iota(jnp.int32, (rows, LANES), 1)
    mixed = jnp.zeros((rows, LANES), jnp.float32)
    for side, start in ((0, 0), (1, cols - LANES)):
        part = slice(start, start + LANES)
        wet = wet_ref[:, part] > 0
        fields = (
            jnp.where(wet, h_ref[:, part], 0.0),
            x_ref[:, part],
            y_ref[:, part],
            jnp.where(wet, class_rate(class_ref[:, part], rates_ref), 0.0),
        )
        for index, field in enumerate(fields):
            first = side * STRIP + index * REACH
            moved = first if side == 0 else first + REACH
            shifted = pltpu.roll(field, moved, 1) if moved else field
            mixed = jnp.where((lane >= first) & (lane < first + REACH), shifted, mixed)
    turned = mixed.T
    low_ref[...] = turned[:STRIP]
    high_ref[...] = turned[STRIP : 2 * STRIP]


def edge_rows_kernel(
    h_ref, x_ref, y_ref, wet_ref, class_ref, rates_ref, left_ref, right_ref, side_ref, low_ref, high_ref
):
    rows, cols = h_ref.shape
    blank = jnp.zeros((LANES - 2 * STRIP, rows), jnp.float32)
    turned = jnp.concatenate((right_ref[...], left_ref[...], blank), axis=0).T
    lane = lax.broadcasted_iota(jnp.int32, (rows, LANES), 1)
    for index in range(FIELDS):
        first = index * REACH
        upper = pltpu.roll(turned, (LANES - first) % LANES, 1) if first else turned
        lower = pltpu.roll(turned, LANES - REACH - STRIP - first, 1)
        tile = jnp.where(lane < REACH, upper, jnp.where(lane >= LANES - REACH, lower, 0.0))
        side_ref[index] = tile
        low_ref[first : first + REACH, cols:] = tile[:REACH]
        high_ref[first : first + REACH, cols:] = tile[rows - REACH :]
    for ref, start, kept in ((low_ref, 0, 0), (high_ref, rows - 8, 8 - REACH)):
        part = slice(start, start + 8)
        wet = wet_ref[part, :] > 0
        fields = (
            jnp.where(wet, h_ref[part, :], 0.0),
            x_ref[part, :],
            y_ref[part, :],
            jnp.where(wet, class_rate(class_ref[part, :], rates_ref), 0.0),
        )
        for index, field in enumerate(fields):
            ref[index * REACH : (index + 1) * REACH, :cols] = field[kept : kept + REACH]


def cell_terms(height, flow_x, flow_y):
    scaled = GRAVITY * height
    inverse = 1.0 / height
    return flow_x * inverse, flow_y * inverse, jnp.sqrt(scaled), inverse


def waves(u_low, c_low, u_high, c_high, both):
    slow_low, slow_high = u_low - c_low, u_high - c_high
    fast_low, fast_high = u_low + c_low, u_high + c_high
    slowest = jnp.minimum(jnp.minimum(slow_low, slow_high), 0.0)
    fastest = jnp.maximum(jnp.maximum(fast_low, fast_high), 0.0)
    inverse = both * (1.0 / (fastest - slowest))
    share_low = fastest * inverse
    share_high = -(slowest * inverse)
    spread = slowest * share_low
    return slowest, fastest, inverse, share_low, share_high, spread, slow_low <= slow_high, fast_low >= fast_high


def speed_terms(slowest, fastest, of_slowest, of_fastest, slow_is_low, fast_is_low):
    of_slowest = jnp.where(slowest < 0.0, of_slowest, 0.0)
    of_fastest = jnp.where(fastest > 0.0, of_fastest, 0.0)
    slow_to_low = jnp.where(slow_is_low, of_slowest, 0.0)
    fast_to_low = jnp.where(fast_is_low, of_fastest, 0.0)
    slow_to_high = of_slowest - slow_to_low
    fast_to_high = of_fastest - fast_to_low
    return (
        fast_to_low + slow_to_low,
        fast_to_low - slow_to_low,
        fast_to_high + slow_to_high,
        fast_to_high - slow_to_high,
    )


def window_kernel(
    h_ref, x_ref, y_ref, wet_ref, class_ref, rates_ref, side_ref, top_ref, bottom_ref, dam_ref, release_ref,
    depth_ref, adjoint_ref, grad_ref,
    state0, state1, mask, faces, walls, weight, last, lam, back, listed,
):
    rows, cols = h_ref.shape
    tiles = cols // LANES + 1
    chunks = rows // 8 + 2
    inner = range(tiles - 1)
    every = range(tiles)
    lane = lax.broadcasted_iota(jnp.int32, (8, LANES), 1)

    def at(ref, k, j, start):
        return ref[k, j, pl.ds(start, 8), :]

    def next_col(values):
        rolled = [pltpu.roll(v, LANES - 1, 1) for v in values]
        return [jnp.where(lane == LANES - 1, rolled[(j + 1) % tiles], rolled[j]) for j in every]

    def previous_col(values):
        rolled = [pltpu.roll(v, 1, 1) for v in values]
        return [jnp.where(lane == 0, rolled[(j - 1) % tiles], rolled[j]) for j in every]

    def previous_row(slot, j, start, value):
        back[slot, j, pl.ds(start + 8, 8), :] = value
        return back[slot, j, pl.ds(start + 7, 8), :]

    def put_cell(ref, j, start, height, flow_x, flow_y):
        u, v, c, inverse = cell_terms(height, flow_x, flow_y)
        for k, value in enumerate((height, flow_x, flow_y, u, v, c, inverse)):
            ref[k, j, pl.ds(start, 8), :] = value

    def put_start(j, start, wet, height, flow_x, flow_y, rate):
        put_cell(
            state0, j, start,
            jnp.where(wet, height, 1.0), jnp.where(wet, flow_x, 0.0), jnp.where(wet, flow_y, 0.0),
        )
        mask[j, pl.ds(start, 8), :] = jnp.where(wet, 1.0, 0.0)
        weight[j, pl.ds(start, 8), :] = rate

    row_first = lax.axis_index("gx") * rows
    col_first = lax.axis_index("gy") * cols
    total_cols = cols * lax.axis_size("gy")

    def list_dam(d, count):
        cell = dam_ref[d]
        row = cell // total_cols
        col = cell - row * total_cols - col_first
        row = row - row_first
        near = (row >= -REACH) & (row < rows + REACH) & (col >= -REACH) & (col < cols + REACH)

        @pl.when(near)
        def _():
            place = jnp.where(col < 0, col + tiles * LANES, col)
            listed[0, count] = d
            listed[1, count] = row + EDGE
            listed[2, count] = place // LANES
            listed[3, count] = place % LANES
            inside = (row >= 0) & (row < rows) & (col >= 0) & (col < cols)
            listed[4, count] = jnp.where(inside, 1, 0)

        return count + jnp.where(near, 1, 0)

    dams = lax.fori_loop(0, dam_ref.shape[0], list_dam, 0)

    zero = jnp.zeros((8, LANES), jnp.float32)
    for j in every:
        for slot in range(back.shape[0]):
            back[slot, j, 0:8, :] = zero
        for ref in (state0, state1):
            for k in range(7):
                ref[k, j, pl.ds(chunks * 8, 8), :] = zero + (1.0 if k in (0, 5, 6) else 0.0)
        mask[j, pl.ds(chunks * 8, 8), :] = zero
        for k in range(3):
            lam[k, j, pl.ds(chunks * 8, 8), :] = zero

    def start_rows(i, carry):
        start = pl.multiple_of(i * 8, 8)
        for j in inner:
            part = pl.ds(j * LANES, LANES)
            wet = wet_ref[pl.ds(start, 8), part] > 0
            rate = jnp.where(wet, class_rate(class_ref[pl.ds(start, 8), part], rates_ref), 0.0)
            put_start(
                j, start + EDGE, wet,
                h_ref[pl.ds(start, 8), part], x_ref[pl.ds(start, 8), part], y_ref[pl.ds(start, 8), part], rate,
            )
        h, x, y, rate = (side_ref[k, pl.ds(start, 8), :] for k in range(FIELDS))
        put_start(tiles - 1, start + EDGE, h > 0.0, h, x, y, rate)
        return carry

    lax.fori_loop(0, rows // 8, start_rows, 0)
    blank = jnp.zeros((8 - REACH, LANES), jnp.float32)
    for j in every:
        part = slice(j * LANES, (j + 1) * LANES)
        above = [jnp.concatenate((blank, top_ref[k * REACH : (k + 1) * REACH, part]), axis=0) for k in range(FIELDS)]
        below = [jnp.concatenate((bottom_ref[k * REACH : (k + 1) * REACH, part], blank), axis=0) for k in range(FIELDS)]
        for start, (h, x, y, rate) in ((0, above), (rows + EDGE, below)):
            put_start(j, start, h > 0.0, h, x, y, rate)

    def add_inflow(step, ref, refresh):
        def one(index, carry):
            d, row, j, col = (listed[k, index] for k in range(4))
            if refresh:
                old = [ref[k, j, pl.ds(row, 1), :] for k in range(3)]
            else:
                old = [ref[j, pl.ds(row, 1), :]]
            here = lax.broadcasted_iota(jnp.int32, (1, LANES), 1) == col
            height = old[0] + jnp.where(here, INFLOW_GAIN * release_ref[d, step], 0.0)
            if refresh:
                terms = (height, old[1], old[2]) + cell_terms(height, old[1], old[2])
                for k, value in enumerate(terms):
                    ref[k, j, pl.ds(row, 1), :] = value
            else:
                ref[j, pl.ds(row, 1), :] = height
            return carry

        lax.fori_loop(0, dams, one, 0)

    def pick(step, gradient):
        lane_row = lax.broadcasted_iota(jnp.int32, (1, LANES), 1)

        def one(index, total):
            d, row, j, col, inside = (listed[k, index] for k in range(5))
            values = lam[0, j, pl.ds(row, 1), :]
            value = jnp.sum(jnp.where(lane_row == col, values, 0.0), axis=1, keepdims=True)
            spot = (lane_row == d + step * dam_ref.shape[0]) & (inside > 0)
            return total + jnp.where(spot, (INFLOW_GAIN / TIME_RATIO) * value, 0.0)

        return lax.fori_loop(0, dams, one, gradient)

    def first_step(i, carry):
        start = pl.multiple_of(i * 8, 8)
        low = [[at(state0, k, j, start) for j in every] for k in range(6)]
        h, x, y, u, v, c = low
        m = [mask[j, pl.ds(start, 8), :] for j in every]
        half = [(0.5 * GRAVITY) * h[j] * h[j] for j in every]
        cross = [x[j] * v[j] for j in every]
        press_x = [x[j] * u[j] + half[j] for j in every]
        press_y = [y[j] * v[j] + half[j] for j in every]
        gain = []
        for j in every:
            hn, xn, yn, un, cn = (at(state0, k, j, start + 1) for k in (0, 1, 2, 3, 5))
            both = m[j] * mask[j, pl.ds(start + 1, 8), :]
            faces[0, j, pl.ds(start, 8), :] = both
            _, _, _, wl, wh, sp, _, _ = waves(u[j], c[j], un, cn, both)
            fh = wl * x[j] + wh * xn + sp * (hn - h[j])
            fn = wl * press_x[j] + wh * (xn * un + (0.5 * GRAVITY) * hn * hn) + sp * (xn - x[j])
            ft = wl * cross[j] + wh * (yn * un) + sp * (yn - y[j])
            both_low = previous_row(0, j, start, both)
            tilt = both_low - both
            shut = 2.0 * m[j] - both - both_low
            walls[0, j, pl.ds(start, 8), :] = tilt
            walls[1, j, pl.ds(start, 8), :] = shut
            gain.append(
                [
                    fh - previous_row(1, j, start, fh),
                    fn - previous_row(2, j, start, fn) + tilt * press_x[j] + shut * ((jnp.abs(u[j]) + c[j]) * x[j]),
                    ft - previous_row(3, j, start, ft),
                ]
            )
        hn, xn, yn, vn, cn, pn, tn, mn = (next_col(q) for q in (h, x, y, v, c, press_y, cross, m))
        flux = [[], [], []]
        both_up = []
        for j in every:
            both = m[j] * mn[j]
            faces[1, j, pl.ds(start, 8), :] = both
            both_up.append(both)
            _, _, _, wl, wh, sp, _, _ = waves(v[j], c[j], vn[j], cn[j], both)
            flux[0].append(wl * y[j] + wh * yn[j] + sp * (hn[j] - h[j]))
            flux[1].append(wl * press_y[j] + wh * pn[j] + sp * (yn[j] - y[j]))
            flux[2].append(wl * cross[j] + wh * tn[j] + sp * (xn[j] - x[j]))
        flux_low = [previous_col(q) for q in flux]
        both_low = previous_col(both_up)
        for j in every:
            tilt = both_low[j] - both_up[j]
            shut = 2.0 * m[j] - both_up[j] - both_low[j]
            walls[2, j, pl.ds(start, 8), :] = tilt
            walls[3, j, pl.ds(start, 8), :] = shut
            change_h = gain[j][0] + (flux[0][j] - flux_low[0][j])
            change_x = gain[j][1] + (flux[2][j] - flux_low[2][j])
            change_y = gain[j][2] + (flux[1][j] - flux_low[1][j])
            change_y = change_y + tilt * press_y[j] + shut * ((jnp.abs(v[j]) + c[j]) * y[j])
            put_cell(
                state1, j, start,
                h[j] - TIME_RATIO * change_h, x[j] - TIME_RATIO * change_x, y[j] - TIME_RATIO * change_y,
            )
        return carry

    lax.fori_loop(0, chunks, first_step, 0)
    add_inflow(0, state1, True)

    def second_step(i, carry):
        start = pl.multiple_of(i * 8, 8)
        h, x, y, u, v, c = [[at(state1, k, j, start) for j in every] for k in range(6)]
        gain = []
        for j in every:
            hn, xn, un, cn = (at(state1, k, j, start + 1) for k in (0, 1, 3, 5))
            _, _, _, wl, wh, sp, _, _ = waves(u[j], c[j], un, cn, at(faces, 0, j, start))
            fh = wl * x[j] + wh * xn + sp * (hn - h[j])
            gain.append(fh - previous_row(0, j, start, fh))
        hn, yn, vn, cn = (next_col(q) for q in (h, y, v, c))
        flux = []
        for j in every:
            _, _, _, wl, wh, sp, _, _ = waves(v[j], c[j], vn[j], cn[j], at(faces, 1, j, start))
            flux.append(wl * y[j] + wh * yn[j] + sp * (hn[j] - h[j]))
        flux_low = previous_col(flux)
        for j in every:
            last[j, pl.ds(start, 8), :] = h[j] - TIME_RATIO * (gain[j] + (flux[j] - flux_low[j]))
        return carry

    lax.fori_loop(0, chunks, second_step, 0)
    add_inflow(1, last, False)

    def finish_depth(i, carry):
        start = pl.multiple_of(i * 8, 8)
        for j in every:
            height = last[j, pl.ds(start, 8), :]
            lam[0, j, pl.ds(start, 8), :] = TIME_RATIO * (weight[j, pl.ds(start, 8), :] * height)
        return carry

    lax.fori_loop(0, chunks, finish_depth, 0)

    def store_depth(i, carry):
        start = pl.multiple_of(i * 8, 8)
        for j in inner:
            part = pl.ds(j * LANES, LANES)
            height = last[j, pl.ds(start + EDGE, 8), :]
            depth_ref[pl.ds(start, 8), part] = jnp.where(
                wet_ref[pl.ds(start, 8), part] > 0, height, h_ref[pl.ds(start, 8), part]
            )
        return carry

    lax.fori_loop(0, rows // 8, store_depth, 0)
    gradient = pick(1, jnp.zeros((1, LANES), jnp.float32))

    def second_back(i, carry):
        start = pl.multiple_of(i * 8, 8)
        h, x, y, u, v, c, r = [[at(state1, k, j, start) for j in every] for k in range(7)]
        lh = [at(lam, 0, j, start) for j in every]

        def face(hl, nl, ul, cl, hh, nh, uh, ch, gl, gh, both):
            slow, fast, inv, wl, wh, sp, slow_low, fast_low = waves(ul, cl, uh, ch, both)
            g = gh - gl
            dn, dh = nh - nl, hh - hl
            to_low, to_high = wl * g, wh * g
            of_slow = -(to_low * inv) * (dn - fast * dh)
            of_fast = -(to_high * inv) * (dn - slow * dh)
            return (to_low, to_high, sp * g) + speed_terms(slow, fast, of_slow, of_fast, slow_low, fast_low)

        partial_h, partial_u, partial_c, flow = [], [], [], []
        for j in every:
            hn, xn, un, cn = (at(state1, k, j, start + 1) for k in (0, 1, 3, 5))
            to_low, to_high, jump, u_low, c_low, u_high, c_high = face(
                h[j], x[j], u[j], c[j], hn, xn, un, cn, lh[j], at(lam, 0, j, start + 1), at(faces, 0, j, start)
            )
            of_u = u_low + previous_row(2, j, start, u_high)
            partial_h.append(previous_row(0, j, start, jump) - jump)
            partial_c.append(c_low + previous_row(3, j, start, c_high))
            partial_u.append(of_u * u[j])
            flow.append(to_low + previous_row(1, j, start, to_high) + of_u * r[j])
        hn, yn, vn, cn, ln = (next_col(q) for q in (h, y, v, c, lh))
        terms = [
            face(h[j], y[j], v[j], c[j], hn[j], yn[j], vn[j], cn[j], lh[j], ln[j], at(faces, 1, j, start))
            for j in every
        ]
        high, jump, u_high, c_high = (previous_col([t[k] for t in terms]) for k in (1, 2, 5, 6))
        for j in every:
            to_low, _, own_jump, u_low, c_low, _, _ = terms[j]
            of_v = u_low + u_high[j]
            of_c = partial_c[j] + c_low + c_high[j]
            of_h = partial_h[j] + (jump[j] - own_jump)
            of_h = of_h + r[j] * (0.5 * (of_c * c[j]) - partial_u[j] - of_v * v[j])
            back[4, j, pl.ds(start + 8, 8), :] = lh[j] + TIME_RATIO * of_h
            lam[1, j, pl.ds(start, 8), :] = TIME_RATIO * flow[j]
            lam[2, j, pl.ds(start, 8), :] = TIME_RATIO * (to_low + high[j] + of_v * r[j])
        return carry

    lax.fori_loop(0, chunks, second_back, 0)

    def move_back(i, carry):
        start = pl.multiple_of(i * 8, 8)
        for j in every:
            lam[0, j, pl.ds(start, 8), :] = back[4, j, pl.ds(start + 8, 8), :]
        return carry

    lax.fori_loop(0, chunks, move_back, 0)
    gradient = pick(0, gradient)
    grad_ref[...] = jnp.broadcast_to(gradient, grad_ref.shape)

    def first_back(i, carry):
        start = pl.multiple_of(i * 8, 8)
        h, x, y, u, v, c, r = [[at(state0, k, j, start) for j in every] for k in range(7)]
        lh, lx, ly = [[at(lam, k, j, start) for j in every] for k in range(3)]
        half = [(0.5 * GRAVITY) * h[j] * h[j] for j in every]
        cross = [x[j] * v[j] for j in every]

        def face(hl, nl, tl, ul, cl, pl_, kl, hh, nh, th, uh, ch, ph, kh, gl, gh, both):
            slow, fast, inv, wl, wh, sp, slow_low, fast_low = waves(ul, cl, uh, ch, both)
            g_h, g_n, g_t = (b - a for a, b in zip(gl, gh))
            dn = nh - nl
            of_flux = g_h * dn + g_n * (ph - pl_) + g_t * (kh - kl)
            of_jump = g_h * (hh - hl) + g_n * dn + g_t * (th - tl)
            of_slow = -(wl * inv) * (of_flux - fast * of_jump)
            of_fast = -(wh * inv) * (of_flux - slow * of_jump)
            return (wl * g_n, wl * g_t, wh * g_n, wh * g_t, sp * g_h) + speed_terms(
                slow, fast, of_slow, of_fast, slow_low, fast_low
            )

        kept = []
        for j in every:
            hn, xn, yn, un, cn = (at(state0, k, j, start + 1) for k in (0, 1, 2, 3, 5))
            nl, tl, nh, th, jump, u_low, c_low, u_high, c_high = face(
                h[j], x[j], y[j], u[j], c[j], x[j] * u[j] + half[j], cross[j],
                hn, xn, yn, un, cn, xn * un + (0.5 * GRAVITY) * hn * hn, yn * un,
                (lh[j], lx[j], ly[j]), tuple(at(lam, k, j, start + 1) for k in range(3)), at(faces, 0, j, start),
            )
            shut = lx[j] * at(walls, 1, j, start)
            normal = nl + previous_row(0, j, start, nh) - lx[j] * at(walls, 0, j, start)
            across = tl + previous_row(1, j, start, th)
            of_u = normal * x[j] + across * y[j] + u_low + previous_row(3, j, start, u_high) - shut * jnp.abs(x[j])
            of_c = c_low + previous_row(4, j, start, c_high) - shut * x[j]
            kept.append((normal, previous_row(2, j, start, jump) - jump, of_u * u[j], of_c))
        press = [y[j] * v[j] + half[j] for j in every]
        hn, xn, yn, vn, cn, pn, kn = (next_col(q) for q in (h, x, y, v, c, press, cross))
        lhn, lxn, lyn = (next_col(q) for q in (lh, lx, ly))
        terms = [
            face(
                h[j], y[j], x[j], v[j], c[j], press[j], cross[j],
                hn[j], yn[j], xn[j], vn[j], cn[j], pn[j], kn[j],
                (lh[j], ly[j], lx[j]), (lhn[j], lyn[j], lxn[j]), at(faces, 1, j, start),
            )
            for j in every
        ]
        nh, th, jump, u_high, c_high = (previous_col([t[k] for t in terms]) for k in (2, 3, 4, 7, 8))
        for j in inner:
            shut = ly[j] * at(walls, 3, j, start)
            normal = terms[j][0] + nh[j] - ly[j] * at(walls, 2, j, start)
            across = terms[j][1] + th[j]
            of_v = normal * y[j] + across * x[j] + terms[j][5] + u_high[j] - shut * jnp.abs(y[j])
            of_c = kept[j][3] + terms[j][6] + c_high[j] - shut * y[j]
            of_h = kept[j][1] + (jump[j] - terms[j][4]) + GRAVITY * h[j] * (kept[j][0] + normal)
            of_h = of_h + r[j] * (0.5 * (of_c * c[j]) - kept[j][2] - of_v * v[j])
            result = (1.0 / TIME_RATIO) * lh[j] + of_h

            @pl.when(i > 0)
            def _():
                adjoint_ref[pl.ds(pl.multiple_of(jnp.maximum(start - EDGE, 0), 8), 8), pl.ds(j * LANES, LANES)] = result

        return carry

    lax.fori_loop(0, chunks - 1, first_back, 0)


def on_device(
    water_depth, momentum_x, momentum_y, wet_mask, damage_class, damage_rates, dam_cell, releases
):
    rows, cols = water_depth.shape
    wide = cols + LANES
    rows_count = lax.axis_size("gx")
    cols_count = lax.axis_size("gy")
    tiles = wide // LANES
    tall = rows + 2 * EDGE + 8
    vmem = pl.BlockSpec(memory_space=pltpu.VMEM)
    smem = pl.BlockSpec(memory_space=pltpu.SMEM)
    f32 = jnp.float32
    params = pltpu.CompilerParams(vmem_limit_bytes=48 * 1024 * 1024)
    local = (water_depth, momentum_x, momentum_y, wet_mask, damage_class, damage_rates)

    def shift(value, axis, count, step):
        pairs = [(i, i + step) for i in range(count) if 0 <= i + step < count]
        return lax.ppermute(value, axis, pairs)

    low, high = pl.pallas_call(
        edge_columns_kernel,
        out_shape=[jax.ShapeDtypeStruct((STRIP, rows), f32)] * 2,
        in_specs=[vmem] * 5 + [smem],
        out_specs=[vmem] * 2,
        compiler_params=params,
        name="edge_columns",
    )(*local)
    right = shift(low, "gy", cols_count, -1)
    left = shift(high, "gy", cols_count, 1)
    side, low, high = pl.pallas_call(
        edge_rows_kernel,
        out_shape=[
            jax.ShapeDtypeStruct((FIELDS, rows, LANES), f32),
            jax.ShapeDtypeStruct((STRIP, wide), f32),
            jax.ShapeDtypeStruct((STRIP, wide), f32),
        ],
        in_specs=[vmem] * 5 + [smem] + [vmem] * 2,
        out_specs=[vmem] * 3,
        compiler_params=params,
        name="edge_rows",
    )(*local, left, right)
    bottom = shift(low, "gx", rows_count, -1)
    top = shift(high, "gx", rows_count, 1)

    def cells(*lead):
        return pltpu.VMEM(lead + (tiles, tall, LANES), f32)

    devices = rows_count * cols_count
    depth, adjoint, parts = pl.pallas_call(
        window_kernel,
        out_shape=[
            jax.ShapeDtypeStruct((rows, cols), f32),
            jax.ShapeDtypeStruct((rows, cols), f32),
            jax.ShapeDtypeStruct((devices, LANES), f32),
        ],
        in_specs=[vmem] * 5 + [smem] + [vmem] * 3 + [smem] * 2,
        out_specs=[vmem] * 3,
        scratch_shapes=[
            cells(7), cells(7), cells(), cells(2), cells(4), cells(), cells(), cells(3), cells(5),
            pltpu.SMEM((5, dam_cell.shape[0]), jnp.int32),
        ],
        compiler_params=params,
        name="window",
    )(*local, side, top, bottom, dam_cell, releases)
    gathered = lax.all_to_all(parts, ("gx", "gy"), 0, 0)
    release_grad = jnp.sum(gathered, axis=0).reshape(releases.shape[1], releases.shape[0]).T
    return (depth, adjoint, release_grad)


def solution(mesh):
    in_specs = (P("gx", "gy"),) * 5 + (P(), P(), P())
    out_specs = (P("gx", "gy"), P("gx", "gy"), P())
    return jax.shard_map(
        on_device, mesh=mesh, in_specs=in_specs, out_specs=out_specs, check_vma=False
    )
```

```python
import jax
import jax.numpy as jnp
from jax import lax
from jax.experimental import pallas as pl
from jax.experimental.pallas import tpu as pltpu
from jax.sharding import PartitionSpec as P

GRAVITY = 9.81
TIME_RATIO = 0.05
INFLOW_GAIN = 0.25

LANES = 128
REACH = 4
EDGE = 8
FIELDS = 4
STRIP = FIELDS * REACH
UNROLL = True


def class_rate(classes, rates_ref):
    rate = jnp.full(classes.shape, rates_ref[0], jnp.float32)
    for index in range(1, rates_ref.shape[0]):
        rate = jnp.where(classes == index, rates_ref[index], rate)
    return rate


def coded_fields(h, x, y, wet, classes):
    return jnp.where(wet > 0, h, 0.0), x, y, classes.astype(jnp.float32)


def edge_kernel(h_hbm, x_hbm, y_hbm, wet_hbm, class_hbm, low_ref, high_ref, values, codes, sems):
    rows, cols = h_hbm.shape
    copies = []
    for index, source in enumerate((h_hbm, x_hbm, y_hbm, wet_hbm, class_hbm)):
        for side in range(2):
            kept = values.at[side, index] if index < 3 else codes.at[side, index - 3]
            part = source.at[:, pl.ds(side * (cols - LANES), LANES)]
            copies.append(pltpu.make_async_copy(part, kept, sems.at[side, index]))
    for copy in copies:
        copy.start()
    for copy in copies:
        copy.wait()
    lane = lax.broadcasted_iota(jnp.int32, (rows, LANES), 1)
    mixed = jnp.zeros((rows, LANES), jnp.float32)
    for side in range(2):
        fields = coded_fields(*(values[side, k] for k in range(3)), *(codes[side, k] for k in range(2)))
        for index, field in enumerate(fields):
            first = (side * FIELDS + index) * EDGE
            moved = first if side == 0 else first + EDGE
            shifted = pltpu.roll(field, moved, 1) if moved else field
            mixed = jnp.where((lane >= first) & (lane < first + EDGE), shifted, mixed)
    turned = mixed.T
    low_ref[...] = turned[: FIELDS * EDGE]
    high_ref[...] = turned[FIELDS * EDGE : 2 * FIELDS * EDGE]


def beside(left_ref, right_ref):
    place = lax.axis_index("gy")
    left = jnp.where(place > 0, left_ref[...], 0.0)
    right = jnp.where(place < lax.axis_size("gy") - 1, right_ref[...], 0.0)
    return left, right


def corner_kernel(h_ref, x_ref, y_ref, wet_ref, class_ref, left_ref, right_ref, side_ref, low_ref, high_ref):
    rows, cols = h_ref.shape
    left, right = beside(left_ref, right_ref)
    blank = jnp.zeros((LANES - 2 * FIELDS * EDGE, rows), jnp.float32)
    turned = jnp.concatenate((right, left, blank), axis=0).T
    lane = lax.broadcasted_iota(jnp.int32, (EDGE, LANES), 1)
    for end, (ref, start, kept) in enumerate(((low_ref, 0, 0), (high_ref, rows - EDGE, EDGE - REACH))):
        part = slice(start, start + EDGE)
        own = coded_fields(h_ref[part, :], x_ref[part, :], y_ref[part, :], wet_ref[part, :], class_ref[part, :])
        for index in range(FIELDS):
            upper = pltpu.roll(turned[part], (LANES - index * EDGE) % LANES, 1) if index else turned[part]
            lower = pltpu.roll(turned[part], LANES - (1 + FIELDS + index) * EDGE, 1)
            tile = jnp.where(lane < EDGE, upper, jnp.where(lane >= LANES - EDGE, lower, 0.0))
            side_ref[end, index] = tile
            place = slice(index * REACH, (index + 1) * REACH)
            ref[place, cols:] = tile[kept : kept + REACH]
            ref[place, :cols] = own[index][kept : kept + REACH]


def cell_terms(height, flow_x, flow_y):
    scaled = GRAVITY * height
    inverse = pltpu.reciprocal(height, approx=True)
    return flow_x * inverse, flow_y * inverse, scaled * lax.rsqrt(scaled), inverse


def waves(u_low, c_low, u_high, c_high, both):
    slow_low, slow_high = u_low - c_low, u_high - c_high
    fast_low, fast_high = u_low + c_low, u_high + c_high
    slowest = jnp.minimum(jnp.minimum(slow_low, slow_high), 0.0)
    fastest = jnp.maximum(jnp.maximum(fast_low, fast_high), 0.0)
    inverse = both * pltpu.reciprocal(fastest - slowest, approx=True)
    share_low = fastest * inverse
    share_high = -(slowest * inverse)
    spread = slowest * share_low
    return slowest, fastest, inverse, share_low, share_high, spread, slow_low <= slow_high, fast_low >= fast_high


def speed_terms(slowest, fastest, of_slowest, of_fastest, slow_is_low, fast_is_low):
    of_slowest = jnp.where(slowest < 0.0, of_slowest, 0.0)
    of_fastest = jnp.where(fastest > 0.0, of_fastest, 0.0)
    slow_to_low = jnp.where(slow_is_low, of_slowest, 0.0)
    fast_to_low = jnp.where(fast_is_low, of_fastest, 0.0)
    slow_to_high = of_slowest - slow_to_low
    fast_to_high = of_fastest - fast_to_low
    return (
        fast_to_low + slow_to_low,
        fast_to_low - slow_to_low,
        fast_to_high + slow_to_high,
        fast_to_high - slow_to_high,
    )


def window(chunks, after, before, put, rates_ref, listed, dams, release_ref, scratch):
    state0, state1, mask, faces, walls, weight, last, lam, back, final = scratch
    tiles = len(after)
    every = range(tiles)
    lane = lax.broadcasted_iota(jnp.int32, (8, LANES), 1)

    def at(ref, k, j, start):
        return ref[k, j, pl.ds(start, 8), :]

    def next_col(values):
        rolled = [pltpu.roll(v, LANES - 1, 1) for v in values]
        return [jnp.where(lane == LANES - 1, rolled[after[j]], rolled[j]) for j in every]

    def previous_col(values):
        rolled = [pltpu.roll(v, 1, 1) for v in values]
        return [jnp.where(lane == 0, rolled[before[j]], rolled[j]) for j in every]

    def previous_row(slot, j, start, value):
        back[slot, j, pl.ds(start + 8, 8), :] = value
        return back[slot, j, pl.ds(start + 7, 8), :]

    def put_cell(ref, j, start, height, flow_x, flow_y):
        u, v, c, inverse = cell_terms(height, flow_x, flow_y)
        for k, value in enumerate((height, flow_x, flow_y, u, v, c, inverse)):
            ref[k, j, pl.ds(start, 8), :] = value

    def fill(j, start, wet, height, flow_x, flow_y, classes):
        put_cell(
            state0, j, start,
            jnp.where(wet, height, 1.0), jnp.where(wet, flow_x, 0.0), jnp.where(wet, flow_y, 0.0),
        )
        mask[j, pl.ds(start, 8), :] = jnp.where(wet, 1.0, 0.0)
        weight[j, pl.ds(start, 8), :] = jnp.where(wet, class_rate(classes, rates_ref), 0.0)

    zero = jnp.zeros((8, LANES), jnp.float32)
    for j in every:
        for slot in range(back.shape[0]):
            back[slot, j, 0:8, :] = zero
        for ref in (state0, state1):
            for k in range(7):
                ref[k, j, pl.ds(chunks * 8, 8), :] = zero + (1.0 if k in (0, 5, 6) else 0.0)
        mask[j, pl.ds(chunks * 8, 8), :] = zero
        for k in range(3):
            lam[k, j, pl.ds(chunks * 8, 8), :] = zero
    put(fill)

    def run(step):
        lax.fori_loop(0, chunks, step, 0, unroll=UNROLL)

    def add_inflow(step, ref, refresh):
        def one(index, carry):
            d, row, j, col = (listed[k, index] for k in range(4))
            if refresh:
                old = [ref[k, j, pl.ds(row, 1), :] for k in range(3)]
            else:
                old = [ref[j, pl.ds(row, 1), :]]
            here = lax.broadcasted_iota(jnp.int32, (1, LANES), 1) == col
            height = old[0] + jnp.where(here, INFLOW_GAIN * release_ref[d, step], 0.0)
            if refresh:
                terms = (height, old[1], old[2]) + cell_terms(height, old[1], old[2])
                for k, value in enumerate(terms):
                    ref[k, j, pl.ds(row, 1), :] = value
            else:
                ref[j, pl.ds(row, 1), :] = height
            return carry

        lax.fori_loop(0, dams, one, 0)

    def pick(step, gradient):
        lane_row = lax.broadcasted_iota(jnp.int32, (1, LANES), 1)

        def one(index, total):
            d, row, j, col, inside = (listed[k, index] for k in range(5))
            values = lam[0, j, pl.ds(row, 1), :]
            value = jnp.sum(jnp.where(lane_row == col, values, 0.0), axis=1, keepdims=True)
            spot = (lane_row == d + step * release_ref.shape[0]) & (inside > 0)
            return total + jnp.where(spot, (INFLOW_GAIN / TIME_RATIO) * value, 0.0)

        return lax.fori_loop(0, dams, one, gradient)

    def first_step(i, carry):
        start = pl.multiple_of(i * 8, 8)
        low = [[at(state0, k, j, start) for j in every] for k in range(6)]
        h, x, y, u, v, c = low
        m = [mask[j, pl.ds(start, 8), :] for j in every]
        half = [(0.5 * GRAVITY) * h[j] * h[j] for j in every]
        cross = [x[j] * v[j] for j in every]
        press_x = [x[j] * u[j] + half[j] for j in every]
        press_y = [y[j] * v[j] + half[j] for j in every]
        gain = []
        for j in every:
            hn, xn, yn, un, cn = (at(state0, k, j, start + 1) for k in (0, 1, 2, 3, 5))
            both = m[j] * mask[j, pl.ds(start + 1, 8), :]
            faces[0, j, pl.ds(start, 8), :] = both
            _, _, _, wl, wh, sp, _, _ = waves(u[j], c[j], un, cn, both)
            fh = wl * x[j] + wh * xn + sp * (hn - h[j])
            fn = wl * press_x[j] + wh * (xn * un + (0.5 * GRAVITY) * hn * hn) + sp * (xn - x[j])
            ft = wl * cross[j] + wh * (yn * un) + sp * (yn - y[j])
            both_low = previous_row(0, j, start, both)
            tilt = both_low - both
            shut = 2.0 * m[j] - both - both_low
            walls[0, j, pl.ds(start, 8), :] = tilt
            walls[1, j, pl.ds(start, 8), :] = shut
            gain.append(
                [
                    fh - previous_row(1, j, start, fh),
                    fn - previous_row(2, j, start, fn) + tilt * press_x[j] + shut * ((jnp.abs(u[j]) + c[j]) * x[j]),
                    ft - previous_row(3, j, start, ft),
                ]
            )
        hn, xn, yn, vn, cn, pn, tn, mn = (next_col(q) for q in (h, x, y, v, c, press_y, cross, m))
        flux = [[], [], []]
        both_up = []
        for j in every:
            both = m[j] * mn[j]
            faces[1, j, pl.ds(start, 8), :] = both
            both_up.append(both)
            _, _, _, wl, wh, sp, _, _ = waves(v[j], c[j], vn[j], cn[j], both)
            flux[0].append(wl * y[j] + wh * yn[j] + sp * (hn[j] - h[j]))
            flux[1].append(wl * press_y[j] + wh * pn[j] + sp * (yn[j] - y[j]))
            flux[2].append(wl * cross[j] + wh * tn[j] + sp * (xn[j] - x[j]))
        flux_low = [previous_col(q) for q in flux]
        both_low = previous_col(both_up)
        for j in every:
            tilt = both_low[j] - both_up[j]
            shut = 2.0 * m[j] - both_up[j] - both_low[j]
            walls[2, j, pl.ds(start, 8), :] = tilt
            walls[3, j, pl.ds(start, 8), :] = shut
            change_h = gain[j][0] + (flux[0][j] - flux_low[0][j])
            change_x = gain[j][1] + (flux[2][j] - flux_low[2][j])
            change_y = gain[j][2] + (flux[1][j] - flux_low[1][j])
            change_y = change_y + tilt * press_y[j] + shut * ((jnp.abs(v[j]) + c[j]) * y[j])
            put_cell(
                state1, j, start,
                h[j] - TIME_RATIO * change_h, x[j] - TIME_RATIO * change_x, y[j] - TIME_RATIO * change_y,
            )
        return carry

    run(first_step)
    add_inflow(0, state1, True)

    def second_step(i, carry):
        start = pl.multiple_of(i * 8, 8)
        h, x, y, u, v, c = [[at(state1, k, j, start) for j in every] for k in range(6)]
        gain = []
        for j in every:
            hn, xn, un, cn = (at(state1, k, j, start + 1) for k in (0, 1, 3, 5))
            _, _, _, wl, wh, sp, _, _ = waves(u[j], c[j], un, cn, at(faces, 0, j, start))
            fh = wl * x[j] + wh * xn + sp * (hn - h[j])
            gain.append(fh - previous_row(0, j, start, fh))
        hn, yn, vn, cn = (next_col(q) for q in (h, y, v, c))
        flux = []
        for j in every:
            _, _, _, wl, wh, sp, _, _ = waves(v[j], c[j], vn[j], cn[j], at(faces, 1, j, start))
            flux.append(wl * y[j] + wh * yn[j] + sp * (hn[j] - h[j]))
        flux_low = previous_col(flux)
        for j in every:
            last[j, pl.ds(start, 8), :] = h[j] - TIME_RATIO * (gain[j] + (flux[j] - flux_low[j]))
        return carry

    run(second_step)
    add_inflow(1, last, False)

    def finish_depth(i, carry):
        start = pl.multiple_of(i * 8, 8)
        for j in every:
            height = last[j, pl.ds(start, 8), :]
            lam[0, j, pl.ds(start, 8), :] = TIME_RATIO * (weight[j, pl.ds(start, 8), :] * height)
        return carry

    run(finish_depth)

    gradient = pick(1, jnp.zeros((1, LANES), jnp.float32))

    def second_back(i, carry):
        start = pl.multiple_of(i * 8, 8)
        h, x, y, u, v, c, r = [[at(state1, k, j, start) for j in every] for k in range(7)]
        lh = [at(lam, 0, j, start) for j in every]

        def face(hl, nl, ul, cl, hh, nh, uh, ch, gl, gh, both):
            slow, fast, inv, wl, wh, sp, slow_low, fast_low = waves(ul, cl, uh, ch, both)
            g = gh - gl
            dn, dh = nh - nl, hh - hl
            to_low, to_high = wl * g, wh * g
            of_slow = -(to_low * inv) * (dn - fast * dh)
            of_fast = -(to_high * inv) * (dn - slow * dh)
            return (to_low, to_high, sp * g) + speed_terms(slow, fast, of_slow, of_fast, slow_low, fast_low)

        partial_h, partial_u, partial_c, flow = [], [], [], []
        for j in every:
            hn, xn, un, cn = (at(state1, k, j, start + 1) for k in (0, 1, 3, 5))
            to_low, to_high, jump, u_low, c_low, u_high, c_high = face(
                h[j], x[j], u[j], c[j], hn, xn, un, cn, lh[j], at(lam, 0, j, start + 1), at(faces, 0, j, start)
            )
            of_u = u_low + previous_row(2, j, start, u_high)
            partial_h.append(previous_row(0, j, start, jump) - jump)
            partial_c.append(c_low + previous_row(3, j, start, c_high))
            partial_u.append(of_u * u[j])
            flow.append(to_low + previous_row(1, j, start, to_high) + of_u * r[j])
        hn, yn, vn, cn, ln = (next_col(q) for q in (h, y, v, c, lh))
        terms = [
            face(h[j], y[j], v[j], c[j], hn[j], yn[j], vn[j], cn[j], lh[j], ln[j], at(faces, 1, j, start))
            for j in every
        ]
        high, jump, u_high, c_high = (previous_col([t[k] for t in terms]) for k in (1, 2, 5, 6))
        for j in every:
            to_low, _, own_jump, u_low, c_low, _, _ = terms[j]
            of_v = u_low + u_high[j]
            of_c = partial_c[j] + c_low + c_high[j]
            of_h = partial_h[j] + (jump[j] - own_jump)
            of_h = of_h + r[j] * (0.5 * (of_c * c[j]) - partial_u[j] - of_v * v[j])
            back[4, j, pl.ds(start + 8, 8), :] = lh[j] + TIME_RATIO * of_h
            lam[1, j, pl.ds(start, 8), :] = TIME_RATIO * flow[j]
            lam[2, j, pl.ds(start, 8), :] = TIME_RATIO * (to_low + high[j] + of_v * r[j])
        return carry

    run(second_back)

    def move_back(i, carry):
        start = pl.multiple_of(i * 8, 8)
        for j in every:
            lam[0, j, pl.ds(start, 8), :] = back[4, j, pl.ds(start + 8, 8), :]
        return carry

    run(move_back)
    gradient = pick(0, gradient)

    def first_back(i, carry):
        start = pl.multiple_of(i * 8, 8)
        h, x, y, u, v, c, r = [[at(state0, k, j, start) for j in every] for k in range(7)]
        lh, lx, ly = [[at(lam, k, j, start) for j in every] for k in range(3)]
        half = [(0.5 * GRAVITY) * h[j] * h[j] for j in every]
        cross = [x[j] * v[j] for j in every]

        def face(hl, nl, tl, ul, cl, pl_, kl, hh, nh, th, uh, ch, ph, kh, gl, gh, both):
            slow, fast, inv, wl, wh, sp, slow_low, fast_low = waves(ul, cl, uh, ch, both)
            g_h, g_n, g_t = (b - a for a, b in zip(gl, gh))
            dn = nh - nl
            of_flux = g_h * dn + g_n * (ph - pl_) + g_t * (kh - kl)
            of_jump = g_h * (hh - hl) + g_n * dn + g_t * (th - tl)
            of_slow = -(wl * inv) * (of_flux - fast * of_jump)
            of_fast = -(wh * inv) * (of_flux - slow * of_jump)
            return (wl * g_n, wl * g_t, wh * g_n, wh * g_t, sp * g_h) + speed_terms(
                slow, fast, of_slow, of_fast, slow_low, fast_low
            )

        kept = []
        for j in every:
            hn, xn, yn, un, cn = (at(state0, k, j, start + 1) for k in (0, 1, 2, 3, 5))
            nl, tl, nh, th, jump, u_low, c_low, u_high, c_high = face(
                h[j], x[j], y[j], u[j], c[j], x[j] * u[j] + half[j], cross[j],
                hn, xn, yn, un, cn, xn * un + (0.5 * GRAVITY) * hn * hn, yn * un,
                (lh[j], lx[j], ly[j]), tuple(at(lam, k, j, start + 1) for k in range(3)), at(faces, 0, j, start),
            )
            shut = lx[j] * at(walls, 1, j, start)
            normal = nl + previous_row(0, j, start, nh) - lx[j] * at(walls, 0, j, start)
            across = tl + previous_row(1, j, start, th)
            of_u = normal * x[j] + across * y[j] + u_low + previous_row(3, j, start, u_high) - shut * jnp.abs(x[j])
            of_c = c_low + previous_row(4, j, start, c_high) - shut * x[j]
            kept.append((normal, previous_row(2, j, start, jump) - jump, of_u * u[j], of_c))
        press = [y[j] * v[j] + half[j] for j in every]
        hn, xn, yn, vn, cn, pn, kn = (next_col(q) for q in (h, x, y, v, c, press, cross))
        lhn, lxn, lyn = (next_col(q) for q in (lh, lx, ly))
        terms = [
            face(
                h[j], y[j], x[j], v[j], c[j], press[j], cross[j],
                hn[j], yn[j], xn[j], vn[j], cn[j], pn[j], kn[j],
                (lh[j], ly[j], lx[j]), (lhn[j], lyn[j], lxn[j]), at(faces, 1, j, start),
            )
            for j in every
        ]
        nh, th, jump, u_high, c_high = (previous_col([t[k] for t in terms]) for k in (2, 3, 4, 7, 8))
        for j in every:
            shut = ly[j] * at(walls, 3, j, start)
            normal = terms[j][0] + nh[j] - ly[j] * at(walls, 2, j, start)
            across = terms[j][1] + th[j]
            of_v = normal * y[j] + across * x[j] + terms[j][5] + u_high[j] - shut * jnp.abs(y[j])
            of_c = kept[j][3] + terms[j][6] + c_high[j] - shut * y[j]
            of_h = kept[j][1] + (jump[j] - terms[j][4]) + GRAVITY * h[j] * (kept[j][0] + normal)
            of_h = of_h + r[j] * (0.5 * (of_c * c[j]) - kept[j][2] - of_v * v[j])
            final[j, pl.ds(start, 8), :] = (1.0 / TIME_RATIO) * lh[j] + of_h
        return carry

    run(first_back)
    return gradient


def list_dams(dam_ref, listed, rows, cols, spots):
    total_cols = cols * lax.axis_size("gy")
    row_first = lax.axis_index("gx") * rows
    col_first = lax.axis_index("gy") * cols

    def one(d, count):
        cell = dam_ref[d]
        row = lax.div(cell, jnp.int32(total_cols))
        col = cell - row * total_cols - col_first
        row = row - row_first
        for held, spot in spots(row, col):
            @pl.when(held)
            def _():
                for k, value in enumerate((d,) + spot):
                    listed[k, count] = value

            count = count + jnp.where(held, 1, 0)
        return count

    return lax.fori_loop(0, dam_ref.shape[0], one, 0, unroll=4)


def within(value, first, end):
    return (value >= first) & (value < end)


def split(place):
    return lax.shift_right_logical(place, LANES.bit_length() - 1), place & (LANES - 1)


def inner_kernel(
    h_ref, x_ref, y_ref, wet_ref, class_ref, rates_ref, dam_ref, release_ref,
    depth_ref, adjoint_ref, grad_ref, listed, *scratch,
):
    rows, cols = h_ref.shape
    tiles = cols // LANES
    chunks = rows // 8

    def spots(row, col):
        tile, lane = split(col)
        own = within(row, REACH, rows - REACH) & within(col, REACH, cols - REACH)
        yield within(row, 0, rows) & within(col, 0, cols), (row, tile, lane, jnp.where(own, 1, 0))

    dams = list_dams(dam_ref, listed, rows, cols, spots)

    def put(fill):
        def one(i, carry):
            part = pl.ds(pl.multiple_of(i * 8, 8), 8)
            for j in range(tiles):
                across = pl.ds(j * LANES, LANES)
                fill(
                    j, pl.multiple_of(i * 8, 8), wet_ref[part, across] > 0,
                    h_ref[part, across], x_ref[part, across], y_ref[part, across], class_ref[part, across],
                )
            return carry

        lax.fori_loop(0, chunks, one, 0, unroll=2)

    after = [(j + 1) % tiles for j in range(tiles)]
    before = [(j - 1) % tiles for j in range(tiles)]
    grad_ref[...] = window(chunks, after, before, put, rates_ref, listed, dams, release_ref, scratch)
    last, final = scratch[6], scratch[9]
    for j in range(tiles):
        across = slice(j * LANES, (j + 1) * LANES)
        depth_ref[:, across] = jnp.where(wet_ref[:, across] > 0, last[j, :rows, :], h_ref[:, across])
        adjoint_ref[:, across] = final[j, :rows, :]


def frame_kernel(
    h_ref, x_ref, y_ref, wet_ref, class_ref, rates_ref, dam_ref, release_ref,
    depth_in, adjoint_in, grad_in, low_ref, high_ref, left_ref, right_ref, side_ref, top_ref, bottom_ref,
    depth_ref, adjoint_ref, grad_ref, listed, *scratch,
):
    rows, cols = h_ref.shape
    tiles = cols // LANES
    chunks = 4
    turned = tiles + 1
    after = [(j + 1) % turned for j in range(turned)] + [turned + 1, turned]
    before = [(j - 1) % turned for j in range(turned)] + [turned + 1, turned]

    def chunk_row(place, count):
        return jnp.where(place < EDGE, place + EDGE, place - count + 3 * EDGE)

    def near_end(place, count):
        return within(place, -REACH, EDGE) | within(place, count - EDGE, count + REACH)

    def at_end(place, count):
        return within(place, 0, REACH) | within(place, count - REACH, count)

    def spots(row, col):
        near = within(row, -REACH, rows + REACH) & within(col, -REACH, cols + REACH)
        tile, lane = split(jnp.where(col < 0, col + (tiles + 1) * LANES, col))
        own = at_end(row, rows) & within(col, 0, cols)
        yield near & near_end(row, rows), (chunk_row(row, rows), tile, lane, jnp.where(own, 1, 0))
        tile, lane = split(jnp.where(row < 0, row + 2 * LANES, row))
        own = at_end(col, cols) & within(row, REACH, rows - REACH)
        yield near & near_end(col, cols), (chunk_row(col, cols), tile + turned, lane, jnp.where(own, 1, 0))

    dams = list_dams(dam_ref, listed, rows, cols, spots)
    place = lax.axis_index("gx")
    above = jnp.where(place > 0, top_ref[...], 0.0)
    below = jnp.where(place < lax.axis_size("gx") - 1, bottom_ref[...], 0.0)
    left, right = beside(left_ref, right_ref)

    def put(fill):
        blank = jnp.zeros((EDGE - REACH, LANES), jnp.float32)

        def coded(j, start, h, x, y, code):
            fill(j, start, h > 0.0, h, x, y, code.astype(jnp.int32))

        for j in range(tiles + 1):
            across = slice(j * LANES, (j + 1) * LANES)
            for start, strip in ((0, above), (3 * EDGE, below)):
                pieces = [strip[k * REACH : (k + 1) * REACH, across] for k in range(FIELDS)]
                coded(j, start, *(jnp.concatenate((blank, v) if start == 0 else (v, blank), axis=0) for v in pieces))
            for end, first in ((0, 0), (1, rows - EDGE)):
                start = (1 + end) * EDGE
                if j < tiles:
                    part = slice(first, first + EDGE)
                    fill(
                        j, start, wet_ref[part, across] > 0,
                        h_ref[part, across], x_ref[part, across], y_ref[part, across], class_ref[part, across],
                    )
                else:
                    coded(j, start, *(side_ref[end, k] for k in range(FIELDS)))
        order = (0, 2, 1, 3)
        for chunk, strip in enumerate((left, low_ref[...], high_ref[...], right)):
            coded(turned, chunk * EDGE, *(strip[k * EDGE : (k + 1) * EDGE] for k in order))
        strips = jnp.concatenate((above, below), axis=0)
        outer = strips[:, tiles * LANES :]
        mixed = jnp.zeros((2 * STRIP, LANES), jnp.float32)
        lane = lax.broadcasted_iota(jnp.int32, (2 * STRIP, LANES), 1)
        pieces = (
            (outer, LANES - EDGE),
            (strips[:, :LANES], 0),
            (strips[:, (tiles - 1) * LANES : tiles * LANES], LANES - EDGE),
            (outer, 0),
        )
        for chunk, (piece, first) in enumerate(pieces):
            moved = (chunk * EDGE - first) % LANES
            mixed = jnp.where(lane // EDGE == chunk, pltpu.roll(piece, moved, 1) if moved else piece, mixed)
        corners = jnp.concatenate((mixed, jnp.zeros((LANES - 2 * STRIP, LANES), jnp.float32)), axis=0).T
        corners = corners[: chunks * EDGE]
        lane = lax.broadcasted_iota(jnp.int32, (chunks * EDGE, LANES), 1)
        fields = []
        for k in order:
            from_above = pltpu.roll(corners, LANES - REACH - k * REACH, 1)
            from_below = pltpu.roll(corners, LANES - STRIP - k * REACH, 1)
            fields.append(jnp.where(lane < REACH, from_below, jnp.where(lane >= LANES - REACH, from_above, 0.0)))
        for chunk in range(chunks):
            coded(turned + 1, chunk * EDGE, *(v[chunk * EDGE : (chunk + 1) * EDGE] for v in fields))

    gradient = window(chunks, after, before, put, rates_ref, listed, dams, release_ref, scratch)
    grad_ref[...] = jnp.broadcast_to(gradient + grad_in[...], grad_ref.shape)

    last, final = scratch[6], scratch[9]
    blank = jnp.zeros((LANES - 4 * EDGE, LANES), jnp.float32)
    ends = slice(EDGE, 3 * EDGE)
    columns = jnp.concatenate((last[turned, ends, :], final[turned, ends, :], blank), axis=0).T
    lane = lax.broadcasted_iota(jnp.int32, (rows, LANES), 1)
    row = lax.broadcasted_iota(jnp.int32, (EDGE, LANES), 0)
    for number, (ref, inner, strip) in enumerate(((depth_ref, depth_in, last), (adjoint_ref, adjoint_in, final))):
        for j in range(tiles):
            across = slice(j * LANES, (j + 1) * LANES)

            def wet_only(value, part):
                if number:
                    return value
                return jnp.where(wet_ref[part, across] > 0, value, h_ref[part, across])

            whole = slice(0, rows)
            block = inner[:, across]
            if j == 0:
                moved = (LANES - 2 * EDGE * number) % LANES
                edge = pltpu.roll(columns, moved, 1) if moved else columns
                block = jnp.where(lane < REACH, wet_only(edge, whole), block)
            if j == tiles - 1:
                edge = pltpu.roll(columns, LANES - 2 * EDGE - 2 * EDGE * number, 1)
                block = jnp.where(lane >= LANES - REACH, wet_only(edge, whole), block)
            middle = slice(EDGE, rows - EDGE)
            ref[middle, across] = block[middle]
            for part, start, own in (
                (slice(0, EDGE), EDGE, row < REACH),
                (slice(rows - EDGE, rows), 2 * EDGE, row >= EDGE - REACH),
            ):
                ref[part, across] = jnp.where(own, wet_only(strip[j, start : start + EDGE, :], part), block[part])


def on_device(
    water_depth, momentum_x, momentum_y, wet_mask, damage_class, damage_rates, dam_cell, releases
):
    rows, cols = water_depth.shape
    tiles = cols // LANES
    wide = cols + LANES
    rows_count = lax.axis_size("gx")
    cols_count = lax.axis_size("gy")
    vmem = pl.BlockSpec(memory_space=pltpu.VMEM)
    smem = pl.BlockSpec(memory_space=pltpu.SMEM)
    hbm = pl.BlockSpec(memory_space=pltpu.HBM)
    f32 = jnp.float32
    params = pltpu.CompilerParams(vmem_limit_bytes=48 * 1024 * 1024)
    local = (water_depth, momentum_x, momentum_y, wet_mask, damage_class)
    given = (damage_rates, dam_cell, releases)

    def shift(value, axis, count, step):
        return lax.ppermute(value, axis, [(i, (i + step) % count) for i in range(count)])

    def array(*shape):
        return jax.ShapeDtypeStruct(shape, f32)

    def scratch(tiles, chunks, spots):
        def cells(*lead):
            return pltpu.VMEM(lead + (tiles, 8 * chunks + 8, LANES), f32)

        listed = pltpu.SMEM((5, spots), jnp.int32)
        return [listed, cells(7), cells(7), cells(), cells(2), cells(4), cells(), cells(), cells(3), cells(5), cells()]

    low, high = pl.pallas_call(
        edge_kernel,
        out_shape=[array(FIELDS * EDGE, rows)] * 2,
        in_specs=[hbm] * 5,
        out_specs=[vmem] * 2,
        scratch_shapes=[
            pltpu.VMEM((2, 3, rows, LANES), f32),
            pltpu.VMEM((2, 2, rows, LANES), jnp.int32),
            pltpu.SemaphoreType.DMA((2, 5)),
        ],
        compiler_params=pltpu.CompilerParams(vmem_limit_bytes=60 * 1024 * 1024),
        name="edges",
    )(*local)
    right = shift(low, "gy", cols_count, -1)
    left = shift(high, "gy", cols_count, 1)
    depth, adjoint, gradient = pl.pallas_call(
        inner_kernel,
        out_shape=[array(rows, cols), array(rows, cols), array(1, LANES)],
        in_specs=[vmem] * 5 + [smem] * 3,
        out_specs=[vmem] * 3,
        scratch_shapes=scratch(tiles, rows // 8, dam_cell.shape[0]),
        compiler_params=params,
        cost_estimate=pl.CostEstimate(flops=500 * rows * cols, bytes_accessed=7 * 4 * rows * cols, transcendentals=0),
        name="inner",
    )(*local, *given)
    side, to_top, to_bottom = pl.pallas_call(
        corner_kernel,
        out_shape=[array(2, FIELDS, EDGE, LANES), array(STRIP, wide), array(STRIP, wide)],
        in_specs=[vmem] * 7,
        out_specs=[vmem] * 3,
        compiler_params=params,
        name="corners",
    )(*local, left, right)
    bottom = shift(to_top, "gx", rows_count, -1)
    top = shift(to_bottom, "gx", rows_count, 1)
    depth, adjoint, parts = pl.pallas_call(
        frame_kernel,
        out_shape=[array(rows, cols), array(rows, cols), array(rows_count * cols_count, LANES)],
        in_specs=[vmem] * 5 + [smem] * 3 + [vmem] * 10,
        out_specs=[vmem] * 3,
        scratch_shapes=scratch(tiles + 3, 4, 2 * dam_cell.shape[0]),
        compiler_params=params,
        name="frame",
    )(*local, *given, depth, adjoint, gradient, low, high, left, right, side, top, bottom)
    gathered = lax.all_to_all(parts, ("gx", "gy"), 0, 0)
    release_grad = jnp.sum(gathered, axis=0).reshape(releases.shape[1], releases.shape[0]).T
    return (depth, adjoint, release_grad)


def solution(mesh):
    in_specs = (P("gx", "gy"),) * 5 + (P(), P(), P())
    out_specs = (P("gx", "gy"), P("gx", "gy"), P())
    return jax.shard_map(
        on_device, mesh=mesh, in_specs=in_specs, out_specs=out_specs, check_vma=False
    )
```

```python
import itertools

import jax
import jax.numpy as jnp
from jax import lax
from jax.experimental import pallas as pl
from jax.experimental.pallas import tpu as pltpu
from jax.sharding import PartitionSpec as P

GRAVITY = 9.81
TIME_RATIO = 0.05
INFLOW_GAIN = 0.25

LANES = 128
REACH = 4
EDGE = 8
FIELDS = 4
STRIP = FIELDS * REACH
UNROLL = True


def class_rate(classes, rates_ref):
    rate = jnp.full(classes.shape, rates_ref[0], jnp.float32)
    for index in range(1, rates_ref.shape[0]):
        rate = jnp.where(classes == index, rates_ref[index], rate)
    return rate


def coded_fields(h, x, y, wet, classes):
    return jnp.where(wet > 0, h, 0.0), x, y, classes.astype(jnp.float32)


def edge_kernel(h_hbm, x_hbm, y_hbm, wet_hbm, class_hbm, low_ref, high_ref, values, codes, sems):
    rows, cols = h_hbm.shape
    copies = []
    for index, source in enumerate((h_hbm, x_hbm, y_hbm, wet_hbm, class_hbm)):
        for side in range(2):
            kept = values.at[side, index] if index < 3 else codes.at[side, index - 3]
            part = source.at[:, pl.ds(side * (cols - LANES), LANES)]
            copies.append(pltpu.make_async_copy(part, kept, sems.at[side, index]))
    for copy in copies:
        copy.start()
    for copy in copies:
        copy.wait()
    lane = lax.broadcasted_iota(jnp.int32, (rows, LANES), 1)
    mixed = jnp.zeros((rows, LANES), jnp.float32)
    for side in range(2):
        fields = coded_fields(*(values[side, k] for k in range(3)), *(codes[side, k] for k in range(2)))
        for index, field in enumerate(fields):
            first = (side * FIELDS + index) * EDGE
            moved = first if side == 0 else first + EDGE
            shifted = pltpu.roll(field, moved, 1) if moved else field
            mixed = jnp.where((lane >= first) & (lane < first + EDGE), shifted, mixed)
    turned = mixed.T
    low_ref[...] = turned[: FIELDS * EDGE]
    high_ref[...] = turned[FIELDS * EDGE : 2 * FIELDS * EDGE]


def beside(left_ref, right_ref):
    place = lax.axis_index("gy")
    left = jnp.where(place > 0, left_ref[...], 0.0)
    right = jnp.where(place < lax.axis_size("gy") - 1, right_ref[...], 0.0)
    return left, right


def corner_kernel(ends_ref, left_ref, right_ref, side_ref, low_ref, high_ref):
    rows = left_ref.shape[1]
    cols = ends_ref.shape[2]
    left, right = beside(left_ref, right_ref)
    blank = jnp.zeros((LANES - 2 * FIELDS * EDGE, rows), jnp.float32)
    turned = jnp.concatenate((right, left, blank), axis=0).T
    lane = lax.broadcasted_iota(jnp.int32, (EDGE, LANES), 1)
    for end, (ref, start, kept) in enumerate(((low_ref, 0, 0), (high_ref, rows - EDGE, EDGE - REACH))):
        part = turned[start : start + EDGE]
        ref[:, :cols] = ends_ref[end]
        for index in range(FIELDS):
            upper = pltpu.roll(part, LANES - index * EDGE, 1) if index else part
            lower = pltpu.roll(part, LANES - (1 + FIELDS + index) * EDGE, 1)
            tile = jnp.where(lane < EDGE, upper, jnp.where(lane >= LANES - EDGE, lower, 0.0))
            side_ref[end, index] = tile
            ref[index * REACH : (index + 1) * REACH, cols:] = tile[kept : kept + REACH]


def cell_terms(height, flow_x, flow_y):
    scaled = GRAVITY * height
    inverse = pltpu.reciprocal(height, approx=True)
    return flow_x * inverse, flow_y * inverse, scaled * lax.rsqrt(scaled), inverse


def waves(u_low, c_low, u_high, c_high, both):
    slow_low, slow_high = u_low - c_low, u_high - c_high
    fast_low, fast_high = u_low + c_low, u_high + c_high
    slowest = jnp.minimum(jnp.minimum(slow_low, slow_high), 0.0)
    fastest = jnp.maximum(jnp.maximum(fast_low, fast_high), 0.0)
    inverse = both * pltpu.reciprocal(fastest - slowest, approx=True)
    share_low = fastest * inverse
    share_high = -(slowest * inverse)
    spread = slowest * share_low
    return slowest, fastest, inverse, share_low, share_high, spread, slow_low <= slow_high, fast_low >= fast_high


def speed_terms(slowest, fastest, of_slowest, of_fastest, slow_is_low, fast_is_low):
    of_slowest = jnp.where(slowest < 0.0, of_slowest, 0.0)
    of_fastest = jnp.where(fastest > 0.0, of_fastest, 0.0)
    slow_to_low = jnp.where(slow_is_low, of_slowest, 0.0)
    fast_to_low = jnp.where(fast_is_low, of_fastest, 0.0)
    slow_to_high = of_slowest - slow_to_low
    fast_to_high = of_fastest - fast_to_low
    return (
        fast_to_low + slow_to_low,
        fast_to_low - slow_to_low,
        fast_to_high + slow_to_high,
        fast_to_high - slow_to_high,
    )


def window(chunks, after, before, put, listed, dams, rates_ref, release_ref, held):
    state0, state1, mask, faces, walls, weight, last, lam0, lam, back, final = (
        held.get(name) for name in (
            "state0", "state1", "mask", "faces", "walls", "weight", "last", "lam0", "lam", "back", "final",
        )
    )
    tiles = len(after)
    every = range(tiles)
    lane = lax.broadcasted_iota(jnp.int32, (8, LANES), 1)

    def at(ref, k, j, start):
        return ref[k, j, pl.ds(start, 8), :]

    def next_col(values):
        rolled = [pltpu.roll(v, LANES - 1, 1) for v in values]
        return [jnp.where(lane == LANES - 1, rolled[after[j]], rolled[j]) for j in every]

    def previous_col(values):
        rolled = [pltpu.roll(v, 1, 1) for v in values]
        return [jnp.where(lane == 0, rolled[before[j]], rolled[j]) for j in every]

    def previous_row(slot, j, start, value):
        back[slot, j, pl.ds(start + 8, 8), :] = value
        return back[slot, j, pl.ds(start + 7, 8), :]

    def put_cell(ref, j, start, height, flow_x, flow_y):
        u, v, c, inverse = cell_terms(height, flow_x, flow_y)
        for k, value in enumerate((height, flow_x, flow_y, u, v, c, inverse)):
            ref[k, j, pl.ds(start, 8), :] = value

    def fill(j, start, wet, height, flow_x, flow_y, classes):
        put_cell(
            state0, j, start,
            jnp.where(wet, height, 1.0), jnp.where(wet, flow_x, 0.0), jnp.where(wet, flow_y, 0.0),
        )
        mask[j, pl.ds(start, 8), :] = jnp.where(wet, 1.0, 0.0)
        weight[j, pl.ds(start, 8), :] = jnp.where(wet, class_rate(classes, rates_ref), 0.0)

    def clear(ref, start, value=0.0):
        index = tuple(range(n) for n in ref.shape[:-2])
        for lead in itertools.product(*index):
            ref[lead + (pl.ds(start, 8), slice(None))] = jnp.full((8, LANES), value, jnp.float32)

    def run(step):
        lax.fori_loop(0, chunks, step, 0, unroll=UNROLL)

    def add_inflow(step, ref, refresh):
        def one(index, carry):
            d, row, j, col = (listed[k, index] for k in range(4))
            if refresh:
                old = [ref[k, j, pl.ds(row, 1), :] for k in range(3)]
            else:
                old = [ref[j, pl.ds(row, 1), :]]
            here = lax.broadcasted_iota(jnp.int32, (1, LANES), 1) == col
            height = old[0] + jnp.where(here, INFLOW_GAIN * release_ref[d, step], 0.0)
            if refresh:
                terms = (height, old[1], old[2]) + cell_terms(height, old[1], old[2])
                for k, value in enumerate(terms):
                    ref[k, j, pl.ds(row, 1), :] = value
            else:
                ref[j, pl.ds(row, 1), :] = height
            return carry

        lax.fori_loop(0, dams, one, 0)

    def pick(step, ref, gradient):
        lane_row = lax.broadcasted_iota(jnp.int32, (1, LANES), 1)

        def one(index, total):
            d, row, j, col, inside = (listed[k, index] for k in range(5))
            values = ref[j, pl.ds(row, 1), :]
            value = jnp.sum(jnp.where(lane_row == col, values, 0.0), axis=1, keepdims=True)
            spot = (lane_row == d + step * release_ref.shape[0]) & (inside > 0)
            return total + jnp.where(spot, (INFLOW_GAIN / TIME_RATIO) * value, 0.0)

        return lax.fori_loop(0, dams, one, gradient)

    def forward():
        clear(back, 0)
        for ref in (state0, state1):
            for k in range(7):
                clear(ref.at[k], chunks * 8, 1.0 if k in (0, 5, 6) else 0.0)
        clear(mask, chunks * 8)
        clear(lam0, chunks * 8)
        put(fill)

        def first_step(i, carry):
            start = pl.multiple_of(i * 8, 8)
            low = [[at(state0, k, j, start) for j in every] for k in range(6)]
            h, x, y, u, v, c = low
            m = [mask[j, pl.ds(start, 8), :] for j in every]
            half = [(0.5 * GRAVITY) * h[j] * h[j] for j in every]
            cross = [x[j] * v[j] for j in every]
            press_x = [x[j] * u[j] + half[j] for j in every]
            press_y = [y[j] * v[j] + half[j] for j in every]
            gain = []
            for j in every:
                hn, xn, yn, un, cn = (at(state0, k, j, start + 1) for k in (0, 1, 2, 3, 5))
                both = m[j] * mask[j, pl.ds(start + 1, 8), :]
                faces[0, j, pl.ds(start, 8), :] = both
                _, _, _, wl, wh, sp, _, _ = waves(u[j], c[j], un, cn, both)
                fh = wl * x[j] + wh * xn + sp * (hn - h[j])
                fn = wl * press_x[j] + wh * (xn * un + (0.5 * GRAVITY) * hn * hn) + sp * (xn - x[j])
                ft = wl * cross[j] + wh * (yn * un) + sp * (yn - y[j])
                both_low = previous_row(0, j, start, both)
                tilt = both_low - both
                shut = 2.0 * m[j] - both - both_low
                walls[0, j, pl.ds(start, 8), :] = tilt
                walls[1, j, pl.ds(start, 8), :] = shut
                gain.append(
                    [
                        fh - previous_row(1, j, start, fh),
                        fn - previous_row(2, j, start, fn) + tilt * press_x[j] + shut * ((jnp.abs(u[j]) + c[j]) * x[j]),
                        ft - previous_row(3, j, start, ft),
                    ]
                )
            hn, xn, yn, vn, cn, pn, tn, mn = (next_col(q) for q in (h, x, y, v, c, press_y, cross, m))
            flux = [[], [], []]
            both_up = []
            for j in every:
                both = m[j] * mn[j]
                faces[1, j, pl.ds(start, 8), :] = both
                both_up.append(both)
                _, _, _, wl, wh, sp, _, _ = waves(v[j], c[j], vn[j], cn[j], both)
                flux[0].append(wl * y[j] + wh * yn[j] + sp * (hn[j] - h[j]))
                flux[1].append(wl * press_y[j] + wh * pn[j] + sp * (yn[j] - y[j]))
                flux[2].append(wl * cross[j] + wh * tn[j] + sp * (xn[j] - x[j]))
            flux_low = [previous_col(q) for q in flux]
            both_low = previous_col(both_up)
            for j in every:
                tilt = both_low[j] - both_up[j]
                shut = 2.0 * m[j] - both_up[j] - both_low[j]
                walls[2, j, pl.ds(start, 8), :] = tilt
                walls[3, j, pl.ds(start, 8), :] = shut
                change_h = gain[j][0] + (flux[0][j] - flux_low[0][j])
                change_x = gain[j][1] + (flux[2][j] - flux_low[2][j])
                change_y = gain[j][2] + (flux[1][j] - flux_low[1][j])
                change_y = change_y + tilt * press_y[j] + shut * ((jnp.abs(v[j]) + c[j]) * y[j])
                put_cell(
                    state1, j, start,
                    h[j] - TIME_RATIO * change_h, x[j] - TIME_RATIO * change_x, y[j] - TIME_RATIO * change_y,
                )
            return carry

        run(first_step)
        add_inflow(0, state1, True)

        def second_step(i, carry):
            start = pl.multiple_of(i * 8, 8)
            h, x, y, u, v, c = [[at(state1, k, j, start) for j in every] for k in range(6)]
            gain = []
            for j in every:
                hn, xn, un, cn = (at(state1, k, j, start + 1) for k in (0, 1, 3, 5))
                _, _, _, wl, wh, sp, _, _ = waves(u[j], c[j], un, cn, at(faces, 0, j, start))
                fh = wl * x[j] + wh * xn + sp * (hn - h[j])
                gain.append(fh - previous_row(0, j, start, fh))
            hn, yn, vn, cn = (next_col(q) for q in (h, y, v, c))
            flux = []
            for j in every:
                _, _, _, wl, wh, sp, _, _ = waves(v[j], c[j], vn[j], cn[j], at(faces, 1, j, start))
                flux.append(wl * y[j] + wh * yn[j] + sp * (hn[j] - h[j]))
            flux_low = previous_col(flux)
            for j in every:
                last[j, pl.ds(start, 8), :] = h[j] - TIME_RATIO * (gain[j] + (flux[j] - flux_low[j]))
            return carry

        run(second_step)
        add_inflow(1, last, False)

        def finish_depth(i, carry):
            start = pl.multiple_of(i * 8, 8)
            for j in every:
                height = last[j, pl.ds(start, 8), :]
                lam0[j, pl.ds(start, 8), :] = TIME_RATIO * (weight[j, pl.ds(start, 8), :] * height)
            return carry

        run(finish_depth)

        return pick(1, lam0, jnp.zeros((1, LANES), jnp.float32))


    def backward(gradient):
        clear(back, 0)
        clear(lam, chunks * 8)

        def second_back(i, carry):
            start = pl.multiple_of(i * 8, 8)
            h, x, y, u, v, c, r = [[at(state1, k, j, start) for j in every] for k in range(7)]
            lh = [lam0[j, pl.ds(start, 8), :] for j in every]

            def face(hl, nl, ul, cl, hh, nh, uh, ch, gl, gh, both):
                slow, fast, inv, wl, wh, sp, slow_low, fast_low = waves(ul, cl, uh, ch, both)
                g = gh - gl
                dn, dh = nh - nl, hh - hl
                to_low, to_high = wl * g, wh * g
                of_slow = -(to_low * inv) * (dn - fast * dh)
                of_fast = -(to_high * inv) * (dn - slow * dh)
                return (to_low, to_high, sp * g) + speed_terms(slow, fast, of_slow, of_fast, slow_low, fast_low)

            partial_h, partial_u, partial_c, flow = [], [], [], []
            for j in every:
                hn, xn, un, cn = (at(state1, k, j, start + 1) for k in (0, 1, 3, 5))
                to_low, to_high, jump, u_low, c_low, u_high, c_high = face(
                    h[j], x[j], u[j], c[j], hn, xn, un, cn, lh[j], lam0[j, pl.ds(start + 1, 8), :], at(faces, 0, j, start)
                )
                of_u = u_low + previous_row(2, j, start, u_high)
                partial_h.append(previous_row(0, j, start, jump) - jump)
                partial_c.append(c_low + previous_row(3, j, start, c_high))
                partial_u.append(of_u * u[j])
                flow.append(to_low + previous_row(1, j, start, to_high) + of_u * r[j])
            hn, yn, vn, cn, ln = (next_col(q) for q in (h, y, v, c, lh))
            terms = [
                face(h[j], y[j], v[j], c[j], hn[j], yn[j], vn[j], cn[j], lh[j], ln[j], at(faces, 1, j, start))
                for j in every
            ]
            high, jump, u_high, c_high = (previous_col([t[k] for t in terms]) for k in (1, 2, 5, 6))
            for j in every:
                to_low, _, own_jump, u_low, c_low, _, _ = terms[j]
                of_v = u_low + u_high[j]
                of_c = partial_c[j] + c_low + c_high[j]
                of_h = partial_h[j] + (jump[j] - own_jump)
                of_h = of_h + r[j] * (0.5 * (of_c * c[j]) - partial_u[j] - of_v * v[j])
                lam[0, j, pl.ds(start, 8), :] = lh[j] + TIME_RATIO * of_h
                lam[1, j, pl.ds(start, 8), :] = TIME_RATIO * flow[j]
                lam[2, j, pl.ds(start, 8), :] = TIME_RATIO * (to_low + high[j] + of_v * r[j])
            return carry

        run(second_back)

        gradient = pick(0, lam.at[0], gradient)

        def first_back(i, carry):
            start = pl.multiple_of(i * 8, 8)
            h, x, y, u, v, c, r = [[at(state0, k, j, start) for j in every] for k in range(7)]
            lh, lx, ly = [[at(lam, k, j, start) for j in every] for k in range(3)]
            half = [(0.5 * GRAVITY) * h[j] * h[j] for j in every]
            cross = [x[j] * v[j] for j in every]

            def face(hl, nl, tl, ul, cl, pl_, kl, hh, nh, th, uh, ch, ph, kh, gl, gh, both):
                slow, fast, inv, wl, wh, sp, slow_low, fast_low = waves(ul, cl, uh, ch, both)
                g_h, g_n, g_t = (b - a for a, b in zip(gl, gh))
                dn = nh - nl
                of_flux = g_h * dn + g_n * (ph - pl_) + g_t * (kh - kl)
                of_jump = g_h * (hh - hl) + g_n * dn + g_t * (th - tl)
                of_slow = -(wl * inv) * (of_flux - fast * of_jump)
                of_fast = -(wh * inv) * (of_flux - slow * of_jump)
                return (wl * g_n, wl * g_t, wh * g_n, wh * g_t, sp * g_h) + speed_terms(
                    slow, fast, of_slow, of_fast, slow_low, fast_low
                )

            kept = []
            for j in every:
                hn, xn, yn, un, cn = (at(state0, k, j, start + 1) for k in (0, 1, 2, 3, 5))
                nl, tl, nh, th, jump, u_low, c_low, u_high, c_high = face(
                    h[j], x[j], y[j], u[j], c[j], x[j] * u[j] + half[j], cross[j],
                    hn, xn, yn, un, cn, xn * un + (0.5 * GRAVITY) * hn * hn, yn * un,
                    (lh[j], lx[j], ly[j]), tuple(at(lam, k, j, start + 1) for k in range(3)), at(faces, 0, j, start),
                )
                shut = lx[j] * at(walls, 1, j, start)
                normal = nl + previous_row(0, j, start, nh) - lx[j] * at(walls, 0, j, start)
                across = tl + previous_row(1, j, start, th)
                of_u = normal * x[j] + across * y[j] + u_low + previous_row(3, j, start, u_high) - shut * jnp.abs(x[j])
                of_c = c_low + previous_row(4, j, start, c_high) - shut * x[j]
                kept.append((normal, previous_row(2, j, start, jump) - jump, of_u * u[j], of_c))
            press = [y[j] * v[j] + half[j] for j in every]
            hn, xn, yn, vn, cn, pn, kn = (next_col(q) for q in (h, x, y, v, c, press, cross))
            lhn, lxn, lyn = (next_col(q) for q in (lh, lx, ly))
            terms = [
                face(
                    h[j], y[j], x[j], v[j], c[j], press[j], cross[j],
                    hn[j], yn[j], xn[j], vn[j], cn[j], pn[j], kn[j],
                    (lh[j], ly[j], lx[j]), (lhn[j], lyn[j], lxn[j]), at(faces, 1, j, start),
                )
                for j in every
            ]
            nh, th, jump, u_high, c_high = (previous_col([t[k] for t in terms]) for k in (2, 3, 4, 7, 8))
            for j in every:
                shut = ly[j] * at(walls, 3, j, start)
                normal = terms[j][0] + nh[j] - ly[j] * at(walls, 2, j, start)
                across = terms[j][1] + th[j]
                of_v = normal * y[j] + across * x[j] + terms[j][5] + u_high[j] - shut * jnp.abs(y[j])
                of_c = kept[j][3] + terms[j][6] + c_high[j] - shut * y[j]
                of_h = kept[j][1] + (jump[j] - terms[j][4]) + GRAVITY * h[j] * (kept[j][0] + normal)
                of_h = of_h + r[j] * (0.5 * (of_c * c[j]) - kept[j][2] - of_v * v[j])
                final[j, pl.ds(start, 8), :] = (1.0 / TIME_RATIO) * lh[j] + of_h
            return carry

        run(first_back)
        return gradient

    return forward, backward


def list_dams(dam_ref, listed, rows, cols, spots):
    total_cols = cols * lax.axis_size("gy")
    row_first = lax.axis_index("gx") * rows
    col_first = lax.axis_index("gy") * cols

    def local(cell):
        if total_cols & (total_cols - 1):
            row = lax.div(cell, jnp.full(jnp.shape(cell), total_cols, jnp.int32))
        else:
            row = lax.shift_right_logical(cell, jnp.full(jnp.shape(cell), total_cols.bit_length() - 1, jnp.int32))
        return row - row_first, cell - row * total_cols - col_first

    cells = dam_ref[...]
    none = cells.shape[1]
    number = lax.broadcasted_iota(jnp.int32, cells.shape, 1)
    row, col = local(cells)
    near = within(row, -REACH, rows + REACH) & within(col, -REACH, cols + REACH)
    number = jnp.where(near, number, none)

    def one(state):
        d, count = state
        row, col = local(jnp.max(jnp.where(number == d, cells, 0)))
        for held, spot in spots(row, col):
            @pl.when(held)
            def _():
                for k, value in enumerate((d,) + spot):
                    listed[k, count] = value

            count = count + jnp.where(held, 1, 0)
        return jnp.min(jnp.where(number > d, number, none)), count

    return lax.while_loop(lambda state: state[0] < none, one, (jnp.min(number), jnp.int32(0)))[1]


def within(value, first, end):
    return (value >= first) & (value < end)


def split(place):
    return lax.shift_right_logical(place, LANES.bit_length() - 1), place & (LANES - 1)


def inner_spots(rows, cols):
    def spots(row, col):
        tile, lane = split(col)
        own = within(row, REACH, rows - REACH) & within(col, REACH, cols - REACH)
        yield within(row, 0, rows) & within(col, 0, cols), (row, tile, lane, jnp.where(own, 1, 0))

    return spots


def ring(tiles):
    return [(j + 1) % tiles for j in range(tiles)], [(j - 1) % tiles for j in range(tiles)]


KEPT = ("state0", "state1", "faces", "walls", "lam0")


def inner_forward_kernel(
    h_ref, x_ref, y_ref, wet_ref, class_ref, rates_ref, dam_ref, release_ref,
    ends_ref, depth_ref, grad_ref, *rest,
):
    held = dict(zip(KEPT + ("listed", "mask", "weight", "last", "back"), rest))
    rows, cols = h_ref.shape
    tiles = cols // LANES
    chunks = rows // 8
    for end, (start, kept) in enumerate(((0, 0), (rows - EDGE, EDGE - REACH))):
        part = slice(start, start + EDGE)
        own = coded_fields(h_ref[part, :], x_ref[part, :], y_ref[part, :], wet_ref[part, :], class_ref[part, :])
        for index in range(FIELDS):
            ends_ref[end, index * REACH : (index + 1) * REACH, :] = own[index][kept : kept + REACH]
    dams = list_dams(dam_ref, held["listed"], rows, cols, inner_spots(rows, cols))

    def put(fill):
        def one(i, carry):
            part = pl.ds(pl.multiple_of(i * 8, 8), 8)
            for j in range(tiles):
                across = pl.ds(j * LANES, LANES)
                fill(
                    j, pl.multiple_of(i * 8, 8), wet_ref[part, across] > 0,
                    h_ref[part, across], x_ref[part, across], y_ref[part, across], class_ref[part, across],
                )
            return carry

        lax.fori_loop(0, chunks, one, 0, unroll=2)

    forward, _ = window(chunks, *ring(tiles), put, held["listed"], dams, rates_ref, release_ref, held)
    grad_ref[...] = forward()
    for j in range(tiles):
        across = slice(j * LANES, (j + 1) * LANES)
        depth_ref[:, across] = jnp.where(wet_ref[:, across] > 0, held["last"][j, :rows, :], h_ref[:, across])


def inner_backward_kernel(*refs):
    names = KEPT + ("dams", "grad_in", "adjoint", "grad", "listed", "lam", "back", "final")
    held = dict(zip(names, refs))
    rows, cols = held["adjoint"].shape
    tiles = cols // LANES
    dams = list_dams(held["dams"], held["listed"], rows, cols, inner_spots(rows, cols))
    shape = jax.ShapeDtypeStruct((held["dams"].shape[1],), jnp.float32)
    _, backward = window(rows // 8, *ring(tiles), None, held["listed"], dams, None, shape, held)
    held["grad"][...] = backward(held["grad_in"][...])
    for j in range(tiles):
        held["adjoint"][:, j * LANES : (j + 1) * LANES] = held["final"][j, :rows, :]


def frame_kernel(
    h_ref, x_ref, y_ref, wet_ref, class_ref, rates_ref, dam_ref, release_ref,
    depth_in, adjoint_in, grad_in, low_ref, high_ref, left_ref, right_ref, side_ref, top_ref, bottom_ref,
    depth_ref, adjoint_ref, grad_ref, *rest,
):
    rows, cols = h_ref.shape
    tiles = cols // LANES
    chunks = 4
    turned = tiles + 1
    after = [(j + 1) % turned for j in range(turned)] + [turned + 1, turned]
    before = [(j - 1) % turned for j in range(turned)] + [turned + 1, turned]

    def chunk_row(place, count):
        return jnp.where(place < EDGE, place + EDGE, place - count + 3 * EDGE)

    def near_end(place, count):
        return within(place, -REACH, EDGE) | within(place, count - EDGE, count + REACH)

    def at_end(place, count):
        return within(place, 0, REACH) | within(place, count - REACH, count)

    def spots(row, col):
        near = within(row, -REACH, rows + REACH) & within(col, -REACH, cols + REACH)
        tile, lane = split(jnp.where(col < 0, col + (tiles + 1) * LANES, col))
        own = at_end(row, rows) & within(col, 0, cols)
        yield near & near_end(row, rows), (chunk_row(row, rows), tile, lane, jnp.where(own, 1, 0))
        tile, lane = split(jnp.where(row < 0, row + 2 * LANES, row))
        own = at_end(col, cols) & within(row, REACH, rows - REACH)
        yield near & near_end(col, cols), (chunk_row(col, cols), tile + turned, lane, jnp.where(own, 1, 0))

    held = dict(zip(KEPT + ("listed", "mask", "weight", "last", "back", "lam", "final"), rest))
    dams = list_dams(dam_ref, held["listed"], rows, cols, spots)
    place = lax.axis_index("gx")
    above = jnp.where(place > 0, top_ref[...], 0.0)
    below = jnp.where(place < lax.axis_size("gx") - 1, bottom_ref[...], 0.0)
    left, right = beside(left_ref, right_ref)

    def put(fill):
        blank = jnp.zeros((EDGE - REACH, LANES), jnp.float32)

        def coded(j, start, h, x, y, code):
            fill(j, start, h > 0.0, h, x, y, code.astype(jnp.int32))

        for j in range(tiles + 1):
            across = slice(j * LANES, (j + 1) * LANES)
            for start, strip in ((0, above), (3 * EDGE, below)):
                pieces = [strip[k * REACH : (k + 1) * REACH, across] for k in range(FIELDS)]
                coded(j, start, *(jnp.concatenate((blank, v) if start == 0 else (v, blank), axis=0) for v in pieces))
            for end, first in ((0, 0), (1, rows - EDGE)):
                start = (1 + end) * EDGE
                if j < tiles:
                    part = slice(first, first + EDGE)
                    fill(
                        j, start, wet_ref[part, across] > 0,
                        h_ref[part, across], x_ref[part, across], y_ref[part, across], class_ref[part, across],
                    )
                else:
                    coded(j, start, *(side_ref[end, k] for k in range(FIELDS)))
        order = (0, 2, 1, 3)
        for chunk, strip in enumerate((left, low_ref[...], high_ref[...], right)):
            coded(turned, chunk * EDGE, *(strip[k * EDGE : (k + 1) * EDGE] for k in order))
        strips = jnp.concatenate((above, below), axis=0)
        outer = strips[:, tiles * LANES :]
        mixed = jnp.zeros((2 * STRIP, LANES), jnp.float32)
        lane = lax.broadcasted_iota(jnp.int32, (2 * STRIP, LANES), 1)
        pieces = (
            (outer, LANES - EDGE),
            (strips[:, :LANES], 0),
            (strips[:, (tiles - 1) * LANES : tiles * LANES], LANES - EDGE),
            (outer, 0),
        )
        for chunk, (piece, first) in enumerate(pieces):
            moved = (chunk * EDGE - first) % LANES
            mixed = jnp.where(lane // EDGE == chunk, pltpu.roll(piece, moved, 1) if moved else piece, mixed)
        corners = jnp.concatenate((mixed, jnp.zeros((LANES - 2 * STRIP, LANES), jnp.float32)), axis=0).T
        corners = corners[: chunks * EDGE]
        lane = lax.broadcasted_iota(jnp.int32, (chunks * EDGE, LANES), 1)
        fields = []
        for k in order:
            from_above = pltpu.roll(corners, LANES - REACH - k * REACH, 1)
            from_below = pltpu.roll(corners, LANES - STRIP - k * REACH, 1)
            fields.append(jnp.where(lane < REACH, from_below, jnp.where(lane >= LANES - REACH, from_above, 0.0)))
        for chunk in range(chunks):
            coded(turned + 1, chunk * EDGE, *(v[chunk * EDGE : (chunk + 1) * EDGE] for v in fields))

    forward, backward = window(chunks, after, before, put, held["listed"], dams, rates_ref, release_ref, held)
    grad_ref[...] = jnp.broadcast_to(backward(forward() + grad_in[...]), grad_ref.shape)
    last, final = held["last"], held["final"]
    blank = jnp.zeros((LANES - 4 * EDGE, LANES), jnp.float32)
    ends = slice(EDGE, 3 * EDGE)
    columns = jnp.concatenate((last[turned, ends, :], final[turned, ends, :], blank), axis=0).T
    lane = lax.broadcasted_iota(jnp.int32, (rows, LANES), 1)
    row = lax.broadcasted_iota(jnp.int32, (EDGE, LANES), 0)
    for number, (ref, inner, strip) in enumerate(((depth_ref, depth_in, last), (adjoint_ref, adjoint_in, final))):
        for j in range(tiles):
            across = slice(j * LANES, (j + 1) * LANES)

            def wet_only(value, part):
                if number:
                    return value
                return jnp.where(wet_ref[part, across] > 0, value, h_ref[part, across])

            whole = slice(0, rows)
            block = inner[:, across]
            if j == 0:
                moved = (LANES - 2 * EDGE * number) % LANES
                edge = pltpu.roll(columns, moved, 1) if moved else columns
                block = jnp.where(lane < REACH, wet_only(edge, whole), block)
            if j == tiles - 1:
                edge = pltpu.roll(columns, LANES - 2 * EDGE - 2 * EDGE * number, 1)
                block = jnp.where(lane >= LANES - REACH, wet_only(edge, whole), block)
            middle = slice(EDGE, rows - EDGE)
            ref[middle, across] = block[middle]
            for part, start, own in (
                (slice(0, EDGE), EDGE, row < REACH),
                (slice(rows - EDGE, rows), 2 * EDGE, row >= EDGE - REACH),
            ):
                ref[part, across] = jnp.where(own, wet_only(strip[j, start : start + EDGE, :], part), block[part])


def on_device(
    water_depth, momentum_x, momentum_y, wet_mask, damage_class, damage_rates, dam_cell, releases
):
    rows, cols = water_depth.shape
    tiles = cols // LANES
    wide = cols + LANES
    rows_count = lax.axis_size("gx")
    cols_count = lax.axis_size("gy")
    vmem = pl.BlockSpec(memory_space=pltpu.VMEM)
    smem = pl.BlockSpec(memory_space=pltpu.SMEM)
    hbm = pl.BlockSpec(memory_space=pltpu.HBM)
    f32 = jnp.float32
    local = (water_depth, momentum_x, momentum_y, wet_mask, damage_class)
    given = (damage_rates, dam_cell.reshape(1, -1), releases)

    def shift(value, axis, count, step):
        return lax.ppermute(value, axis, [(i, (i + step) % count) for i in range(count)])

    def array(*shape):
        return jax.ShapeDtypeStruct(shape, f32)

    def need(names, tiles, chunks):
        leads = dict(state0=(7,), state1=(7,), faces=(2,), walls=(4,), lam=(3,), back=(5,))
        return [array(*leads.get(name, ()), tiles, 8 * chunks + 8, LANES) for name in names]

    def scratch(names, tiles, chunks, spots):
        listed = pltpu.SMEM((5, spots), jnp.int32)
        return [listed] + [pltpu.VMEM(v.shape, v.dtype) for v in need(names, tiles, chunks)]

    low, high = pl.pallas_call(
        edge_kernel,
        out_shape=[array(FIELDS * EDGE, rows)] * 2,
        in_specs=[hbm] * 5,
        out_specs=[vmem] * 2,
        scratch_shapes=[
            pltpu.VMEM((2, 3, rows, LANES), f32),
            pltpu.VMEM((2, 2, rows, LANES), jnp.int32),
            pltpu.SemaphoreType.DMA((2, 5)),
        ],
        compiler_params=pltpu.CompilerParams(vmem_limit_bytes=60 * 1024 * 1024),
        cost_estimate=pl.CostEstimate(flops=10**9, bytes_accessed=4 * 10**7, transcendentals=0),
        name="edges",
    )(*local)
    right = shift(low, "gy", cols_count, -1)
    left = shift(high, "gy", cols_count, 1)
    kept = need(KEPT, tiles, rows // 8)
    dams = dam_cell.shape[0]
    inner_params = pltpu.CompilerParams(vmem_limit_bytes=16 * 1024 * 1024)
    ends, depth, gradient, *kept = pl.pallas_call(
        inner_forward_kernel,
        out_shape=[array(2, STRIP, cols), array(rows, cols), array(1, LANES)] + kept,
        in_specs=[vmem] * 5 + [smem, vmem, smem],
        out_specs=[vmem] * (3 + len(kept)),
        scratch_shapes=scratch(("mask", "weight", "last", "back"), tiles, rows // 8, dams),
        compiler_params=inner_params,
        cost_estimate=pl.CostEstimate(flops=200 * rows * cols, bytes_accessed=6 * 4 * rows * cols, transcendentals=0),
        name="inner_forward",
    )(*local, *given)
    side, to_top, to_bottom = pl.pallas_call(
        corner_kernel,
        out_shape=[array(2, FIELDS, EDGE, LANES), array(STRIP, wide), array(STRIP, wide)],
        in_specs=[vmem] * 3,
        out_specs=[vmem] * 3,
        compiler_params=inner_params,
        name="corners",
    )(ends, left, right)
    adjoint, gradient = pl.pallas_call(
        inner_backward_kernel,
        out_shape=[array(rows, cols), array(1, LANES)],
        in_specs=[vmem] * (len(kept) + 2),
        out_specs=[vmem] * 2,
        scratch_shapes=scratch(("lam", "back", "final"), tiles, rows // 8, dams),
        compiler_params=inner_params,
        cost_estimate=pl.CostEstimate(flops=300 * rows * cols, bytes_accessed=6 * 4 * rows * cols, transcendentals=0),
        name="inner_backward",
    )(*kept, given[1], gradient)
    bottom = shift(to_top, "gx", rows_count, -1)
    top = shift(to_bottom, "gx", rows_count, 1)
    depth, adjoint, parts = pl.pallas_call(
        frame_kernel,
        out_shape=[array(rows, cols), array(rows, cols), array(rows_count * cols_count, LANES)],
        in_specs=[vmem] * 5 + [smem, vmem, smem] + [vmem] * 10,
        out_specs=[vmem] * 3,
        scratch_shapes=(
            [pltpu.VMEM(v.shape, v.dtype) for v in need(KEPT, tiles + 3, 4)]
            + scratch(("mask", "weight", "last", "back", "lam", "final"), tiles + 3, 4, 2 * dams)
        ),
        compiler_params=inner_params,
        name="frame",
    )(*local, *given, depth, adjoint, gradient, low, high, left, right, side, top, bottom)
    gathered = lax.all_to_all(parts, ("gx", "gy"), 0, 0)
    release_grad = jnp.sum(gathered, axis=0).reshape(releases.shape[1], releases.shape[0]).T
    return (depth, adjoint, release_grad)


def solution(mesh):
    in_specs = (P("gx", "gy"),) * 5 + (P(), P(), P())
    out_specs = (P("gx", "gy"), P("gx", "gy"), P())
    return jax.shard_map(
        on_device, mesh=mesh, in_specs=in_specs, out_specs=out_specs, check_vma=False
    )
```

```python
import itertools

import jax
import jax.numpy as jnp
from jax import lax
from jax.experimental import pallas as pl
from jax.experimental.pallas import tpu as pltpu
from jax.sharding import PartitionSpec as P

GRAVITY = 9.81
TIME_RATIO = 0.05
INFLOW_GAIN = 0.25

LANES = 128
REACH = 4
EDGE = 8
FIELDS = 4
STRIP = FIELDS * REACH
UNROLL = True


def class_rate(classes, rates_ref):
    rate = jnp.full(classes.shape, rates_ref[0], jnp.float32)
    for index in range(1, rates_ref.shape[0]):
        rate = jnp.where(classes == index, rates_ref[index], rate)
    return rate


def coded_fields(h, x, y, wet, classes):
    return jnp.where(wet > 0, h, 0.0), x, y, classes.astype(jnp.float32)


def is_even(axis):
    return (lax.axis_index(axis) & 1) == 0


def low_and_high(axis, near, far):
    even = is_even(axis)
    return jnp.where(even, far, near), jnp.where(even, near, far)


def edge_kernel(h_hbm, x_hbm, y_hbm, wet_hbm, class_hbm, near_ref, far_ref, values, codes, sems):
    rows, cols = h_hbm.shape
    copies = []
    for index, source in enumerate((h_hbm, x_hbm, y_hbm, wet_hbm, class_hbm)):
        for side in range(2):
            kept = values.at[side, index] if index < 3 else codes.at[side, index - 3]
            part = source.at[:, pl.ds(side * (cols - LANES), LANES)]
            copies.append(pltpu.make_async_copy(part, kept, sems.at[side, index]))
    for copy in copies:
        copy.start()
    for copy in copies:
        copy.wait()
    lane = lax.broadcasted_iota(jnp.int32, (rows, LANES), 1)
    mixed = jnp.zeros((rows, LANES), jnp.float32)
    for side in range(2):
        fields = coded_fields(*(values[side, k] for k in range(3)), *(codes[side, k] for k in range(2)))
        for index, field in enumerate(fields):
            first = (side * FIELDS + index) * EDGE
            moved = first if side == 0 else first + EDGE
            shifted = pltpu.roll(field, moved, 1) if moved else field
            mixed = jnp.where((lane >= first) & (lane < first + EDGE), shifted, mixed)
    turned = mixed.T
    far_ref[...], near_ref[...] = low_and_high("gy", turned[FIELDS * EDGE : 2 * FIELDS * EDGE], turned[: FIELDS * EDGE])


def beside(axis, near_ref, far_ref):
    place = lax.axis_index(axis)
    low, high = low_and_high(axis, near_ref[...], far_ref[...])
    return jnp.where(place > 0, low, 0.0), jnp.where(place < lax.axis_size(axis) - 1, high, 0.0)


def corner_kernel(ends_ref, near_in, far_in, side_ref, near_ref, far_ref):
    rows = near_in.shape[1]
    cols = ends_ref.shape[2]
    even = is_even("gx")
    left, right = beside("gy", near_in, far_in)
    blank = jnp.zeros((LANES - 2 * FIELDS * EDGE, rows), jnp.float32)
    turned = jnp.concatenate((right, left, blank), axis=0).T
    lane = lax.broadcasted_iota(jnp.int32, (EDGE, LANES), 1)
    strips = []
    for end, start, kept in ((0, 0, 0), (1, rows - EDGE, EDGE - REACH)):
        part = turned[start : start + EDGE]
        pieces = []
        for index in range(FIELDS):
            upper = pltpu.roll(part, LANES - index * EDGE, 1) if index else part
            lower = pltpu.roll(part, LANES - (1 + FIELDS + index) * EDGE, 1)
            tile = jnp.where(lane < EDGE, upper, jnp.where(lane >= LANES - EDGE, lower, 0.0))
            side_ref[end, index] = tile
            pieces.append(tile[kept : kept + REACH])
        strips.append((ends_ref[end], jnp.concatenate(pieces, axis=0)))
    for part, low, high in zip((slice(0, cols), slice(cols, cols + LANES)), *strips):
        near_ref[:, part] = jnp.where(even, high, low)
        far_ref[:, part] = jnp.where(even, low, high)


def cell_terms(height, flow_x, flow_y):
    scaled = GRAVITY * height
    inverse = pltpu.reciprocal(height, approx=True)
    return flow_x * inverse, flow_y * inverse, scaled * lax.rsqrt(scaled), inverse


def waves(u_low, c_low, u_high, c_high, both):
    slow_low, slow_high = u_low - c_low, u_high - c_high
    fast_low, fast_high = u_low + c_low, u_high + c_high
    slowest = jnp.minimum(jnp.minimum(slow_low, slow_high), 0.0)
    fastest = jnp.maximum(jnp.maximum(fast_low, fast_high), 0.0)
    inverse = both * pltpu.reciprocal(fastest - slowest, approx=True)
    share_low = fastest * inverse
    share_high = -(slowest * inverse)
    spread = slowest * share_low
    return slowest, fastest, inverse, share_low, share_high, spread, slow_low <= slow_high, fast_low >= fast_high


def speed_terms(slowest, fastest, of_slowest, of_fastest, slow_is_low, fast_is_low):
    of_slowest = jnp.where(slowest < 0.0, of_slowest, 0.0)
    of_fastest = jnp.where(fastest > 0.0, of_fastest, 0.0)
    slow_to_low = jnp.where(slow_is_low, of_slowest, 0.0)
    fast_to_low = jnp.where(fast_is_low, of_fastest, 0.0)
    slow_to_high = of_slowest - slow_to_low
    fast_to_high = of_fastest - fast_to_low
    return (
        fast_to_low + slow_to_low,
        fast_to_low - slow_to_low,
        fast_to_high + slow_to_high,
        fast_to_high - slow_to_high,
    )


def window(chunks, after, before, put, listed, dams, rates_ref, release_ref, held):
    state0, state1, mask, faces, walls, weight, last, lam0, lam, back, final = (
        held.get(name) for name in (
            "state0", "state1", "mask", "faces", "walls", "weight", "last", "lam0", "lam", "back", "final",
        )
    )
    tiles = len(after)
    every = range(tiles)
    lane = lax.broadcasted_iota(jnp.int32, (8, LANES), 1)

    def at(ref, k, j, start):
        return ref[k, j, pl.ds(start, 8), :]

    def next_col(values):
        rolled = [pltpu.roll(v, LANES - 1, 1) for v in values]
        return [jnp.where(lane == LANES - 1, rolled[after[j]], rolled[j]) for j in every]

    def previous_col(values):
        rolled = [pltpu.roll(v, 1, 1) for v in values]
        return [jnp.where(lane == 0, rolled[before[j]], rolled[j]) for j in every]

    def previous_row(slot, j, start, value):
        back[slot, j, pl.ds(start + 8, 8), :] = value
        return back[slot, j, pl.ds(start + 7, 8), :]

    def put_cell(ref, j, start, height, flow_x, flow_y):
        u, v, c, inverse = cell_terms(height, flow_x, flow_y)
        for k, value in enumerate((height, flow_x, flow_y, u, v, c, inverse)):
            ref[k, j, pl.ds(start, 8), :] = value

    def fill(j, start, wet, height, flow_x, flow_y, classes):
        put_cell(
            state0, j, start,
            jnp.where(wet, height, 1.0), jnp.where(wet, flow_x, 0.0), jnp.where(wet, flow_y, 0.0),
        )
        mask[j, pl.ds(start, 8), :] = jnp.where(wet, 1.0, 0.0)
        weight[j, pl.ds(start, 8), :] = jnp.where(wet, class_rate(classes, rates_ref), 0.0)

    def clear(ref, start, value=0.0):
        index = tuple(range(n) for n in ref.shape[:-2])
        for lead in itertools.product(*index):
            ref[lead + (pl.ds(start, 8), slice(None))] = jnp.full((8, LANES), value, jnp.float32)

    def run(step):
        lax.fori_loop(0, chunks, step, 0, unroll=UNROLL)

    def add_inflow(step, ref, refresh):
        def one(index, carry):
            d, row, j, col = (listed[k, index] for k in range(4))
            if refresh:
                old = [ref[k, j, pl.ds(row, 1), :] for k in range(3)]
            else:
                old = [ref[j, pl.ds(row, 1), :]]
            here = lax.broadcasted_iota(jnp.int32, (1, LANES), 1) == col
            height = old[0] + jnp.where(here, INFLOW_GAIN * release_ref[d, step], 0.0)
            if refresh:
                terms = (height, old[1], old[2]) + cell_terms(height, old[1], old[2])
                for k, value in enumerate(terms):
                    ref[k, j, pl.ds(row, 1), :] = value
            else:
                ref[j, pl.ds(row, 1), :] = height
            return carry

        lax.fori_loop(0, dams, one, 0)

    def pick(step, ref, gradient):
        lane_row = lax.broadcasted_iota(jnp.int32, (1, LANES), 1)

        def one(index, total):
            d, row, j, col, inside = (listed[k, index] for k in range(5))
            values = ref[j, pl.ds(row, 1), :]
            value = jnp.sum(jnp.where(lane_row == col, values, 0.0), axis=1, keepdims=True)
            spot = (lane_row == d + step * release_ref.shape[0]) & (inside > 0)
            return total + jnp.where(spot, (INFLOW_GAIN / TIME_RATIO) * value, 0.0)

        return lax.fori_loop(0, dams, one, gradient)

    def forward():
        clear(back, 0)
        for ref in (state0, state1):
            for k in range(7):
                clear(ref.at[k], chunks * 8, 1.0 if k in (0, 5, 6) else 0.0)
        clear(mask, chunks * 8)
        clear(lam0, chunks * 8)
        put(fill)

        def first_step(i, carry):
            start = pl.multiple_of(i * 8, 8)
            low = [[at(state0, k, j, start) for j in every] for k in range(6)]
            h, x, y, u, v, c = low
            m = [mask[j, pl.ds(start, 8), :] for j in every]
            half = [(0.5 * GRAVITY) * h[j] * h[j] for j in every]
            cross = [x[j] * v[j] for j in every]
            press_x = [x[j] * u[j] + half[j] for j in every]
            press_y = [y[j] * v[j] + half[j] for j in every]
            gain = []
            for j in every:
                hn, xn, yn, un, cn = (at(state0, k, j, start + 1) for k in (0, 1, 2, 3, 5))
                both = m[j] * mask[j, pl.ds(start + 1, 8), :]
                faces[0, j, pl.ds(start, 8), :] = both
                _, _, _, wl, wh, sp, _, _ = waves(u[j], c[j], un, cn, both)
                fh = wl * x[j] + wh * xn + sp * (hn - h[j])
                fn = wl * press_x[j] + wh * (xn * un + (0.5 * GRAVITY) * hn * hn) + sp * (xn - x[j])
                ft = wl * cross[j] + wh * (yn * un) + sp * (yn - y[j])
                both_low = previous_row(0, j, start, both)
                tilt = both_low - both
                shut = 2.0 * m[j] - both - both_low
                walls[0, j, pl.ds(start, 8), :] = tilt
                walls[1, j, pl.ds(start, 8), :] = shut
                gain.append(
                    [
                        fh - previous_row(1, j, start, fh),
                        fn - previous_row(2, j, start, fn) + tilt * press_x[j] + shut * ((jnp.abs(u[j]) + c[j]) * x[j]),
                        ft - previous_row(3, j, start, ft),
                    ]
                )
            hn, xn, yn, vn, cn, pn, tn, mn = (next_col(q) for q in (h, x, y, v, c, press_y, cross, m))
            flux = [[], [], []]
            both_up = []
            for j in every:
                both = m[j] * mn[j]
                faces[1, j, pl.ds(start, 8), :] = both
                both_up.append(both)
                _, _, _, wl, wh, sp, _, _ = waves(v[j], c[j], vn[j], cn[j], both)
                flux[0].append(wl * y[j] + wh * yn[j] + sp * (hn[j] - h[j]))
                flux[1].append(wl * press_y[j] + wh * pn[j] + sp * (yn[j] - y[j]))
                flux[2].append(wl * cross[j] + wh * tn[j] + sp * (xn[j] - x[j]))
            flux_low = [previous_col(q) for q in flux]
            both_low = previous_col(both_up)
            for j in every:
                tilt = both_low[j] - both_up[j]
                shut = 2.0 * m[j] - both_up[j] - both_low[j]
                walls[2, j, pl.ds(start, 8), :] = tilt
                walls[3, j, pl.ds(start, 8), :] = shut
                change_h = gain[j][0] + (flux[0][j] - flux_low[0][j])
                change_x = gain[j][1] + (flux[2][j] - flux_low[2][j])
                change_y = gain[j][2] + (flux[1][j] - flux_low[1][j])
                change_y = change_y + tilt * press_y[j] + shut * ((jnp.abs(v[j]) + c[j]) * y[j])
                put_cell(
                    state1, j, start,
                    h[j] - TIME_RATIO * change_h, x[j] - TIME_RATIO * change_x, y[j] - TIME_RATIO * change_y,
                )
            return carry

        run(first_step)
        add_inflow(0, state1, True)

        def second_step(i, carry):
            start = pl.multiple_of(i * 8, 8)
            h, x, y, u, v, c = [[at(state1, k, j, start) for j in every] for k in range(6)]
            gain = []
            for j in every:
                hn, xn, un, cn = (at(state1, k, j, start + 1) for k in (0, 1, 3, 5))
                _, _, _, wl, wh, sp, _, _ = waves(u[j], c[j], un, cn, at(faces, 0, j, start))
                fh = wl * x[j] + wh * xn + sp * (hn - h[j])
                gain.append(fh - previous_row(0, j, start, fh))
            hn, yn, vn, cn = (next_col(q) for q in (h, y, v, c))
            flux = []
            for j in every:
                _, _, _, wl, wh, sp, _, _ = waves(v[j], c[j], vn[j], cn[j], at(faces, 1, j, start))
                flux.append(wl * y[j] + wh * yn[j] + sp * (hn[j] - h[j]))
            flux_low = previous_col(flux)
            for j in every:
                last[j, pl.ds(start, 8), :] = h[j] - TIME_RATIO * (gain[j] + (flux[j] - flux_low[j]))
            return carry

        run(second_step)
        add_inflow(1, last, False)

        def finish_depth(i, carry):
            start = pl.multiple_of(i * 8, 8)
            for j in every:
                height = last[j, pl.ds(start, 8), :]
                lam0[j, pl.ds(start, 8), :] = TIME_RATIO * (weight[j, pl.ds(start, 8), :] * height)
            return carry

        run(finish_depth)

        return pick(1, lam0, jnp.zeros((1, LANES), jnp.float32))


    def backward(gradient):
        clear(back, 0)
        clear(lam, chunks * 8)

        def second_back(i, carry):
            start = pl.multiple_of(i * 8, 8)
            h, x, y, u, v, c, r = [[at(state1, k, j, start) for j in every] for k in range(7)]
            lh = [lam0[j, pl.ds(start, 8), :] for j in every]

            def face(hl, nl, ul, cl, hh, nh, uh, ch, gl, gh, both):
                slow, fast, inv, wl, wh, sp, slow_low, fast_low = waves(ul, cl, uh, ch, both)
                g = gh - gl
                dn, dh = nh - nl, hh - hl
                to_low, to_high = wl * g, wh * g
                of_slow = -(to_low * inv) * (dn - fast * dh)
                of_fast = -(to_high * inv) * (dn - slow * dh)
                return (to_low, to_high, sp * g) + speed_terms(slow, fast, of_slow, of_fast, slow_low, fast_low)

            partial_h, partial_u, partial_c, flow = [], [], [], []
            for j in every:
                hn, xn, un, cn = (at(state1, k, j, start + 1) for k in (0, 1, 3, 5))
                to_low, to_high, jump, u_low, c_low, u_high, c_high = face(
                    h[j], x[j], u[j], c[j], hn, xn, un, cn, lh[j], lam0[j, pl.ds(start + 1, 8), :], at(faces, 0, j, start)
                )
                of_u = u_low + previous_row(2, j, start, u_high)
                partial_h.append(previous_row(0, j, start, jump) - jump)
                partial_c.append(c_low + previous_row(3, j, start, c_high))
                partial_u.append(of_u * u[j])
                flow.append(to_low + previous_row(1, j, start, to_high) + of_u * r[j])
            hn, yn, vn, cn, ln = (next_col(q) for q in (h, y, v, c, lh))
            terms = [
                face(h[j], y[j], v[j], c[j], hn[j], yn[j], vn[j], cn[j], lh[j], ln[j], at(faces, 1, j, start))
                for j in every
            ]
            high, jump, u_high, c_high = (previous_col([t[k] for t in terms]) for k in (1, 2, 5, 6))
            for j in every:
                to_low, _, own_jump, u_low, c_low, _, _ = terms[j]
                of_v = u_low + u_high[j]
                of_c = partial_c[j] + c_low + c_high[j]
                of_h = partial_h[j] + (jump[j] - own_jump)
                of_h = of_h + r[j] * (0.5 * (of_c * c[j]) - partial_u[j] - of_v * v[j])
                lam[0, j, pl.ds(start, 8), :] = lh[j] + TIME_RATIO * of_h
                lam[1, j, pl.ds(start, 8), :] = TIME_RATIO * flow[j]
                lam[2, j, pl.ds(start, 8), :] = TIME_RATIO * (to_low + high[j] + of_v * r[j])
            return carry

        run(second_back)

        gradient = pick(0, lam.at[0], gradient)

        def first_back(i, carry):
            start = pl.multiple_of(i * 8, 8)
            h, x, y, u, v, c, r = [[at(state0, k, j, start) for j in every] for k in range(7)]
            lh, lx, ly = [[at(lam, k, j, start) for j in every] for k in range(3)]
            half = [(0.5 * GRAVITY) * h[j] * h[j] for j in every]
            cross = [x[j] * v[j] for j in every]

            def face(hl, nl, tl, ul, cl, pl_, kl, hh, nh, th, uh, ch, ph, kh, gl, gh, both):
                slow, fast, inv, wl, wh, sp, slow_low, fast_low = waves(ul, cl, uh, ch, both)
                g_h, g_n, g_t = (b - a for a, b in zip(gl, gh))
                dn = nh - nl
                of_flux = g_h * dn + g_n * (ph - pl_) + g_t * (kh - kl)
                of_jump = g_h * (hh - hl) + g_n * dn + g_t * (th - tl)
                of_slow = -(wl * inv) * (of_flux - fast * of_jump)
                of_fast = -(wh * inv) * (of_flux - slow * of_jump)
                return (wl * g_n, wl * g_t, wh * g_n, wh * g_t, sp * g_h) + speed_terms(
                    slow, fast, of_slow, of_fast, slow_low, fast_low
                )

            kept = []
            for j in every:
                hn, xn, yn, un, cn = (at(state0, k, j, start + 1) for k in (0, 1, 2, 3, 5))
                nl, tl, nh, th, jump, u_low, c_low, u_high, c_high = face(
                    h[j], x[j], y[j], u[j], c[j], x[j] * u[j] + half[j], cross[j],
                    hn, xn, yn, un, cn, xn * un + (0.5 * GRAVITY) * hn * hn, yn * un,
                    (lh[j], lx[j], ly[j]), tuple(at(lam, k, j, start + 1) for k in range(3)), at(faces, 0, j, start),
                )
                shut = lx[j] * at(walls, 1, j, start)
                normal = nl + previous_row(0, j, start, nh) - lx[j] * at(walls, 0, j, start)
                across = tl + previous_row(1, j, start, th)
                of_u = normal * x[j] + across * y[j] + u_low + previous_row(3, j, start, u_high) - shut * jnp.abs(x[j])
                of_c = c_low + previous_row(4, j, start, c_high) - shut * x[j]
                kept.append((normal, previous_row(2, j, start, jump) - jump, of_u * u[j], of_c))
            press = [y[j] * v[j] + half[j] for j in every]
            hn, xn, yn, vn, cn, pn, kn = (next_col(q) for q in (h, x, y, v, c, press, cross))
            lhn, lxn, lyn = (next_col(q) for q in (lh, lx, ly))
            terms = [
                face(
                    h[j], y[j], x[j], v[j], c[j], press[j], cross[j],
                    hn[j], yn[j], xn[j], vn[j], cn[j], pn[j], kn[j],
                    (lh[j], ly[j], lx[j]), (lhn[j], lyn[j], lxn[j]), at(faces, 1, j, start),
                )
                for j in every
            ]
            nh, th, jump, u_high, c_high = (previous_col([t[k] for t in terms]) for k in (2, 3, 4, 7, 8))
            for j in every:
                shut = ly[j] * at(walls, 3, j, start)
                normal = terms[j][0] + nh[j] - ly[j] * at(walls, 2, j, start)
                across = terms[j][1] + th[j]
                of_v = normal * y[j] + across * x[j] + terms[j][5] + u_high[j] - shut * jnp.abs(y[j])
                of_c = kept[j][3] + terms[j][6] + c_high[j] - shut * y[j]
                of_h = kept[j][1] + (jump[j] - terms[j][4]) + GRAVITY * h[j] * (kept[j][0] + normal)
                of_h = of_h + r[j] * (0.5 * (of_c * c[j]) - kept[j][2] - of_v * v[j])
                final[j, pl.ds(start, 8), :] = (1.0 / TIME_RATIO) * lh[j] + of_h
            return carry

        run(first_back)
        return gradient

    return forward, backward


def list_dams(dam_ref, listed, rows, cols, spots):
    total_cols = cols * lax.axis_size("gy")
    row_first = lax.axis_index("gx") * rows
    col_first = lax.axis_index("gy") * cols

    def local(cell):
        if total_cols & (total_cols - 1):
            row = lax.div(cell, jnp.full(jnp.shape(cell), total_cols, jnp.int32))
        else:
            row = lax.shift_right_logical(cell, jnp.full(jnp.shape(cell), total_cols.bit_length() - 1, jnp.int32))
        return row - row_first, cell - row * total_cols - col_first

    cells = dam_ref[...]
    none = cells.shape[1]
    number = lax.broadcasted_iota(jnp.int32, cells.shape, 1)
    row, col = local(cells)
    near = within(row, -REACH, rows + REACH) & within(col, -REACH, cols + REACH)
    number = jnp.where(near, number, none)

    def one(state):
        d, count = state
        row, col = local(jnp.max(jnp.where(number == d, cells, 0)))
        for held, spot in spots(row, col):
            @pl.when(held)
            def _():
                for k, value in enumerate((d,) + spot):
                    listed[k, count] = value

            count = count + jnp.where(held, 1, 0)
        return jnp.min(jnp.where(number > d, number, none)), count

    return lax.while_loop(lambda state: state[0] < none, one, (jnp.min(number), jnp.int32(0)))[1]


def within(value, first, end):
    return (value >= first) & (value < end)


def split(place):
    return lax.shift_right_logical(place, LANES.bit_length() - 1), place & (LANES - 1)


def inner_spots(rows, cols):
    def spots(row, col):
        tile, lane = split(col)
        own = within(row, REACH, rows - REACH) & within(col, REACH, cols - REACH)
        yield within(row, 0, rows) & within(col, 0, cols), (row, tile, lane, jnp.where(own, 1, 0))

    return spots


def ring(tiles):
    return [(j + 1) % tiles for j in range(tiles)], [(j - 1) % tiles for j in range(tiles)]


KEPT = ("state0", "state1", "faces", "walls", "lam0")


def inner_forward_kernel(
    h_ref, x_ref, y_ref, wet_ref, class_ref, rates_ref, dam_ref, release_ref,
    ends_ref, depth_ref, grad_ref, *rest,
):
    held = dict(zip(KEPT + ("listed", "mask", "weight", "last", "back"), rest))
    rows, cols = h_ref.shape
    tiles = cols // LANES
    chunks = rows // 8
    for end, (start, kept) in enumerate(((0, 0), (rows - EDGE, EDGE - REACH))):
        part = slice(start, start + EDGE)
        own = coded_fields(h_ref[part, :], x_ref[part, :], y_ref[part, :], wet_ref[part, :], class_ref[part, :])
        for index in range(FIELDS):
            ends_ref[end, index * REACH : (index + 1) * REACH, :] = own[index][kept : kept + REACH]
    dams = list_dams(dam_ref, held["listed"], rows, cols, inner_spots(rows, cols))

    def put(fill):
        def one(i, carry):
            part = pl.ds(pl.multiple_of(i * 8, 8), 8)
            for j in range(tiles):
                across = pl.ds(j * LANES, LANES)
                fill(
                    j, pl.multiple_of(i * 8, 8), wet_ref[part, across] > 0,
                    h_ref[part, across], x_ref[part, across], y_ref[part, across], class_ref[part, across],
                )
            return carry

        lax.fori_loop(0, chunks, one, 0, unroll=2)

    forward, _ = window(chunks, *ring(tiles), put, held["listed"], dams, rates_ref, release_ref, held)
    grad_ref[...] = forward()
    for j in range(tiles):
        across = slice(j * LANES, (j + 1) * LANES)
        depth_ref[:, across] = jnp.where(wet_ref[:, across] > 0, held["last"][j, :rows, :], h_ref[:, across])


def inner_backward_kernel(*refs):
    names = KEPT + ("dams", "grad_in", "adjoint", "grad", "listed", "lam", "back", "final")
    held = dict(zip(names, refs))
    rows, cols = held["adjoint"].shape
    tiles = cols // LANES
    dams = list_dams(held["dams"], held["listed"], rows, cols, inner_spots(rows, cols))
    shape = jax.ShapeDtypeStruct((held["dams"].shape[1],), jnp.float32)
    _, backward = window(rows // 8, *ring(tiles), None, held["listed"], dams, None, shape, held)
    held["grad"][...] = backward(held["grad_in"][...])
    for j in range(tiles):
        held["adjoint"][:, j * LANES : (j + 1) * LANES] = held["final"][j, :rows, :]


def frame_kernel(
    h_ref, x_ref, y_ref, wet_ref, class_ref, rates_ref, dam_ref, release_ref,
    depth_in, adjoint_in, grad_in, near_own, far_own, near_col, far_col, side_ref, near_row, far_row,
    depth_ref, adjoint_ref, grad_ref, *rest,
):
    rows, cols = h_ref.shape
    tiles = cols // LANES
    chunks = 4
    turned = tiles + 1
    after = [(j + 1) % turned for j in range(turned)] + [turned + 1, turned]
    before = [(j - 1) % turned for j in range(turned)] + [turned + 1, turned]

    def chunk_row(place, count):
        return jnp.where(place < EDGE, place + EDGE, place - count + 3 * EDGE)

    def near_end(place, count):
        return within(place, -REACH, EDGE) | within(place, count - EDGE, count + REACH)

    def at_end(place, count):
        return within(place, 0, REACH) | within(place, count - REACH, count)

    def spots(row, col):
        near = within(row, -REACH, rows + REACH) & within(col, -REACH, cols + REACH)
        tile, lane = split(jnp.where(col < 0, col + (tiles + 1) * LANES, col))
        own = at_end(row, rows) & within(col, 0, cols)
        yield near & near_end(row, rows), (chunk_row(row, rows), tile, lane, jnp.where(own, 1, 0))
        tile, lane = split(jnp.where(row < 0, row + 2 * LANES, row))
        own = at_end(col, cols) & within(row, REACH, rows - REACH)
        yield near & near_end(col, cols), (chunk_row(col, cols), tile + turned, lane, jnp.where(own, 1, 0))

    held = dict(zip(KEPT + ("listed", "mask", "weight", "last", "back", "lam", "final"), rest))
    dams = list_dams(dam_ref, held["listed"], rows, cols, spots)
    above, below = beside("gx", near_row, far_row)
    left, right = beside("gy", near_col, far_col)
    first_cols, last_cols = low_and_high("gy", near_own[...], far_own[...])

    def put(fill):
        blank = jnp.zeros((EDGE - REACH, LANES), jnp.float32)

        def coded(j, start, h, x, y, code):
            fill(j, start, h > 0.0, h, x, y, code.astype(jnp.int32))

        for j in range(tiles + 1):
            across = slice(j * LANES, (j + 1) * LANES)
            for start, strip in ((0, above), (3 * EDGE, below)):
                pieces = [strip[k * REACH : (k + 1) * REACH, across] for k in range(FIELDS)]
                coded(j, start, *(jnp.concatenate((blank, v) if start == 0 else (v, blank), axis=0) for v in pieces))
            for end, first in ((0, 0), (1, rows - EDGE)):
                start = (1 + end) * EDGE
                if j < tiles:
                    part = slice(first, first + EDGE)
                    fill(
                        j, start, wet_ref[part, across] > 0,
                        h_ref[part, across], x_ref[part, across], y_ref[part, across], class_ref[part, across],
                    )
                else:
                    coded(j, start, *(side_ref[end, k] for k in range(FIELDS)))
        order = (0, 2, 1, 3)
        for chunk, strip in enumerate((left, first_cols, last_cols, right)):
            coded(turned, chunk * EDGE, *(strip[k * EDGE : (k + 1) * EDGE] for k in order))
        strips = jnp.concatenate((above, below), axis=0)
        outer = strips[:, tiles * LANES :]
        mixed = jnp.zeros((2 * STRIP, LANES), jnp.float32)
        lane = lax.broadcasted_iota(jnp.int32, (2 * STRIP, LANES), 1)
        pieces = (
            (outer, LANES - EDGE),
            (strips[:, :LANES], 0),
            (strips[:, (tiles - 1) * LANES : tiles * LANES], LANES - EDGE),
            (outer, 0),
        )
        for chunk, (piece, first) in enumerate(pieces):
            moved = (chunk * EDGE - first) % LANES
            mixed = jnp.where(lane // EDGE == chunk, pltpu.roll(piece, moved, 1) if moved else piece, mixed)
        corners = jnp.concatenate((mixed, jnp.zeros((LANES - 2 * STRIP, LANES), jnp.float32)), axis=0).T
        corners = corners[: chunks * EDGE]
        lane = lax.broadcasted_iota(jnp.int32, (chunks * EDGE, LANES), 1)
        fields = []
        for k in order:
            from_above = pltpu.roll(corners, LANES - REACH - k * REACH, 1)
            from_below = pltpu.roll(corners, LANES - STRIP - k * REACH, 1)
            fields.append(jnp.where(lane < REACH, from_below, jnp.where(lane >= LANES - REACH, from_above, 0.0)))
        for chunk in range(chunks):
            coded(turned + 1, chunk * EDGE, *(v[chunk * EDGE : (chunk + 1) * EDGE] for v in fields))

    forward, backward = window(chunks, after, before, put, held["listed"], dams, rates_ref, release_ref, held)
    grad_ref[...] = jnp.broadcast_to(backward(forward() + grad_in[...]), grad_ref.shape)
    last, final = held["last"], held["final"]
    blank = jnp.zeros((LANES - 4 * EDGE, LANES), jnp.float32)
    ends = slice(EDGE, 3 * EDGE)
    columns = jnp.concatenate((last[turned, ends, :], final[turned, ends, :], blank), axis=0).T
    lane = lax.broadcasted_iota(jnp.int32, (rows, LANES), 1)
    row = lax.broadcasted_iota(jnp.int32, (EDGE, LANES), 0)
    for number, (ref, inner, strip) in enumerate(((depth_ref, depth_in, last), (adjoint_ref, adjoint_in, final))):
        for j in range(tiles):
            across = slice(j * LANES, (j + 1) * LANES)

            def wet_only(value, part):
                if number:
                    return value
                return jnp.where(wet_ref[part, across] > 0, value, h_ref[part, across])

            whole = slice(0, rows)
            block = inner[:, across]
            if j == 0:
                moved = (LANES - 2 * EDGE * number) % LANES
                edge = pltpu.roll(columns, moved, 1) if moved else columns
                block = jnp.where(lane < REACH, wet_only(edge, whole), block)
            if j == tiles - 1:
                edge = pltpu.roll(columns, LANES - 2 * EDGE - 2 * EDGE * number, 1)
                block = jnp.where(lane >= LANES - REACH, wet_only(edge, whole), block)
            middle = slice(EDGE, rows - EDGE)
            ref[middle, across] = block[middle]
            for part, start, own in (
                (slice(0, EDGE), EDGE, row < REACH),
                (slice(rows - EDGE, rows), 2 * EDGE, row >= EDGE - REACH),
            ):
                ref[part, across] = jnp.where(own, wet_only(strip[j, start : start + EDGE, :], part), block[part])


def total_kernel(parts_ref, out_ref):
    total = jnp.sum(parts_ref[...], axis=0, keepdims=True)
    steps, dams = out_ref.shape
    for step in range(steps):
        moved = pltpu.roll(total, LANES - step * dams, 1) if step else total
        out_ref[step : step + 1, :] = moved[:, :dams]


def on_device(
    water_depth, momentum_x, momentum_y, wet_mask, damage_class, damage_rates, dam_cell, releases
):
    rows, cols = water_depth.shape
    tiles = cols // LANES
    wide = cols + LANES
    rows_count = lax.axis_size("gx")
    cols_count = lax.axis_size("gy")
    vmem = pl.BlockSpec(memory_space=pltpu.VMEM)
    smem = pl.BlockSpec(memory_space=pltpu.SMEM)
    hbm = pl.BlockSpec(memory_space=pltpu.HBM)
    f32 = jnp.float32
    local = (water_depth, momentum_x, momentum_y, wet_mask, damage_class)
    given = (damage_rates, dam_cell.reshape(1, -1), releases)

    def swap(near, far, axis, count):
        near = lax.ppermute(near, axis, [(i, i + 1 - 2 * (i % 2)) for i in range(count)])
        return near, lax.ppermute(far, axis, [(i, (i - 1 + 2 * (i % 2)) % count) for i in range(count)])

    def array(*shape):
        return jax.ShapeDtypeStruct(shape, f32)

    def need(names, tiles, chunks):
        leads = dict(state0=(7,), state1=(7,), faces=(2,), walls=(4,), lam=(3,), back=(5,))
        return [array(*leads.get(name, ()), tiles, 8 * chunks + 8, LANES) for name in names]

    def scratch(names, tiles, chunks, spots):
        listed = pltpu.SMEM((5, spots), jnp.int32)
        return [listed] + [pltpu.VMEM(v.shape, v.dtype) for v in need(names, tiles, chunks)]

    own = pl.pallas_call(
        edge_kernel,
        out_shape=[array(FIELDS * EDGE, rows)] * 2,
        in_specs=[hbm] * 5,
        out_specs=[vmem] * 2,
        scratch_shapes=[
            pltpu.VMEM((2, 3, rows, LANES), f32),
            pltpu.VMEM((2, 2, rows, LANES), jnp.int32),
            pltpu.SemaphoreType.DMA((2, 5)),
        ],
        compiler_params=pltpu.CompilerParams(vmem_limit_bytes=60 * 1024 * 1024),
        cost_estimate=pl.CostEstimate(flops=10**9, bytes_accessed=4 * 10**7, transcendentals=0),
        name="edges",
    )(*local)
    beside_cols = swap(*own, "gy", cols_count)
    kept = need(KEPT, tiles, rows // 8)
    dams = dam_cell.shape[0]
    inner_params = pltpu.CompilerParams(vmem_limit_bytes=16 * 1024 * 1024)
    ends, depth, gradient, *kept = pl.pallas_call(
        inner_forward_kernel,
        out_shape=[array(2, STRIP, cols), array(rows, cols), array(1, LANES)] + kept,
        in_specs=[vmem] * 5 + [smem, vmem, smem],
        out_specs=[vmem] * (3 + len(kept)),
        scratch_shapes=scratch(("mask", "weight", "last", "back"), tiles, rows // 8, dams),
        compiler_params=inner_params,
        cost_estimate=pl.CostEstimate(flops=200 * rows * cols, bytes_accessed=6 * 4 * rows * cols, transcendentals=0),
        name="inner_forward",
    )(*local, *given)
    side, *to_rows = pl.pallas_call(
        corner_kernel,
        out_shape=[array(2, FIELDS, EDGE, LANES), array(STRIP, wide), array(STRIP, wide)],
        in_specs=[vmem] * 3,
        out_specs=[vmem] * 3,
        compiler_params=inner_params,
        name="corners",
    )(ends, *beside_cols)
    adjoint, gradient = pl.pallas_call(
        inner_backward_kernel,
        out_shape=[array(rows, cols), array(1, LANES)],
        in_specs=[vmem] * (len(kept) + 2),
        out_specs=[vmem] * 2,
        scratch_shapes=scratch(("lam", "back", "final"), tiles, rows // 8, dams),
        compiler_params=inner_params,
        cost_estimate=pl.CostEstimate(flops=300 * rows * cols, bytes_accessed=6 * 4 * rows * cols, transcendentals=0),
        name="inner_backward",
    )(*kept, given[1], gradient)
    beside_rows = swap(*to_rows, "gx", rows_count)
    depth, adjoint, parts = pl.pallas_call(
        frame_kernel,
        out_shape=[array(rows, cols), array(rows, cols), array(rows_count * cols_count, LANES)],
        in_specs=[vmem] * 5 + [smem, vmem, smem] + [vmem] * 10,
        out_specs=[vmem] * 3,
        scratch_shapes=(
            [pltpu.VMEM(v.shape, v.dtype) for v in need(KEPT, tiles + 3, 4)]
            + scratch(("mask", "weight", "last", "back", "lam", "final"), tiles + 3, 4, 2 * dams)
        ),
        compiler_params=inner_params,
        name="frame",
    )(*local, *given, depth, adjoint, gradient, *own, *beside_cols, side, *beside_rows)
    gathered = lax.all_to_all(parts, ("gx", "gy"), 0, 0)
    release_grad = pl.pallas_call(
        total_kernel,
        out_shape=array(releases.shape[1], releases.shape[0]),
        in_specs=[vmem],
        out_specs=vmem,
        compiler_params=inner_params,
        name="total",
    )(gathered)
    return (depth, adjoint, release_grad.T)


def solution(mesh):
    in_specs = (P("gx", "gy"),) * 5 + (P(), P(), P())
    out_specs = (P("gx", "gy"), P("gx", "gy"), P())
    return jax.shard_map(
        on_device, mesh=mesh, in_specs=in_specs, out_specs=out_specs, check_vma=False
    )
```

```python
import itertools

import jax
import jax.numpy as jnp
from jax import lax
from jax.experimental import pallas as pl
from jax.experimental.pallas import tpu as pltpu
from jax.sharding import PartitionSpec as P

GRAVITY = 9.81
TIME_RATIO = 0.05
INFLOW_GAIN = 0.25

LANES = 128
REACH = 4
EDGE = 8
FIELDS = 4
STRIP = FIELDS * REACH
UNROLL = True


def class_rate(classes, rates_ref):
    rate = jnp.full(classes.shape, rates_ref[0], jnp.float32)
    for index in range(1, rates_ref.shape[0]):
        rate = jnp.where(classes == index, rates_ref[index], rate)
    return rate


def coded_fields(h, x, y, wet, classes):
    return jnp.where(wet > 0, h, 0.0), x, y, classes.astype(jnp.float32)


def is_even(axis):
    return (lax.axis_index(axis) & 1) == 0


def low_and_high(axis, near, far):
    even = is_even(axis)
    return jnp.where(even, far, near), jnp.where(even, near, far)


def edge_kernel(h_hbm, x_hbm, y_hbm, wet_hbm, class_hbm, near_ref, far_ref, values, codes, sems):
    rows, cols = h_hbm.shape
    copies = []
    for index, source in enumerate((h_hbm, x_hbm, y_hbm, wet_hbm, class_hbm)):
        for side in range(2):
            kept = values.at[side, index] if index < 3 else codes.at[side, index - 3]
            part = source.at[:, pl.ds(side * (cols - LANES), LANES)]
            copies.append(pltpu.make_async_copy(part, kept, sems.at[side, index]))
    for copy in copies:
        copy.start()
    for copy in copies:
        copy.wait()
    lane = lax.broadcasted_iota(jnp.int32, (rows, LANES), 1)
    mixed = jnp.zeros((rows, LANES), jnp.float32)
    for side in range(2):
        fields = coded_fields(*(values[side, k] for k in range(3)), *(codes[side, k] for k in range(2)))
        for index, field in enumerate(fields):
            first = (side * FIELDS + index) * EDGE
            moved = first if side == 0 else first + EDGE
            shifted = pltpu.roll(field, moved, 1) if moved else field
            mixed = jnp.where((lane >= first) & (lane < first + EDGE), shifted, mixed)
    turned = mixed.T
    far_ref[...], near_ref[...] = low_and_high("gy", turned[FIELDS * EDGE : 2 * FIELDS * EDGE], turned[: FIELDS * EDGE])


def beside(axis, near_ref, far_ref):
    place = lax.axis_index(axis)
    low, high = low_and_high(axis, near_ref[...], far_ref[...])
    return jnp.where(place > 0, low, 0.0), jnp.where(place < lax.axis_size(axis) - 1, high, 0.0)


def corner_kernel(ends_ref, near_in, far_in, side_ref, near_ref, far_ref):
    rows = near_in.shape[1]
    cols = ends_ref.shape[2]
    even = is_even("gx")
    left, right = beside("gy", near_in, far_in)
    blank = jnp.zeros((LANES - 2 * FIELDS * EDGE, rows), jnp.float32)
    turned = jnp.concatenate((right, left, blank), axis=0).T
    lane = lax.broadcasted_iota(jnp.int32, (EDGE, LANES), 1)
    strips = []
    for end, start, kept in ((0, 0, 0), (1, rows - EDGE, EDGE - REACH)):
        part = turned[start : start + EDGE]
        pieces = []
        for index in range(FIELDS):
            upper = pltpu.roll(part, LANES - index * EDGE, 1) if index else part
            lower = pltpu.roll(part, LANES - (1 + FIELDS + index) * EDGE, 1)
            tile = jnp.where(lane < EDGE, upper, jnp.where(lane >= LANES - EDGE, lower, 0.0))
            side_ref[end, index] = tile
            pieces.append(tile[kept : kept + REACH])
        strips.append((ends_ref[end], jnp.concatenate(pieces, axis=0)))
    for part, low, high in zip((slice(0, cols), slice(cols, cols + LANES)), *strips):
        near_ref[:, part] = jnp.where(even, high, low)
        far_ref[:, part] = jnp.where(even, low, high)


def cell_terms(height, flow_x, flow_y):
    scaled = GRAVITY * height
    inverse = pltpu.reciprocal(height, approx=True)
    return flow_x * inverse, flow_y * inverse, scaled * lax.rsqrt(scaled), inverse


def waves(u_low, c_low, u_high, c_high, both):
    slow_low, slow_high = u_low - c_low, u_high - c_high
    fast_low, fast_high = u_low + c_low, u_high + c_high
    slowest = jnp.minimum(jnp.minimum(slow_low, slow_high), 0.0)
    fastest = jnp.maximum(jnp.maximum(fast_low, fast_high), 0.0)
    inverse = both * pltpu.reciprocal(fastest - slowest, approx=True)
    share_low = fastest * inverse
    share_high = -(slowest * inverse)
    spread = slowest * share_low
    return slowest, fastest, inverse, share_low, share_high, spread, slow_low <= slow_high, fast_low >= fast_high


def speed_terms(slowest, fastest, of_slowest, of_fastest, slow_is_low, fast_is_low):
    of_slowest = jnp.where(slowest < 0.0, of_slowest, 0.0)
    of_fastest = jnp.where(fastest > 0.0, of_fastest, 0.0)
    slow_to_low = jnp.where(slow_is_low, of_slowest, 0.0)
    fast_to_low = jnp.where(fast_is_low, of_fastest, 0.0)
    slow_to_high = of_slowest - slow_to_low
    fast_to_high = of_fastest - fast_to_low
    return (
        fast_to_low + slow_to_low,
        fast_to_low - slow_to_low,
        fast_to_high + slow_to_high,
        fast_to_high - slow_to_high,
    )


def window(chunks, after, before, put, listed, dams, rates_ref, release_ref, held):
    state0, state1, mask, faces, walls, weight, last, lam0, lam, back, final = (
        held.get(name) for name in (
            "state0", "state1", "mask", "faces", "walls", "weight", "last", "lam0", "lam", "back", "final",
        )
    )
    tiles = len(after)
    every = range(tiles)
    lane = lax.broadcasted_iota(jnp.int32, (8, LANES), 1)

    def at(ref, k, j, start):
        return ref[k, j, pl.ds(start, 8), :]

    def next_col(values):
        rolled = [pltpu.roll(v, LANES - 1, 1) for v in values]
        return [jnp.where(lane == LANES - 1, rolled[after[j]], rolled[j]) for j in every]

    def previous_col(values):
        rolled = [pltpu.roll(v, 1, 1) for v in values]
        return [jnp.where(lane == 0, rolled[before[j]], rolled[j]) for j in every]

    def previous_row(slot, j, start, value):
        back[slot, j, pl.ds(start + 8, 8), :] = value
        return back[slot, j, pl.ds(start + 7, 8), :]

    def put_cell(ref, j, start, height, flow_x, flow_y):
        u, v, c, inverse = cell_terms(height, flow_x, flow_y)
        for k, value in enumerate((height, flow_x, flow_y, u, v, c, inverse)):
            ref[k, j, pl.ds(start, 8), :] = value

    def fill(j, start, wet, height, flow_x, flow_y, classes):
        put_cell(
            state0, j, start,
            jnp.where(wet, height, 1.0), jnp.where(wet, flow_x, 0.0), jnp.where(wet, flow_y, 0.0),
        )
        mask[j, pl.ds(start, 8), :] = jnp.where(wet, 1.0, 0.0)
        weight[j, pl.ds(start, 8), :] = jnp.where(wet, class_rate(classes, rates_ref), 0.0)

    def clear(ref, start, value=0.0):
        index = tuple(range(n) for n in ref.shape[:-2])
        for lead in itertools.product(*index):
            ref[lead + (pl.ds(start, 8), slice(None))] = jnp.full((8, LANES), value, jnp.float32)

    def run(step, count=chunks):
        lax.fori_loop(0, count, step, 0, unroll=UNROLL)

    def add_inflow(step, ref, refresh):
        def one(index, carry):
            d, row, j, col = (listed[k, index] for k in range(4))
            if refresh:
                old = [ref[k, j, pl.ds(row, 1), :] for k in range(3)]
            else:
                old = [ref[j, pl.ds(row, 1), :]]
            here = lax.broadcasted_iota(jnp.int32, (1, LANES), 1) == col
            height = old[0] + jnp.where(here, INFLOW_GAIN * release_ref[step, d], 0.0)
            if refresh:
                terms = (height, old[1], old[2]) + cell_terms(height, old[1], old[2])
                for k, value in enumerate(terms):
                    ref[k, j, pl.ds(row, 1), :] = value
            else:
                ref[j, pl.ds(row, 1), :] = height
            return carry

        lax.fori_loop(0, dams, one, 0)

    def pick(step, ref, gradient):
        lane_row = lax.broadcasted_iota(jnp.int32, (1, LANES), 1)

        def one(index, total):
            d, row, j, col, inside = (listed[k, index] for k in range(5))
            values = ref[j, pl.ds(row, 1), :]
            value = jnp.sum(jnp.where(lane_row == col, values, 0.0), axis=1, keepdims=True)
            spot = (lane_row == d + step * release_ref.shape[1]) & (inside > 0)
            return total + jnp.where(spot, (INFLOW_GAIN / TIME_RATIO) * value, 0.0)

        return lax.fori_loop(0, dams, one, gradient)

    def forward():
        clear(back, 0)
        for ref in (state0, state1):
            for k in range(7):
                clear(ref.at[k], chunks * 8, 1.0 if k in (0, 5, 6) else 0.0)
        clear(mask, chunks * 8)
        clear(lam0, chunks * 8)
        put(fill)

        def first_step(i, carry):
            start = pl.multiple_of(i * 8, 8)
            low = [[at(state0, k, j, start) for j in every] for k in range(6)]
            h, x, y, u, v, c = low
            m = [mask[j, pl.ds(start, 8), :] for j in every]
            half = [(0.5 * GRAVITY) * h[j] * h[j] for j in every]
            cross = [x[j] * v[j] for j in every]
            press_x = [x[j] * u[j] + half[j] for j in every]
            press_y = [y[j] * v[j] + half[j] for j in every]
            gain = []
            for j in every:
                hn, xn, yn, un, cn = (at(state0, k, j, start + 1) for k in (0, 1, 2, 3, 5))
                both = m[j] * mask[j, pl.ds(start + 1, 8), :]
                faces[0, j, pl.ds(start, 8), :] = both
                _, _, _, wl, wh, sp, _, _ = waves(u[j], c[j], un, cn, both)
                fh = wl * x[j] + wh * xn + sp * (hn - h[j])
                fn = wl * press_x[j] + wh * (xn * un + (0.5 * GRAVITY) * hn * hn) + sp * (xn - x[j])
                ft = wl * cross[j] + wh * (yn * un) + sp * (yn - y[j])
                both_low = previous_row(0, j, start, both)
                tilt = both_low - both
                shut = 2.0 * m[j] - both - both_low
                walls[0, j, pl.ds(start, 8), :] = tilt
                walls[1, j, pl.ds(start, 8), :] = shut
                gain.append(
                    [
                        fh - previous_row(1, j, start, fh),
                        fn - previous_row(2, j, start, fn) + tilt * press_x[j] + shut * ((jnp.abs(u[j]) + c[j]) * x[j]),
                        ft - previous_row(3, j, start, ft),
                    ]
                )
            hn, xn, yn, vn, cn, pn, tn, mn = (next_col(q) for q in (h, x, y, v, c, press_y, cross, m))
            flux = [[], [], []]
            both_up = []
            for j in every:
                both = m[j] * mn[j]
                faces[1, j, pl.ds(start, 8), :] = both
                both_up.append(both)
                _, _, _, wl, wh, sp, _, _ = waves(v[j], c[j], vn[j], cn[j], both)
                flux[0].append(wl * y[j] + wh * yn[j] + sp * (hn[j] - h[j]))
                flux[1].append(wl * press_y[j] + wh * pn[j] + sp * (yn[j] - y[j]))
                flux[2].append(wl * cross[j] + wh * tn[j] + sp * (xn[j] - x[j]))
            flux_low = [previous_col(q) for q in flux]
            both_low = previous_col(both_up)
            for j in every:
                tilt = both_low[j] - both_up[j]
                shut = 2.0 * m[j] - both_up[j] - both_low[j]
                walls[2, j, pl.ds(start, 8), :] = tilt
                walls[3, j, pl.ds(start, 8), :] = shut
                change_h = gain[j][0] + (flux[0][j] - flux_low[0][j])
                change_x = gain[j][1] + (flux[2][j] - flux_low[2][j])
                change_y = gain[j][2] + (flux[1][j] - flux_low[1][j])
                change_y = change_y + tilt * press_y[j] + shut * ((jnp.abs(v[j]) + c[j]) * y[j])
                put_cell(
                    state1, j, start,
                    h[j] - TIME_RATIO * change_h, x[j] - TIME_RATIO * change_x, y[j] - TIME_RATIO * change_y,
                )
            return carry

        run(first_step)
        add_inflow(0, state1, True)

        def second_step(i, carry):
            start = pl.multiple_of(i * 8, 8)
            h, x, y, u, v, c = [[at(state1, k, j, start) for j in every] for k in range(6)]
            gain = []
            for j in every:
                hn, xn, un, cn = (at(state1, k, j, start + 1) for k in (0, 1, 3, 5))
                _, _, _, wl, wh, sp, _, _ = waves(u[j], c[j], un, cn, at(faces, 0, j, start))
                fh = wl * x[j] + wh * xn + sp * (hn - h[j])
                gain.append(fh - previous_row(0, j, start, fh))
            hn, yn, vn, cn = (next_col(q) for q in (h, y, v, c))
            flux = []
            for j in every:
                _, _, _, wl, wh, sp, _, _ = waves(v[j], c[j], vn[j], cn[j], at(faces, 1, j, start))
                flux.append(wl * y[j] + wh * yn[j] + sp * (hn[j] - h[j]))
            flux_low = previous_col(flux)
            for j in every:
                last[j, pl.ds(start, 8), :] = h[j] - TIME_RATIO * (gain[j] + (flux[j] - flux_low[j]))
            return carry

        run(second_step)
        add_inflow(1, last, False)

        def finish_depth(i, carry):
            start = pl.multiple_of(i * 8, 8)
            for j in every:
                height = last[j, pl.ds(start, 8), :]
                lam0[j, pl.ds(start, 8), :] = TIME_RATIO * (weight[j, pl.ds(start, 8), :] * height)
            return carry

        run(finish_depth)

        return pick(1, lam0, jnp.zeros((1, LANES), jnp.float32))


    def backward(gradient):
        clear(back, 0)
        clear(lam, chunks * 8)

        def second_back(i, carry):
            start = pl.multiple_of(i * 8, 8)
            h, x, y, u, v, c, r = [[at(state1, k, j, start) for j in every] for k in range(7)]
            lh = [lam0[j, pl.ds(start, 8), :] for j in every]

            def face(hl, nl, ul, cl, hh, nh, uh, ch, gl, gh, both):
                slow, fast, inv, wl, wh, sp, slow_low, fast_low = waves(ul, cl, uh, ch, both)
                g = gh - gl
                dn, dh = nh - nl, hh - hl
                to_low, to_high = wl * g, wh * g
                of_slow = -(to_low * inv) * (dn - fast * dh)
                of_fast = -(to_high * inv) * (dn - slow * dh)
                return (to_low, to_high, sp * g) + speed_terms(slow, fast, of_slow, of_fast, slow_low, fast_low)

            partial_h, partial_u, partial_c, flow = [], [], [], []
            for j in every:
                hn, xn, un, cn = (at(state1, k, j, start + 1) for k in (0, 1, 3, 5))
                to_low, to_high, jump, u_low, c_low, u_high, c_high = face(
                    h[j], x[j], u[j], c[j], hn, xn, un, cn, lh[j], lam0[j, pl.ds(start + 1, 8), :], at(faces, 0, j, start)
                )
                of_u = u_low + previous_row(2, j, start, u_high)
                partial_h.append(previous_row(0, j, start, jump) - jump)
                partial_c.append(c_low + previous_row(3, j, start, c_high))
                partial_u.append(of_u * u[j])
                flow.append(to_low + previous_row(1, j, start, to_high) + of_u * r[j])
            hn, yn, vn, cn, ln = (next_col(q) for q in (h, y, v, c, lh))
            terms = [
                face(h[j], y[j], v[j], c[j], hn[j], yn[j], vn[j], cn[j], lh[j], ln[j], at(faces, 1, j, start))
                for j in every
            ]
            high, jump, u_high, c_high = (previous_col([t[k] for t in terms]) for k in (1, 2, 5, 6))
            for j in every:
                to_low, _, own_jump, u_low, c_low, _, _ = terms[j]
                of_v = u_low + u_high[j]
                of_c = partial_c[j] + c_low + c_high[j]
                of_h = partial_h[j] + (jump[j] - own_jump)
                of_h = of_h + r[j] * (0.5 * (of_c * c[j]) - partial_u[j] - of_v * v[j])
                lam[0, j, pl.ds(start, 8), :] = lh[j] + TIME_RATIO * of_h
                lam[1, j, pl.ds(start, 8), :] = TIME_RATIO * flow[j]
                lam[2, j, pl.ds(start, 8), :] = TIME_RATIO * (to_low + high[j] + of_v * r[j])
            return carry

        run(second_back)

        gradient = pick(0, lam.at[0], gradient)

        def first_back(i, carry):
            start = pl.multiple_of(i * 8, 8)
            h, x, y, u, v, c, r = [[at(state0, k, j, start) for j in every] for k in range(7)]
            lh, lx, ly = [[at(lam, k, j, start) for j in every] for k in range(3)]
            half = [(0.5 * GRAVITY) * h[j] * h[j] for j in every]
            cross = [x[j] * v[j] for j in every]

            def face(hl, nl, tl, ul, cl, pl_, kl, hh, nh, th, uh, ch, ph, kh, gl, gh, both):
                slow, fast, inv, wl, wh, sp, slow_low, fast_low = waves(ul, cl, uh, ch, both)
                g_h, g_n, g_t = (b - a for a, b in zip(gl, gh))
                dn = nh - nl
                of_flux = g_h * dn + g_n * (ph - pl_) + g_t * (kh - kl)
                of_jump = g_h * (hh - hl) + g_n * dn + g_t * (th - tl)
                of_slow = -(wl * inv) * (of_flux - fast * of_jump)
                of_fast = -(wh * inv) * (of_flux - slow * of_jump)
                return (wl * g_n, wl * g_t, wh * g_n, wh * g_t, sp * g_h) + speed_terms(
                    slow, fast, of_slow, of_fast, slow_low, fast_low
                )

            kept = []
            for j in every:
                hn, xn, yn, un, cn = (at(state0, k, j, start + 1) for k in (0, 1, 2, 3, 5))
                nl, tl, nh, th, jump, u_low, c_low, u_high, c_high = face(
                    h[j], x[j], y[j], u[j], c[j], x[j] * u[j] + half[j], cross[j],
                    hn, xn, yn, un, cn, xn * un + (0.5 * GRAVITY) * hn * hn, yn * un,
                    (lh[j], lx[j], ly[j]), tuple(at(lam, k, j, start + 1) for k in range(3)), at(faces, 0, j, start),
                )
                shut = lx[j] * at(walls, 1, j, start)
                normal = nl + previous_row(0, j, start, nh) - lx[j] * at(walls, 0, j, start)
                across = tl + previous_row(1, j, start, th)
                of_u = normal * x[j] + across * y[j] + u_low + previous_row(3, j, start, u_high) - shut * jnp.abs(x[j])
                of_c = c_low + previous_row(4, j, start, c_high) - shut * x[j]
                kept.append((normal, previous_row(2, j, start, jump) - jump, of_u * u[j], of_c))
            press = [y[j] * v[j] + half[j] for j in every]
            hn, xn, yn, vn, cn, pn, kn = (next_col(q) for q in (h, x, y, v, c, press, cross))
            lhn, lxn, lyn = (next_col(q) for q in (lh, lx, ly))
            terms = [
                face(
                    h[j], y[j], x[j], v[j], c[j], press[j], cross[j],
                    hn[j], yn[j], xn[j], vn[j], cn[j], pn[j], kn[j],
                    (lh[j], ly[j], lx[j]), (lhn[j], lyn[j], lxn[j]), at(faces, 1, j, start),
                )
                for j in every
            ]
            nh, th, jump, u_high, c_high = (previous_col([t[k] for t in terms]) for k in (2, 3, 4, 7, 8))
            for j in every:
                shut = ly[j] * at(walls, 3, j, start)
                normal = terms[j][0] + nh[j] - ly[j] * at(walls, 2, j, start)
                across = terms[j][1] + th[j]
                of_v = normal * y[j] + across * x[j] + terms[j][5] + u_high[j] - shut * jnp.abs(y[j])
                of_c = kept[j][3] + terms[j][6] + c_high[j] - shut * y[j]
                of_h = kept[j][1] + (jump[j] - terms[j][4]) + GRAVITY * h[j] * (kept[j][0] + normal)
                of_h = of_h + r[j] * (0.5 * (of_c * c[j]) - kept[j][2] - of_v * v[j])
                final[j, pl.ds(start, 8), :] = (1.0 / TIME_RATIO) * lh[j] + of_h
            return carry

        run(first_back, held.get("needed", chunks))
        return gradient

    return forward, backward


def list_dams(dam_ref, listed, rows, cols, spots):
    total_cols = cols * lax.axis_size("gy")
    row_first = lax.axis_index("gx") * rows
    col_first = lax.axis_index("gy") * cols

    def local(cell):
        if total_cols & (total_cols - 1):
            row = lax.div(cell, jnp.full(jnp.shape(cell), total_cols, jnp.int32))
        else:
            row = lax.shift_right_logical(cell, jnp.full(jnp.shape(cell), total_cols.bit_length() - 1, jnp.int32))
        return row - row_first, cell - row * total_cols - col_first

    cells = dam_ref[...]
    none = cells.shape[1]
    number = lax.broadcasted_iota(jnp.int32, cells.shape, 1)
    row, col = local(cells)
    near = within(row, -REACH, rows + REACH) & within(col, -REACH, cols + REACH)
    number = jnp.where(near, number, none)

    def one(state):
        d, count = state
        row, col = local(jnp.max(jnp.where(number == d, cells, 0)))
        for held, spot in spots(row, col):
            @pl.when(held)
            def _():
                for k, value in enumerate((d,) + spot):
                    listed[k, count] = value

            count = count + jnp.where(held, 1, 0)
        return jnp.min(jnp.where(number > d, number, none)), count

    return lax.while_loop(lambda state: state[0] < none, one, (jnp.min(number), jnp.int32(0)))[1]


def within(value, first, end):
    return (value >= first) & (value < end)


def split(place):
    return lax.shift_right_logical(place, LANES.bit_length() - 1), place & (LANES - 1)


def inner_spots(rows, cols):
    def spots(row, col):
        tile, lane = split(col)
        own = within(row, REACH, rows - REACH) & within(col, REACH, cols - REACH)
        yield within(row, 0, rows) & within(col, 0, cols), (row, tile, lane, jnp.where(own, 1, 0))

    return spots


def ring(tiles):
    return [(j + 1) % tiles for j in range(tiles)], [(j - 1) % tiles for j in range(tiles)]


KEPT = ("state0", "state1", "faces", "walls", "lam0")


def inner_forward_kernel(
    h_ref, x_ref, y_ref, wet_ref, class_ref, rates_ref, dam_ref, release_ref,
    ends_ref, depth_ref, grad_ref, *rest,
):
    held = dict(zip(KEPT + ("listed", "mask", "weight", "last", "back"), rest))
    rows, cols = h_ref.shape
    tiles = cols // LANES
    chunks = rows // 8
    for end, (start, kept) in enumerate(((0, 0), (rows - EDGE, EDGE - REACH))):
        part = slice(start, start + EDGE)
        own = coded_fields(h_ref[part, :], x_ref[part, :], y_ref[part, :], wet_ref[part, :], class_ref[part, :])
        for index in range(FIELDS):
            ends_ref[end, index * REACH : (index + 1) * REACH, :] = own[index][kept : kept + REACH]
    dams = list_dams(dam_ref, held["listed"], rows, cols, inner_spots(rows, cols))

    def put(fill):
        def one(i, carry):
            part = pl.ds(pl.multiple_of(i * 8, 8), 8)
            for j in range(tiles):
                across = pl.ds(j * LANES, LANES)
                fill(
                    j, pl.multiple_of(i * 8, 8), wet_ref[part, across] > 0,
                    h_ref[part, across], x_ref[part, across], y_ref[part, across], class_ref[part, across],
                )
            return carry

        lax.fori_loop(0, chunks, one, 0, unroll=2)

    forward, _ = window(chunks, *ring(tiles), put, held["listed"], dams, rates_ref, release_ref, held)
    grad_ref[...] = forward()
    for j in range(tiles):
        across = slice(j * LANES, (j + 1) * LANES)
        depth_ref[:, across] = jnp.where(wet_ref[:, across] > 0, held["last"][j, :rows, :], h_ref[:, across])


def inner_backward_kernel(*refs):
    names = KEPT + ("dams", "grad_in", "adjoint", "grad", "listed", "lam", "back", "final")
    held = dict(zip(names, refs))
    rows, cols = held["adjoint"].shape
    tiles = cols // LANES
    dams = list_dams(held["dams"], held["listed"], rows, cols, inner_spots(rows, cols))
    shape = jax.ShapeDtypeStruct((1, held["dams"].shape[1]), jnp.float32)
    _, backward = window(rows // 8, *ring(tiles), None, held["listed"], dams, None, shape, held)
    held["grad"][...] = backward(held["grad_in"][...])
    for j in range(tiles):
        held["adjoint"][:, j * LANES : (j + 1) * LANES] = held["final"][j, :rows, :]


def frame_kernel(
    h_ref, x_ref, y_ref, wet_ref, class_ref, rates_ref, dam_ref, release_ref,
    depth_in, adjoint_in, grad_in, near_own, far_own, near_col, far_col, side_ref, near_row, far_row,
    depth_ref, adjoint_ref, grad_ref, *rest,
):
    rows, cols = h_ref.shape
    tiles = cols // LANES
    chunks = 4
    turned = tiles + 1
    after = [(j + 1) % turned for j in range(turned)] + [turned + 1, turned]
    before = [(j - 1) % turned for j in range(turned)] + [turned + 1, turned]

    def chunk_row(place, count):
        return jnp.where(place < EDGE, place + EDGE, place - count + 3 * EDGE)

    def near_end(place, count):
        return within(place, -REACH, EDGE) | within(place, count - EDGE, count + REACH)

    def at_end(place, count):
        return within(place, 0, REACH) | within(place, count - REACH, count)

    def spots(row, col):
        near = within(row, -REACH, rows + REACH) & within(col, -REACH, cols + REACH)
        tile, lane = split(jnp.where(col < 0, col + (tiles + 1) * LANES, col))
        own = at_end(row, rows) & within(col, 0, cols)
        yield near & near_end(row, rows), (chunk_row(row, rows), tile, lane, jnp.where(own, 1, 0))
        tile, lane = split(jnp.where(row < 0, row + 2 * LANES, row))
        own = at_end(col, cols) & within(row, REACH, rows - REACH)
        yield near & near_end(col, cols), (chunk_row(col, cols), tile + turned, lane, jnp.where(own, 1, 0))

    names = KEPT + ("listed", "mask", "weight", "last", "back", "lam", "final")
    held = dict(zip(names + ("row_patch", "column_patch", "sems"), rest))
    dams = list_dams(dam_ref, held["listed"], rows, cols, spots)
    above, below = beside("gx", near_row, far_row)
    left, right = beside("gy", near_col, far_col)
    first_cols, last_cols = low_and_high("gy", near_own[...], far_own[...])

    def put(fill):
        blank = jnp.zeros((EDGE - REACH, LANES), jnp.float32)

        def coded(j, start, h, x, y, code):
            fill(j, start, h > 0.0, h, x, y, code.astype(jnp.int32))

        for j in range(tiles + 1):
            across = slice(j * LANES, (j + 1) * LANES)
            for start, strip in ((0, above), (3 * EDGE, below)):
                pieces = [strip[k * REACH : (k + 1) * REACH, across] for k in range(FIELDS)]
                coded(j, start, *(jnp.concatenate((blank, v) if start == 0 else (v, blank), axis=0) for v in pieces))
            for end, first in ((0, 0), (1, rows - EDGE)):
                start = (1 + end) * EDGE
                if j < tiles:
                    part = slice(first, first + EDGE)
                    fill(
                        j, start, wet_ref[part, across] > 0,
                        h_ref[part, across], x_ref[part, across], y_ref[part, across], class_ref[part, across],
                    )
                else:
                    coded(j, start, *(side_ref[end, k] for k in range(FIELDS)))
        order = (0, 2, 1, 3)
        for chunk, strip in enumerate((left, first_cols, last_cols, right)):
            coded(turned, chunk * EDGE, *(strip[k * EDGE : (k + 1) * EDGE] for k in order))
        strips = jnp.concatenate((above, below), axis=0)
        outer = strips[:, tiles * LANES :]
        mixed = jnp.zeros((2 * STRIP, LANES), jnp.float32)
        lane = lax.broadcasted_iota(jnp.int32, (2 * STRIP, LANES), 1)
        pieces = (
            (outer, LANES - EDGE),
            (strips[:, :LANES], 0),
            (strips[:, (tiles - 1) * LANES : tiles * LANES], LANES - EDGE),
            (outer, 0),
        )
        for chunk, (piece, first) in enumerate(pieces):
            moved = (chunk * EDGE - first) % LANES
            mixed = jnp.where(lane // EDGE == chunk, pltpu.roll(piece, moved, 1) if moved else piece, mixed)
        corners = jnp.concatenate((mixed, jnp.zeros((LANES - 2 * STRIP, LANES), jnp.float32)), axis=0).T
        corners = corners[: chunks * EDGE]
        lane = lax.broadcasted_iota(jnp.int32, (chunks * EDGE, LANES), 1)
        fields = []
        for k in order:
            from_above = pltpu.roll(corners, LANES - REACH - k * REACH, 1)
            from_below = pltpu.roll(corners, LANES - STRIP - k * REACH, 1)
            fields.append(jnp.where(lane < REACH, from_below, jnp.where(lane >= LANES - REACH, from_above, 0.0)))
        for chunk in range(chunks):
            coded(turned + 1, chunk * EDGE, *(v[chunk * EDGE : (chunk + 1) * EDGE] for v in fields))

    held["needed"] = chunks - 1
    forward, backward = window(chunks, after, before, put, held["listed"], dams, rates_ref, release_ref, held)
    row_patch, column_patch, sems = held["row_patch"], held["column_patch"], held["sems"]
    lane = lax.broadcasted_iota(jnp.int32, (rows, LANES), 1)
    row = lax.broadcasted_iota(jnp.int32, (EDGE, LANES), 0)
    middle = slice(EDGE, rows - EDGE)
    blocks = [
        pltpu.make_async_copy(depth_in, depth_ref, sems.at[0, 0]),
        pltpu.make_async_copy(adjoint_in, adjoint_ref, sems.at[1, 0]),
    ]
    for block in blocks:
        block.start()

    def send(number, ref, inner, frame, wet_only):
        blank = jnp.zeros((LANES - 2 * EDGE, LANES), jnp.float32)
        columns = jnp.concatenate((frame[turned, EDGE : 3 * EDGE, :], blank), axis=0).T
        columns = {0: columns, tiles - 1: pltpu.roll(columns, LANES - 2 * EDGE, 1)}

        def with_columns(j, part, across):
            own = (lane < REACH) if j == 0 else (lane >= LANES - REACH)
            return jnp.where(own[part], wet_only(columns[j][part], part, across), inner[part, across])

        for j in range(tiles):
            across = slice(j * LANES, (j + 1) * LANES)
            for end, own in ((0, row < REACH), (1, row >= EDGE - REACH)):
                part = slice(end * (rows - EDGE), end * (rows - EDGE) + EDGE)
                value = frame[j, (1 + end) * EDGE : (2 + end) * EDGE, :]
                base = with_columns(j, part, across) if j in columns else inner[part, across]
                row_patch[number, end, :, across] = jnp.where(own, wet_only(value, part, across), base)
            if j in columns:
                column_patch[number, 0 if j == 0 else 1] = with_columns(j, middle, across)
        blocks[number].wait()
        copies = []
        for end in range(2):
            part = pl.ds(end * (rows - EDGE), EDGE)
            across = pl.ds(end * (cols - LANES), LANES)
            copies += [
                pltpu.make_async_copy(row_patch.at[number, end], ref.at[part, :], sems.at[number, 1 + end]),
                pltpu.make_async_copy(
                    column_patch.at[number, end], ref.at[pl.ds(EDGE, rows - 2 * EDGE), across], sems.at[number, 3 + end]
                ),
            ]
        for copy in copies:
            copy.start()
        return copies

    gradient = forward() + grad_in[...]
    copies = send(
        0, depth_ref, depth_in, held["last"],
        lambda value, part, across: jnp.where(wet_ref[part, across] > 0, value, h_ref[part, across]),
    )
    gradient = backward(gradient)
    copies += send(1, adjoint_ref, adjoint_in, held["final"], lambda value, part, across: value)
    grad_ref[...] = jnp.broadcast_to(gradient, grad_ref.shape)
    for copy in copies:
        copy.wait()


def total_kernel(parts_ref, out_ref):
    total = jnp.sum(parts_ref[...], axis=0, keepdims=True)
    steps, dams = out_ref.shape
    for step in range(steps):
        moved = pltpu.roll(total, LANES - step * dams, 1) if step else total
        out_ref[step : step + 1, :] = moved[:, :dams]


def on_device(
    water_depth, momentum_x, momentum_y, wet_mask, damage_class, damage_rates, dam_cell, releases
):
    rows, cols = water_depth.shape
    tiles = cols // LANES
    wide = cols + LANES
    rows_count = lax.axis_size("gx")
    cols_count = lax.axis_size("gy")
    vmem = pl.BlockSpec(memory_space=pltpu.VMEM)
    smem = pl.BlockSpec(memory_space=pltpu.SMEM)
    hbm = pl.BlockSpec(memory_space=pltpu.HBM)
    f32 = jnp.float32
    local = (water_depth, momentum_x, momentum_y, wet_mask, damage_class)
    given = (damage_rates, dam_cell.reshape(1, -1), releases.T)

    def swap(near, far, axis, count):
        near = lax.ppermute(near, axis, [(i, i + 1 - 2 * (i % 2)) for i in range(count)])
        return near, lax.ppermute(far, axis, [(i, (i - 1 + 2 * (i % 2)) % count) for i in range(count)])

    def array(*shape):
        return jax.ShapeDtypeStruct(shape, f32)

    def need(names, tiles, chunks):
        leads = dict(state0=(7,), state1=(7,), faces=(2,), walls=(4,), lam=(3,), back=(5,))
        return [array(*leads.get(name, ()), tiles, 8 * chunks + 8, LANES) for name in names]

    def scratch(names, tiles, chunks, spots):
        listed = pltpu.SMEM((5, spots), jnp.int32)
        return [listed] + [pltpu.VMEM(v.shape, v.dtype) for v in need(names, tiles, chunks)]

    own = pl.pallas_call(
        edge_kernel,
        out_shape=[array(FIELDS * EDGE, rows)] * 2,
        in_specs=[hbm] * 5,
        out_specs=[vmem] * 2,
        scratch_shapes=[
            pltpu.VMEM((2, 3, rows, LANES), f32),
            pltpu.VMEM((2, 2, rows, LANES), jnp.int32),
            pltpu.SemaphoreType.DMA((2, 5)),
        ],
        compiler_params=pltpu.CompilerParams(vmem_limit_bytes=60 * 1024 * 1024),
        cost_estimate=pl.CostEstimate(flops=10**9, bytes_accessed=4 * 10**7, transcendentals=0),
        name="edges",
    )(*local)
    beside_cols = swap(*own, "gy", cols_count)
    kept = need(KEPT, tiles, rows // 8)
    dams = dam_cell.shape[0]
    inner_params = pltpu.CompilerParams(vmem_limit_bytes=16 * 1024 * 1024)
    ends, depth, gradient, *kept = pl.pallas_call(
        inner_forward_kernel,
        out_shape=[array(2, STRIP, cols), array(rows, cols), array(1, LANES)] + kept,
        in_specs=[vmem] * 5 + [smem, vmem, smem],
        out_specs=[vmem] * (3 + len(kept)),
        scratch_shapes=scratch(("mask", "weight", "last", "back"), tiles, rows // 8, dams),
        compiler_params=inner_params,
        cost_estimate=pl.CostEstimate(flops=200 * rows * cols, bytes_accessed=6 * 4 * rows * cols, transcendentals=0),
        name="inner_forward",
    )(*local, *given)
    side, *to_rows = pl.pallas_call(
        corner_kernel,
        out_shape=[array(2, FIELDS, EDGE, LANES), array(STRIP, wide), array(STRIP, wide)],
        in_specs=[vmem] * 3,
        out_specs=[vmem] * 3,
        compiler_params=inner_params,
        name="corners",
    )(ends, *beside_cols)
    adjoint, gradient = pl.pallas_call(
        inner_backward_kernel,
        out_shape=[array(rows, cols), array(1, LANES)],
        in_specs=[vmem] * (len(kept) + 2),
        out_specs=[vmem] * 2,
        scratch_shapes=scratch(("lam", "back", "final"), tiles, rows // 8, dams),
        compiler_params=inner_params,
        cost_estimate=pl.CostEstimate(flops=300 * rows * cols, bytes_accessed=6 * 4 * rows * cols, transcendentals=0),
        name="inner_backward",
    )(*kept, given[1], gradient)
    beside_rows = swap(*to_rows, "gx", rows_count)
    depth, adjoint, parts = pl.pallas_call(
        frame_kernel,
        out_shape=[array(rows, cols), array(rows, cols), array(rows_count * cols_count, LANES)],
        in_specs=[vmem] * 5 + [smem, vmem, smem] + [vmem] * 10,
        out_specs=[hbm, hbm, vmem],
        scratch_shapes=(
            [pltpu.VMEM(v.shape, v.dtype) for v in need(KEPT, tiles + 3, 4)]
            + scratch(("mask", "weight", "last", "back", "lam", "final"), tiles + 3, 4, 2 * dams)
            + [
                pltpu.VMEM((2, 2, EDGE, cols), f32),
                pltpu.VMEM((2, 2, rows - 2 * EDGE, LANES), f32),
                pltpu.SemaphoreType.DMA((2, 5)),
            ]
        ),
        compiler_params=inner_params,
        name="frame",
    )(*local, *given, depth, adjoint, gradient, *own, *beside_cols, side, *beside_rows)
    gathered = lax.all_to_all(parts, ("gx", "gy"), 0, 0)
    release_grad = pl.pallas_call(
        total_kernel,
        out_shape=array(releases.shape[1], releases.shape[0]),
        in_specs=[vmem],
        out_specs=vmem,
        compiler_params=inner_params,
        name="total",
    )(gathered)
    return (depth, adjoint, release_grad.T)


def solution(mesh):
    in_specs = (P("gx", "gy"),) * 5 + (P(), P(), P())
    out_specs = (P("gx", "gy"), P("gx", "gy"), P())
    return jax.shard_map(
        on_device, mesh=mesh, in_specs=in_specs, out_specs=out_specs, check_vma=False
    )
```

```python
import itertools

import jax
import jax.numpy as jnp
from jax import lax
from jax.experimental import pallas as pl
from jax.experimental.pallas import tpu as pltpu
from jax.sharding import PartitionSpec as P

GRAVITY = 9.81
TIME_RATIO = 0.05
INFLOW_GAIN = 0.25

LANES = 128
REACH = 4
EDGE = 8
FIELDS = 4
STRIP = FIELDS * REACH
UNROLL = True


def class_rate(classes, rates_ref):
    rate = jnp.full(classes.shape, rates_ref[0], jnp.float32)
    for index in range(1, rates_ref.shape[0]):
        rate = jnp.where(classes == index, rates_ref[index], rate)
    return rate


def coded_fields(h, x, y, wet, classes):
    return jnp.where(wet > 0, h, 0.0), x, y, classes.astype(jnp.float32)


def is_even(axis):
    return (lax.axis_index(axis) & 1) == 0


def low_and_high(axis, near, far):
    even = is_even(axis)
    return jnp.where(even, far, near), jnp.where(even, near, far)


def edge_kernel(h_hbm, x_hbm, y_hbm, wet_hbm, class_hbm, near_ref, far_ref, values, codes, sems):
    rows, cols = h_hbm.shape
    copies = []
    for index, source in enumerate((h_hbm, x_hbm, y_hbm, wet_hbm, class_hbm)):
        for side in range(2):
            kept = values.at[side, index] if index < 3 else codes.at[side, index - 3]
            part = source.at[:, pl.ds(side * (cols - LANES), LANES)]
            copies.append(pltpu.make_async_copy(part, kept, sems.at[side, index]))
    for copy in copies:
        copy.start()
    for copy in copies:
        copy.wait()
    lane = lax.broadcasted_iota(jnp.int32, (rows, LANES), 1)
    mixed = jnp.zeros((rows, LANES), jnp.float32)
    for side in range(2):
        fields = coded_fields(*(values[side, k] for k in range(3)), *(codes[side, k] for k in range(2)))
        for index, field in enumerate(fields):
            first = (side * FIELDS + index) * EDGE
            moved = first if side == 0 else first + EDGE
            shifted = pltpu.roll(field, moved, 1) if moved else field
            mixed = jnp.where((lane >= first) & (lane < first + EDGE), shifted, mixed)
    turned = mixed.T
    far_ref[...], near_ref[...] = low_and_high("gy", turned[FIELDS * EDGE : 2 * FIELDS * EDGE], turned[: FIELDS * EDGE])


def beside(axis, near_ref, far_ref):
    place = lax.axis_index(axis)
    low, high = low_and_high(axis, near_ref[...], far_ref[...])
    return jnp.where(place > 0, low, 0.0), jnp.where(place < lax.axis_size(axis) - 1, high, 0.0)


def corner_kernel(ends_ref, near_in, far_in, side_ref, near_ref, far_ref):
    rows = near_in.shape[1]
    cols = ends_ref.shape[2]
    even = is_even("gx")
    left, right = beside("gy", near_in, far_in)
    blank = jnp.zeros((LANES - 2 * FIELDS * EDGE, rows), jnp.float32)
    turned = jnp.concatenate((right, left, blank), axis=0).T
    lane = lax.broadcasted_iota(jnp.int32, (EDGE, LANES), 1)
    strips = []
    for end, start, kept in ((0, 0, 0), (1, rows - EDGE, EDGE - REACH)):
        part = turned[start : start + EDGE]
        pieces = []
        for index in range(FIELDS):
            upper = pltpu.roll(part, LANES - index * EDGE, 1) if index else part
            lower = pltpu.roll(part, LANES - (1 + FIELDS + index) * EDGE, 1)
            tile = jnp.where(lane < EDGE, upper, jnp.where(lane >= LANES - EDGE, lower, 0.0))
            side_ref[end, index] = tile
            pieces.append(tile[kept : kept + REACH])
        strips.append((ends_ref[end], jnp.concatenate(pieces, axis=0)))
    for part, low, high in zip((slice(0, cols), slice(cols, cols + LANES)), *strips):
        near_ref[:, part] = jnp.where(even, high, low)
        far_ref[:, part] = jnp.where(even, low, high)


def cell_terms(height, flow_x, flow_y):
    scaled = GRAVITY * height
    inverse = pltpu.reciprocal(height, approx=True)
    return flow_x * inverse, flow_y * inverse, scaled * lax.rsqrt(scaled), inverse


def waves(u_low, c_low, u_high, c_high, both):
    slow_low, slow_high = u_low - c_low, u_high - c_high
    fast_low, fast_high = u_low + c_low, u_high + c_high
    slowest = jnp.minimum(jnp.minimum(slow_low, slow_high), 0.0)
    fastest = jnp.maximum(jnp.maximum(fast_low, fast_high), 0.0)
    inverse = both * pltpu.reciprocal(fastest - slowest, approx=True)
    share_low = fastest * inverse
    share_high = -(slowest * inverse)
    spread = slowest * share_low
    return slowest, fastest, inverse, share_low, share_high, spread, slow_low <= slow_high, fast_low >= fast_high


def speed_terms(slowest, fastest, of_slowest, of_fastest, slow_is_low, fast_is_low):
    of_slowest = jnp.where(slowest < 0.0, of_slowest, 0.0)
    of_fastest = jnp.where(fastest > 0.0, of_fastest, 0.0)
    slow_to_low = jnp.where(slow_is_low, of_slowest, 0.0)
    fast_to_low = jnp.where(fast_is_low, of_fastest, 0.0)
    slow_to_high = of_slowest - slow_to_low
    fast_to_high = of_fastest - fast_to_low
    return (
        fast_to_low + slow_to_low,
        fast_to_low - slow_to_low,
        fast_to_high + slow_to_high,
        fast_to_high - slow_to_high,
    )


def window(chunks, after, before, put, listed, dams, rates_ref, release_ref, held):
    state0, state1, mask, faces, walls, weight, last, lam0, lam, back, final = (
        held.get(name) for name in (
            "state0", "state1", "mask", "faces", "walls", "weight", "last", "lam0", "lam", "back", "final",
        )
    )
    tiles = len(after)
    every = range(tiles)
    wanted = held.get("wanted", every)
    lane = lax.broadcasted_iota(jnp.int32, (8, LANES), 1)

    def at(ref, k, j, start):
        return ref[k, j, pl.ds(start, 8), :]

    def next_col(values):
        rolled = [pltpu.roll(v, LANES - 1, 1) for v in values]
        return [jnp.where(lane == LANES - 1, rolled[after[j]], rolled[j]) for j in every]

    def previous_col(values):
        rolled = [pltpu.roll(v, 1, 1) for v in values]
        return [jnp.where(lane == 0, rolled[before[j]], rolled[j]) for j in every]

    def previous_row(slot, j, start, value):
        back[slot, j, pl.ds(start + 8, 8), :] = value
        return back[slot, j, pl.ds(start + 7, 8), :]

    def put_cell(ref, j, start, height, flow_x, flow_y):
        u, v, c, inverse = cell_terms(height, flow_x, flow_y)
        for k, value in enumerate((height, flow_x, flow_y, u, v, c, inverse)):
            ref[k, j, pl.ds(start, 8), :] = value

    def fill(j, start, wet, height, flow_x, flow_y, classes):
        put_cell(
            state0, j, start,
            jnp.where(wet, height, 1.0), jnp.where(wet, flow_x, 0.0), jnp.where(wet, flow_y, 0.0),
        )
        mask[j, pl.ds(start, 8), :] = jnp.where(wet, 1.0, 0.0)
        weight[j, pl.ds(start, 8), :] = jnp.where(wet, class_rate(classes, rates_ref), 0.0)

    def clear(ref, start, value=0.0):
        index = tuple(range(n) for n in ref.shape[:-2])
        for lead in itertools.product(*index):
            ref[lead + (pl.ds(start, 8), slice(None))] = jnp.full((8, LANES), value, jnp.float32)

    def run(step, count=chunks):
        lax.fori_loop(0, count, step, 0, unroll=UNROLL)

    def add_inflow(step, ref, refresh):
        def one(index, carry):
            d, row, j, col = (listed[k, index] for k in range(4))
            if refresh:
                old = [ref[k, j, pl.ds(row, 1), :] for k in range(3)]
            else:
                old = [ref[j, pl.ds(row, 1), :]]
            here = lax.broadcasted_iota(jnp.int32, (1, LANES), 1) == col
            height = old[0] + jnp.where(here, INFLOW_GAIN * release_ref[step, d], 0.0)
            if refresh:
                terms = (height, old[1], old[2]) + cell_terms(height, old[1], old[2])
                for k, value in enumerate(terms):
                    ref[k, j, pl.ds(row, 1), :] = value
            else:
                ref[j, pl.ds(row, 1), :] = height
            return carry

        lax.fori_loop(0, dams, one, 0)

    def pick(step, ref, gradient):
        lane_row = lax.broadcasted_iota(jnp.int32, (1, LANES), 1)

        def one(index, total):
            d, row, j, col, inside = (listed[k, index] for k in range(5))
            values = ref[j, pl.ds(row, 1), :]
            value = jnp.sum(jnp.where(lane_row == col, values, 0.0), axis=1, keepdims=True)
            spot = (lane_row == d + step * release_ref.shape[1]) & (inside > 0)
            return total + jnp.where(spot, (INFLOW_GAIN / TIME_RATIO) * value, 0.0)

        return lax.fori_loop(0, dams, one, gradient)

    def forward():
        clear(back, 0)
        for ref in (state0, state1):
            for k in range(7):
                clear(ref.at[k], chunks * 8, 1.0 if k in (0, 5, 6) else 0.0)
        clear(mask, chunks * 8)
        clear(lam0, chunks * 8)
        put(fill)

        def first_step(i, carry):
            start = pl.multiple_of(i * 8, 8)
            low = [[at(state0, k, j, start) for j in every] for k in range(6)]
            h, x, y, u, v, c = low
            m = [mask[j, pl.ds(start, 8), :] for j in every]
            half = [(0.5 * GRAVITY) * h[j] * h[j] for j in every]
            cross = [x[j] * v[j] for j in every]
            press_x = [x[j] * u[j] + half[j] for j in every]
            press_y = [y[j] * v[j] + half[j] for j in every]
            gain = []
            for j in every:
                hn, xn, yn, un, cn = (at(state0, k, j, start + 1) for k in (0, 1, 2, 3, 5))
                both = m[j] * mask[j, pl.ds(start + 1, 8), :]
                faces[0, j, pl.ds(start, 8), :] = both
                _, _, _, wl, wh, sp, _, _ = waves(u[j], c[j], un, cn, both)
                fh = wl * x[j] + wh * xn + sp * (hn - h[j])
                fn = wl * press_x[j] + wh * (xn * un + (0.5 * GRAVITY) * hn * hn) + sp * (xn - x[j])
                ft = wl * cross[j] + wh * (yn * un) + sp * (yn - y[j])
                both_low = previous_row(0, j, start, both)
                tilt = both_low - both
                shut = 2.0 * m[j] - both - both_low
                walls[0, j, pl.ds(start, 8), :] = tilt
                walls[1, j, pl.ds(start, 8), :] = shut
                gain.append(
                    [
                        fh - previous_row(1, j, start, fh),
                        fn - previous_row(2, j, start, fn) + tilt * press_x[j] + shut * ((jnp.abs(u[j]) + c[j]) * x[j]),
                        ft - previous_row(3, j, start, ft),
                    ]
                )
            hn, xn, yn, vn, cn, pn, tn, mn = (next_col(q) for q in (h, x, y, v, c, press_y, cross, m))
            flux = [[], [], []]
            both_up = []
            for j in every:
                both = m[j] * mn[j]
                faces[1, j, pl.ds(start, 8), :] = both
                both_up.append(both)
                _, _, _, wl, wh, sp, _, _ = waves(v[j], c[j], vn[j], cn[j], both)
                flux[0].append(wl * y[j] + wh * yn[j] + sp * (hn[j] - h[j]))
                flux[1].append(wl * press_y[j] + wh * pn[j] + sp * (yn[j] - y[j]))
                flux[2].append(wl * cross[j] + wh * tn[j] + sp * (xn[j] - x[j]))
            flux_low = [previous_col(q) for q in flux]
            both_low = previous_col(both_up)
            for j in every:
                tilt = both_low[j] - both_up[j]
                shut = 2.0 * m[j] - both_up[j] - both_low[j]
                walls[2, j, pl.ds(start, 8), :] = tilt
                walls[3, j, pl.ds(start, 8), :] = shut
                change_h = gain[j][0] + (flux[0][j] - flux_low[0][j])
                change_x = gain[j][1] + (flux[2][j] - flux_low[2][j])
                change_y = gain[j][2] + (flux[1][j] - flux_low[1][j])
                change_y = change_y + tilt * press_y[j] + shut * ((jnp.abs(v[j]) + c[j]) * y[j])
                put_cell(
                    state1, j, start,
                    h[j] - TIME_RATIO * change_h, x[j] - TIME_RATIO * change_x, y[j] - TIME_RATIO * change_y,
                )
            return carry

        run(first_step)
        add_inflow(0, state1, True)

        def second_step(i, carry):
            start = pl.multiple_of(i * 8, 8)
            h, x, y, u, v, c = [[at(state1, k, j, start) for j in every] for k in range(6)]
            gain = []
            for j in every:
                hn, xn, un, cn = (at(state1, k, j, start + 1) for k in (0, 1, 3, 5))
                _, _, _, wl, wh, sp, _, _ = waves(u[j], c[j], un, cn, at(faces, 0, j, start))
                fh = wl * x[j] + wh * xn + sp * (hn - h[j])
                gain.append(fh - previous_row(0, j, start, fh))
            hn, yn, vn, cn = (next_col(q) for q in (h, y, v, c))
            flux = []
            for j in every:
                _, _, _, wl, wh, sp, _, _ = waves(v[j], c[j], vn[j], cn[j], at(faces, 1, j, start))
                flux.append(wl * y[j] + wh * yn[j] + sp * (hn[j] - h[j]))
            flux_low = previous_col(flux)
            for j in every:
                last[j, pl.ds(start, 8), :] = h[j] - TIME_RATIO * (gain[j] + (flux[j] - flux_low[j]))
            return carry

        run(second_step)
        add_inflow(1, last, False)

        def finish_depth(i, carry):
            start = pl.multiple_of(i * 8, 8)
            for j in every:
                height = last[j, pl.ds(start, 8), :]
                lam0[j, pl.ds(start, 8), :] = TIME_RATIO * (weight[j, pl.ds(start, 8), :] * height)
            return carry

        run(finish_depth)

        return pick(1, lam0, jnp.zeros((1, LANES), jnp.float32))


    def backward(gradient):
        clear(back, 0)
        clear(lam, chunks * 8)

        def second_back(i, carry):
            start = pl.multiple_of(i * 8, 8)
            h, x, y, u, v, c, r = [[at(state1, k, j, start) for j in every] for k in range(7)]
            lh = [lam0[j, pl.ds(start, 8), :] for j in every]

            def face(hl, nl, ul, cl, hh, nh, uh, ch, gl, gh, both):
                slow, fast, inv, wl, wh, sp, slow_low, fast_low = waves(ul, cl, uh, ch, both)
                g = gh - gl
                dn, dh = nh - nl, hh - hl
                to_low, to_high = wl * g, wh * g
                of_slow = -(to_low * inv) * (dn - fast * dh)
                of_fast = -(to_high * inv) * (dn - slow * dh)
                return (to_low, to_high, sp * g) + speed_terms(slow, fast, of_slow, of_fast, slow_low, fast_low)

            partial_h, partial_u, partial_c, flow = [], [], [], []
            for j in every:
                hn, xn, un, cn = (at(state1, k, j, start + 1) for k in (0, 1, 3, 5))
                to_low, to_high, jump, u_low, c_low, u_high, c_high = face(
                    h[j], x[j], u[j], c[j], hn, xn, un, cn, lh[j], lam0[j, pl.ds(start + 1, 8), :], at(faces, 0, j, start)
                )
                of_u = u_low + previous_row(2, j, start, u_high)
                partial_h.append(previous_row(0, j, start, jump) - jump)
                partial_c.append(c_low + previous_row(3, j, start, c_high))
                partial_u.append(of_u * u[j])
                flow.append(to_low + previous_row(1, j, start, to_high) + of_u * r[j])
            hn, yn, vn, cn, ln = (next_col(q) for q in (h, y, v, c, lh))
            terms = [
                face(h[j], y[j], v[j], c[j], hn[j], yn[j], vn[j], cn[j], lh[j], ln[j], at(faces, 1, j, start))
                for j in every
            ]
            high, jump, u_high, c_high = (previous_col([t[k] for t in terms]) for k in (1, 2, 5, 6))
            for j in every:
                to_low, _, own_jump, u_low, c_low, _, _ = terms[j]
                of_v = u_low + u_high[j]
                of_c = partial_c[j] + c_low + c_high[j]
                of_h = partial_h[j] + (jump[j] - own_jump)
                of_h = of_h + r[j] * (0.5 * (of_c * c[j]) - partial_u[j] - of_v * v[j])
                lam[0, j, pl.ds(start, 8), :] = lh[j] + TIME_RATIO * of_h
                lam[1, j, pl.ds(start, 8), :] = TIME_RATIO * flow[j]
                lam[2, j, pl.ds(start, 8), :] = TIME_RATIO * (to_low + high[j] + of_v * r[j])
            return carry

        run(second_back)

        gradient = pick(0, lam.at[0], gradient)

        def first_back(i, carry):
            start = pl.multiple_of(i * 8, 8)
            h, x, y, u, v, c, r = [[at(state0, k, j, start) for j in every] for k in range(7)]
            lh, lx, ly = [[at(lam, k, j, start) for j in every] for k in range(3)]
            half = [(0.5 * GRAVITY) * h[j] * h[j] for j in every]
            cross = [x[j] * v[j] for j in every]

            def face(hl, nl, tl, ul, cl, pl_, kl, hh, nh, th, uh, ch, ph, kh, gl, gh, both):
                slow, fast, inv, wl, wh, sp, slow_low, fast_low = waves(ul, cl, uh, ch, both)
                g_h, g_n, g_t = (b - a for a, b in zip(gl, gh))
                dn = nh - nl
                of_flux = g_h * dn + g_n * (ph - pl_) + g_t * (kh - kl)
                of_jump = g_h * (hh - hl) + g_n * dn + g_t * (th - tl)
                of_slow = -(wl * inv) * (of_flux - fast * of_jump)
                of_fast = -(wh * inv) * (of_flux - slow * of_jump)
                return (wl * g_n, wl * g_t, wh * g_n, wh * g_t, sp * g_h) + speed_terms(
                    slow, fast, of_slow, of_fast, slow_low, fast_low
                )

            kept = {}
            for j in wanted:
                hn, xn, yn, un, cn = (at(state0, k, j, start + 1) for k in (0, 1, 2, 3, 5))
                nl, tl, nh, th, jump, u_low, c_low, u_high, c_high = face(
                    h[j], x[j], y[j], u[j], c[j], x[j] * u[j] + half[j], cross[j],
                    hn, xn, yn, un, cn, xn * un + (0.5 * GRAVITY) * hn * hn, yn * un,
                    (lh[j], lx[j], ly[j]), tuple(at(lam, k, j, start + 1) for k in range(3)), at(faces, 0, j, start),
                )
                shut = lx[j] * at(walls, 1, j, start)
                normal = nl + previous_row(0, j, start, nh) - lx[j] * at(walls, 0, j, start)
                across = tl + previous_row(1, j, start, th)
                of_u = normal * x[j] + across * y[j] + u_low + previous_row(3, j, start, u_high) - shut * jnp.abs(x[j])
                of_c = c_low + previous_row(4, j, start, c_high) - shut * x[j]
                kept[j] = (normal, previous_row(2, j, start, jump) - jump, of_u * u[j], of_c)
            press = [y[j] * v[j] + half[j] for j in every]
            hn, xn, yn, vn, cn, pn, kn = (next_col(q) for q in (h, x, y, v, c, press, cross))
            lhn, lxn, lyn = (next_col(q) for q in (lh, lx, ly))
            terms = [
                face(
                    h[j], y[j], x[j], v[j], c[j], press[j], cross[j],
                    hn[j], yn[j], xn[j], vn[j], cn[j], pn[j], kn[j],
                    (lh[j], ly[j], lx[j]), (lhn[j], lyn[j], lxn[j]), at(faces, 1, j, start),
                )
                for j in every
            ]
            nh, th, jump, u_high, c_high = (previous_col([t[k] for t in terms]) for k in (2, 3, 4, 7, 8))
            for j in wanted:
                shut = ly[j] * at(walls, 3, j, start)
                normal = terms[j][0] + nh[j] - ly[j] * at(walls, 2, j, start)
                across = terms[j][1] + th[j]
                of_v = normal * y[j] + across * x[j] + terms[j][5] + u_high[j] - shut * jnp.abs(y[j])
                of_c = kept[j][3] + terms[j][6] + c_high[j] - shut * y[j]
                of_h = kept[j][1] + (jump[j] - terms[j][4]) + GRAVITY * h[j] * (kept[j][0] + normal)
                of_h = of_h + r[j] * (0.5 * (of_c * c[j]) - kept[j][2] - of_v * v[j])
                final[j, pl.ds(start, 8), :] = (1.0 / TIME_RATIO) * lh[j] + of_h
            return carry

        run(first_back, held.get("needed", chunks))
        return gradient

    return forward, backward


def list_dams(dam_ref, listed, rows, cols, spots):
    total_cols = cols * lax.axis_size("gy")
    row_first = lax.axis_index("gx") * rows
    col_first = lax.axis_index("gy") * cols

    def local(cell):
        if total_cols & (total_cols - 1):
            row = lax.div(cell, jnp.full(jnp.shape(cell), total_cols, jnp.int32))
        else:
            row = lax.shift_right_logical(cell, jnp.full(jnp.shape(cell), total_cols.bit_length() - 1, jnp.int32))
        return row - row_first, cell - row * total_cols - col_first

    cells = dam_ref[...]
    none = cells.shape[1]
    number = lax.broadcasted_iota(jnp.int32, cells.shape, 1)
    row, col = local(cells)
    near = within(row, -REACH, rows + REACH) & within(col, -REACH, cols + REACH)
    number = jnp.where(near, number, none)

    def one(state):
        d, count = state
        row, col = local(jnp.max(jnp.where(number == d, cells, 0)))
        for held, spot in spots(row, col):
            @pl.when(held)
            def _():
                for k, value in enumerate((d,) + spot):
                    listed[k, count] = value

            count = count + jnp.where(held, 1, 0)
        return jnp.min(jnp.where(number > d, number, none)), count

    return lax.while_loop(lambda state: state[0] < none, one, (jnp.min(number), jnp.int32(0)))[1]


def within(value, first, end):
    return (value >= first) & (value < end)


def split(place):
    return lax.shift_right_logical(place, LANES.bit_length() - 1), place & (LANES - 1)


def inner_spots(rows, cols):
    def spots(row, col):
        tile, lane = split(col)
        own = within(row, REACH, rows - REACH) & within(col, REACH, cols - REACH)
        yield within(row, 0, rows) & within(col, 0, cols), (row, tile, lane, jnp.where(own, 1, 0))

    return spots


def ring(tiles):
    return [(j + 1) % tiles for j in range(tiles)], [(j - 1) % tiles for j in range(tiles)]


KEPT = ("state0", "state1", "faces", "walls", "lam0")


def inner_forward_kernel(
    h_ref, x_ref, y_ref, wet_ref, class_ref, rates_ref, dam_ref, release_ref,
    ends_ref, depth_ref, grad_ref, *rest,
):
    held = dict(zip(KEPT + ("listed", "mask", "weight", "last", "back"), rest))
    rows, cols = h_ref.shape
    tiles = cols // LANES
    chunks = rows // 8
    for end, (start, kept) in enumerate(((0, 0), (rows - EDGE, EDGE - REACH))):
        part = slice(start, start + EDGE)
        own = coded_fields(h_ref[part, :], x_ref[part, :], y_ref[part, :], wet_ref[part, :], class_ref[part, :])
        for index in range(FIELDS):
            ends_ref[end, index * REACH : (index + 1) * REACH, :] = own[index][kept : kept + REACH]
    dams = list_dams(dam_ref, held["listed"], rows, cols, inner_spots(rows, cols))

    def put(fill):
        def one(i, carry):
            part = pl.ds(pl.multiple_of(i * 8, 8), 8)
            for j in range(tiles):
                across = pl.ds(j * LANES, LANES)
                fill(
                    j, pl.multiple_of(i * 8, 8), wet_ref[part, across] > 0,
                    h_ref[part, across], x_ref[part, across], y_ref[part, across], class_ref[part, across],
                )
            return carry

        lax.fori_loop(0, chunks, one, 0, unroll=2)

    forward, _ = window(chunks, *ring(tiles), put, held["listed"], dams, rates_ref, release_ref, held)
    grad_ref[...] = forward()
    for j in range(tiles):
        across = slice(j * LANES, (j + 1) * LANES)
        depth_ref[:, across] = jnp.where(wet_ref[:, across] > 0, held["last"][j, :rows, :], h_ref[:, across])


def inner_backward_kernel(*refs):
    names = KEPT + ("dams", "grad_in", "adjoint", "grad", "listed", "lam", "back", "final")
    held = dict(zip(names, refs))
    rows, cols = held["adjoint"].shape
    tiles = cols // LANES
    dams = list_dams(held["dams"], held["listed"], rows, cols, inner_spots(rows, cols))
    shape = jax.ShapeDtypeStruct((1, held["dams"].shape[1]), jnp.float32)
    _, backward = window(rows // 8, *ring(tiles), None, held["listed"], dams, None, shape, held)
    held["grad"][...] = backward(held["grad_in"][...])
    for j in range(tiles):
        held["adjoint"][:, j * LANES : (j + 1) * LANES] = held["final"][j, :rows, :]


def frame_kernel(
    h_ref, x_ref, y_ref, wet_ref, class_ref, rates_ref, dam_ref, release_ref,
    depth_in, adjoint_in, grad_in, near_own, far_own, near_col, far_col, side_ref, near_row, far_row,
    depth_ref, adjoint_ref, grad_ref, *rest,
):
    rows, cols = h_ref.shape
    tiles = cols // LANES
    chunks = 4
    turned = tiles + 1
    after = [(j + 1) % turned for j in range(turned)] + [turned + 1, turned]
    before = [(j - 1) % turned for j in range(turned)] + [turned + 1, turned]

    def chunk_row(place, count):
        return jnp.where(place < EDGE, place + EDGE, place - count + 3 * EDGE)

    def near_end(place, count):
        return within(place, -REACH, EDGE) | within(place, count - EDGE, count + REACH)

    def at_end(place, count):
        return within(place, 0, REACH) | within(place, count - REACH, count)

    def spots(row, col):
        near = within(row, -REACH, rows + REACH) & within(col, -REACH, cols + REACH)
        tile, lane = split(jnp.where(col < 0, col + (tiles + 1) * LANES, col))
        own = at_end(row, rows) & within(col, 0, cols)
        yield near & near_end(row, rows), (chunk_row(row, rows), tile, lane, jnp.where(own, 1, 0))
        tile, lane = split(jnp.where(row < 0, row + 2 * LANES, row))
        own = at_end(col, cols) & within(row, REACH, rows - REACH)
        yield near & near_end(col, cols), (chunk_row(col, cols), tile + turned, lane, jnp.where(own, 1, 0))

    names = KEPT + ("listed", "mask", "weight", "last", "back", "lam", "final")
    held = dict(zip(names + ("row_patch", "column_patch", "sems"), rest))
    dams = list_dams(dam_ref, held["listed"], rows, cols, spots)
    above, below = beside("gx", near_row, far_row)
    left, right = beside("gy", near_col, far_col)
    first_cols, last_cols = low_and_high("gy", near_own[...], far_own[...])

    def put(fill):
        blank = jnp.zeros((EDGE - REACH, LANES), jnp.float32)

        def coded(j, start, h, x, y, code):
            fill(j, start, h > 0.0, h, x, y, code.astype(jnp.int32))

        for j in range(tiles + 1):
            across = slice(j * LANES, (j + 1) * LANES)
            for start, strip in ((0, above), (3 * EDGE, below)):
                pieces = [strip[k * REACH : (k + 1) * REACH, across] for k in range(FIELDS)]
                coded(j, start, *(jnp.concatenate((blank, v) if start == 0 else (v, blank), axis=0) for v in pieces))
            for end, first in ((0, 0), (1, rows - EDGE)):
                start = (1 + end) * EDGE
                if j < tiles:
                    part = slice(first, first + EDGE)
                    fill(
                        j, start, wet_ref[part, across] > 0,
                        h_ref[part, across], x_ref[part, across], y_ref[part, across], class_ref[part, across],
                    )
                else:
                    coded(j, start, *(side_ref[end, k] for k in range(FIELDS)))
        order = (0, 2, 1, 3)
        for chunk, strip in enumerate((left, first_cols, last_cols, right)):
            coded(turned, chunk * EDGE, *(strip[k * EDGE : (k + 1) * EDGE] for k in order))
        strips = jnp.concatenate((above, below), axis=0)
        outer = strips[:, tiles * LANES :]
        mixed = jnp.zeros((2 * STRIP, LANES), jnp.float32)
        lane = lax.broadcasted_iota(jnp.int32, (2 * STRIP, LANES), 1)
        pieces = (
            (outer, LANES - EDGE),
            (strips[:, :LANES], 0),
            (strips[:, (tiles - 1) * LANES : tiles * LANES], LANES - EDGE),
            (outer, 0),
        )
        for chunk, (piece, first) in enumerate(pieces):
            moved = (chunk * EDGE - first) % LANES
            mixed = jnp.where(lane // EDGE == chunk, pltpu.roll(piece, moved, 1) if moved else piece, mixed)
        corners = jnp.concatenate((mixed, jnp.zeros((LANES - 2 * STRIP, LANES), jnp.float32)), axis=0).T
        corners = corners[: chunks * EDGE]
        lane = lax.broadcasted_iota(jnp.int32, (chunks * EDGE, LANES), 1)
        fields = []
        for k in order:
            from_above = pltpu.roll(corners, LANES - REACH - k * REACH, 1)
            from_below = pltpu.roll(corners, LANES - STRIP - k * REACH, 1)
            fields.append(jnp.where(lane < REACH, from_below, jnp.where(lane >= LANES - REACH, from_above, 0.0)))
        for chunk in range(chunks):
            coded(turned + 1, chunk * EDGE, *(v[chunk * EDGE : (chunk + 1) * EDGE] for v in fields))

    held["needed"] = chunks - 1
    held["wanted"] = [*range(tiles), turned]
    forward, backward = window(chunks, after, before, put, held["listed"], dams, rates_ref, release_ref, held)
    row_patch, column_patch, sems = held["row_patch"], held["column_patch"], held["sems"]
    lane = lax.broadcasted_iota(jnp.int32, (rows, LANES), 1)
    row = lax.broadcasted_iota(jnp.int32, (EDGE, LANES), 0)
    middle = slice(EDGE, rows - EDGE)
    blocks = [
        pltpu.make_async_copy(depth_in, depth_ref, sems.at[0, 0]),
        pltpu.make_async_copy(adjoint_in, adjoint_ref, sems.at[1, 0]),
    ]
    for block in blocks:
        block.start()

    def send(number, ref, inner, frame, wet_only):
        blank = jnp.zeros((LANES - 2 * EDGE, LANES), jnp.float32)
        columns = jnp.concatenate((frame[turned, EDGE : 3 * EDGE, :], blank), axis=0).T
        columns = {0: columns, tiles - 1: pltpu.roll(columns, LANES - 2 * EDGE, 1)}

        def with_columns(j, part, across):
            own = (lane < REACH) if j == 0 else (lane >= LANES - REACH)
            return jnp.where(own[part], wet_only(columns[j][part], part, across), inner[part, across])

        for j in range(tiles):
            across = slice(j * LANES, (j + 1) * LANES)
            for end, own in ((0, row < REACH), (1, row >= EDGE - REACH)):
                part = slice(end * (rows - EDGE), end * (rows - EDGE) + EDGE)
                value = frame[j, (1 + end) * EDGE : (2 + end) * EDGE, :]
                base = with_columns(j, part, across) if j in columns else inner[part, across]
                row_patch[number, end, :, across] = jnp.where(own, wet_only(value, part, across), base)
            if j in columns:
                column_patch[number, 0 if j == 0 else 1] = with_columns(j, middle, across)
        blocks[number].wait()
        copies = []
        for end in range(2):
            part = pl.ds(end * (rows - EDGE), EDGE)
            across = pl.ds(end * (cols - LANES), LANES)
            copies += [
                pltpu.make_async_copy(row_patch.at[number, end], ref.at[part, :], sems.at[number, 1 + end]),
                pltpu.make_async_copy(
                    column_patch.at[number, end], ref.at[pl.ds(EDGE, rows - 2 * EDGE), across], sems.at[number, 3 + end]
                ),
            ]
        for copy in copies:
            copy.start()
        return copies

    gradient = forward() + grad_in[...]
    copies = send(
        0, depth_ref, depth_in, held["last"],
        lambda value, part, across: jnp.where(wet_ref[part, across] > 0, value, h_ref[part, across]),
    )
    gradient = backward(gradient)
    copies += send(1, adjoint_ref, adjoint_in, held["final"], lambda value, part, across: value)
    grad_ref[...] = jnp.broadcast_to(gradient, grad_ref.shape)
    for copy in copies:
        copy.wait()


def total_kernel(parts_ref, out_ref):
    total = jnp.sum(parts_ref[...], axis=0, keepdims=True)
    steps, dams = out_ref.shape
    for step in range(steps):
        moved = pltpu.roll(total, LANES - step * dams, 1) if step else total
        out_ref[step : step + 1, :] = moved[:, :dams]


def on_device(
    water_depth, momentum_x, momentum_y, wet_mask, damage_class, damage_rates, dam_cell, releases
):
    rows, cols = water_depth.shape
    tiles = cols // LANES
    wide = cols + LANES
    rows_count = lax.axis_size("gx")
    cols_count = lax.axis_size("gy")
    vmem = pl.BlockSpec(memory_space=pltpu.VMEM)
    smem = pl.BlockSpec(memory_space=pltpu.SMEM)
    hbm = pl.BlockSpec(memory_space=pltpu.HBM)
    f32 = jnp.float32
    local = (water_depth, momentum_x, momentum_y, wet_mask, damage_class)
    given = (damage_rates, dam_cell.reshape(1, -1), releases.T)

    def swap(near, far, axis, count):
        near = lax.ppermute(near, axis, [(i, i + 1 - 2 * (i % 2)) for i in range(count)])
        return near, lax.ppermute(far, axis, [(i, (i - 1 + 2 * (i % 2)) % count) for i in range(count)])

    def array(*shape):
        return jax.ShapeDtypeStruct(shape, f32)

    def need(names, tiles, chunks):
        leads = dict(state0=(7,), state1=(7,), faces=(2,), walls=(4,), lam=(3,), back=(5,))
        return [array(*leads.get(name, ()), tiles, 8 * chunks + 8, LANES) for name in names]

    def scratch(names, tiles, chunks, spots):
        listed = pltpu.SMEM((5, spots), jnp.int32)
        return [listed] + [pltpu.VMEM(v.shape, v.dtype) for v in need(names, tiles, chunks)]

    own = pl.pallas_call(
        edge_kernel,
        out_shape=[array(FIELDS * EDGE, rows)] * 2,
        in_specs=[hbm] * 5,
        out_specs=[vmem] * 2,
        scratch_shapes=[
            pltpu.VMEM((2, 3, rows, LANES), f32),
            pltpu.VMEM((2, 2, rows, LANES), jnp.int32),
            pltpu.SemaphoreType.DMA((2, 5)),
        ],
        compiler_params=pltpu.CompilerParams(vmem_limit_bytes=60 * 1024 * 1024),
        cost_estimate=pl.CostEstimate(flops=10**9, bytes_accessed=4 * 10**7, transcendentals=0),
        name="edges",
    )(*local)
    beside_cols = swap(*own, "gy", cols_count)
    kept = need(KEPT, tiles, rows // 8)
    dams = dam_cell.shape[0]
    inner_params = pltpu.CompilerParams(vmem_limit_bytes=16 * 1024 * 1024)
    ends, depth, gradient, *kept = pl.pallas_call(
        inner_forward_kernel,
        out_shape=[array(2, STRIP, cols), array(rows, cols), array(1, LANES)] + kept,
        in_specs=[vmem] * 5 + [smem, vmem, smem],
        out_specs=[vmem] * (3 + len(kept)),
        scratch_shapes=scratch(("mask", "weight", "last", "back"), tiles, rows // 8, dams),
        compiler_params=inner_params,
        cost_estimate=pl.CostEstimate(flops=200 * rows * cols, bytes_accessed=6 * 4 * rows * cols, transcendentals=0),
        name="inner_forward",
    )(*local, *given)
    side, *to_rows = pl.pallas_call(
        corner_kernel,
        out_shape=[array(2, FIELDS, EDGE, LANES), array(STRIP, wide), array(STRIP, wide)],
        in_specs=[vmem] * 3,
        out_specs=[vmem] * 3,
        compiler_params=inner_params,
        name="corners",
    )(ends, *beside_cols)
    adjoint, gradient = pl.pallas_call(
        inner_backward_kernel,
        out_shape=[array(rows, cols), array(1, LANES)],
        in_specs=[vmem] * (len(kept) + 2),
        out_specs=[vmem] * 2,
        scratch_shapes=scratch(("lam", "back", "final"), tiles, rows // 8, dams),
        compiler_params=inner_params,
        cost_estimate=pl.CostEstimate(flops=300 * rows * cols, bytes_accessed=6 * 4 * rows * cols, transcendentals=0),
        name="inner_backward",
    )(*kept, given[1], gradient)
    beside_rows = swap(*to_rows, "gx", rows_count)
    depth, adjoint, parts = pl.pallas_call(
        frame_kernel,
        out_shape=[array(rows, cols), array(rows, cols), array(rows_count * cols_count, LANES)],
        in_specs=[vmem] * 5 + [smem, vmem, smem] + [vmem] * 10,
        out_specs=[hbm, hbm, vmem],
        scratch_shapes=(
            [pltpu.VMEM(v.shape, v.dtype) for v in need(KEPT, tiles + 3, 4)]
            + scratch(("mask", "weight", "last", "back", "lam", "final"), tiles + 3, 4, 2 * dams)
            + [
                pltpu.VMEM((2, 2, EDGE, cols), f32),
                pltpu.VMEM((2, 2, rows - 2 * EDGE, LANES), f32),
                pltpu.SemaphoreType.DMA((2, 5)),
            ]
        ),
        compiler_params=inner_params,
        name="frame",
    )(*local, *given, depth, adjoint, gradient, *own, *beside_cols, side, *beside_rows)
    gathered = lax.all_to_all(parts, ("gx", "gy"), 0, 0)
    release_grad = pl.pallas_call(
        total_kernel,
        out_shape=array(releases.shape[1], releases.shape[0]),
        in_specs=[vmem],
        out_specs=vmem,
        compiler_params=inner_params,
        name="total",
    )(gathered)
    return (depth, adjoint, release_grad.T)


def solution(mesh):
    in_specs = (P("gx", "gy"),) * 5 + (P(), P(), P())
    out_specs = (P("gx", "gy"), P("gx", "gy"), P())
    return jax.shard_map(
        on_device, mesh=mesh, in_specs=in_specs, out_specs=out_specs, check_vma=False
    )
```
